32 devices in a mesh: sq: 8 (over y, x, core), tp: 4 (over z).
Axes of the slice: x: 2, y: 2, z: 4, core: 2. Of those that a mesh axis runs over, the one named last changes fastest.
Arguments:
- inputs: bfloat16 [2048, 4, 2048], P('sq', None, 'tp'), may hold values from -6 to 6
- lengths: int32 [4], replicated, may hold values from 256 to 2048, as said below
- routes: int32 [2048, 4, 8], P('sq'), may hold values from 0 to 15, all different within a row; in each aligned block of 1024 rows (0 to 1023, 1024 to 2047, ..., all dimensions but the last counted through in order) at most 1024 rows name the same one
- attn_gain: float32 [2048], replicated, may hold values from 0.5 to 1.5
- w_query: bfloat16 [2048, 2048], P(None, 'tp'), may hold values from -0.125 to 0.125
- w_key: bfloat16 [2048, 2048], P(None, 'tp'), may hold values from -0.125 to 0.125
- w_value: bfloat16 [2048, 2048], P(None, 'tp'), may hold values from -0.125 to 0.125
- query_gain: float32 [2048], P('tp'), may hold values from 0.1 to 1.9
- key_gain: float32 [2048], P('tp'), may hold values from 0.1 to 1.9
- w_out: bfloat16 [2048, 2048], P('tp'), may hold values from -2 to 2
- ffn_gain: float32 [2048], replicated, may hold values from 0.5 to 1.5
- router: bfloat16 [2048, 16], replicated, may hold values from -0.0625 to 0.0625
- w_gate: bfloat16 [16, 2048, 1024], P('tp'), may hold values from -0.125 to 0.125
- w_up: bfloat16 [16, 2048, 1024], P('tp'), may hold values from -0.125 to 0.125
- w_down: bfloat16 [16, 1024, 2048], P('tp'), may hold values from -1.5859375 to 1.5859375
- cotangent: bfloat16 [2048, 4, 2048], P('sq', None, 'tp'), may hold values from -6 to 6
Outputs:
- output: bfloat16 [2048, 4, 2048], P('sq', None, 'tp')
- input_grad: float32 [2048, 4, 2048], P('sq', None, 'tp')
- attn_gain_grad: float32 [2048], replicated
- w_query_grad: float32 [2048, 2048], P('sq', 'tp')
- w_key_grad: float32 [2048, 2048], P('sq', 'tp')
- w_value_grad: float32 [2048, 2048], P('sq', 'tp')
- query_gain_grad: float32 [2048], replicated
- key_gain_grad: float32 [2048], replicated
- w_out_grad: float32 [2048, 2048], P('tp', 'sq')
- ffn_gain_grad: float32 [2048], replicated
- router_grad: float32 [2048, 16], replicated
- w_gate_grad: float32 [16, 2048, 1024], P('tp', 'sq')
- w_up_grad: float32 [16, 2048, 1024], P('tp', 'sq')
- w_down_grad: float32 [16, 1024, 2048], P('tp', None, 'sq')
The draws below stay inside these ranges and needn't reach their ends.
Inputs may be any that keep to these rules, and one draw needn't show every extreme that they name: `routes`: each row names 8 different experts. In the rows of one index of sq (aligned blocks of 1024 rows in the array's order) no expert is named by more than 1024 rows, a bound that some block reaches. `lengths`: positions at or past a sequence's length are padding: no query attends to them. Some sequence has all 2048 positions valid.
All inputs are finite; a program needn't handle non-finite values.
Results may differ from the reference program's by a relative error of at most 0.028.
Values may be sent and summed in bfloat16 or wider, within the bound.
No kernel may reach another device: no remote copies, remote signals or barrier semaphores. Data moves between devices by JAX's collectives and lax.ppermute only.
A program may use at most 512 MiB of HBM per device.

```python
import math
import jax
import jax.numpy as jnp
import numpy as np
from jax import lax

D = 2048
HEADS = 16
HD = 128
FF = 1024
TOP = 8
EXPERTS = 16
L_DEV = 256
SEQS = 4
LEN = 2048
CAP = 1024
N_SQ = 8


def draw_lengths(key, part):
    key = jax.random.fold_in(key, 7)
    first_key, second_key = jax.random.split(key)
    spread = jax.random.randint(first_key, (SEQS,), LEN // 8, LEN)
    longest = jax.random.randint(second_key, (), 0, SEQS)
    return jnp.where(jnp.arange(SEQS) == longest, LEN, spread).astype(jnp.int32)


def levels(rng, extent, cuts, smallest, high):
    factor_of, own = 1.0, jax.random.fold_in(rng, 6)
    for dim, blocks in cuts:
        heights = jnp.exp(jax.random.uniform(jax.random.fold_in(own, dim), (blocks,), jnp.float32, smallest / len(cuts), high / len(cuts)))
        factor_of = factor_of * jnp.repeat(heights, extent[dim] // blocks).reshape([-1 if axis == dim else 1 for axis in range(len(extent))])
    return factor_of


def assign_block(own_key, own, number, rows, amount, top, reach, skew):
    order = jax.random.permutation(own_key, amount)
    crowded, usual = portions_of(amount, rows * top, reach, skew, True), portions_of(amount, rows * top, reach, skew, False)
    places = jnp.arange(amount)

    def named(tallies, rotation):
        used = int((tallies > 0).sum())
        fixed = max(1, used // 4)
        passed = fixed + (places - fixed + rotation * (used - fixed)) % max(1, amount - fixed)
        return jnp.zeros((amount,), jnp.int32).at[order[jnp.where(places < fixed, places, passed)]].set(jnp.asarray(tallies, jnp.int32))

    tallies = jnp.where(number % 4 == 0, named(crowded, number // 4), named(usual, number - number // 4 - 1))
    mixed = jax.random.permutation(jax.random.fold_in(own, 3), amount)
    giver, receiver = mixed[0:amount // 2 * 2:2], mixed[1:amount // 2 * 2:2]
    room = jnp.minimum(tallies[giver] - 1, reach - tallies[receiver]) // 2
    room = jnp.where((giver == order[0]) | (receiver == order[0]) | (tallies[receiver] == 0), 0, jnp.maximum(room, 0))
    passed = jax.random.randint(jax.random.fold_in(own, 4), (amount // 2,), 0, 1 << 20) % (room + 1)
    tallies = tallies.at[giver].add(-passed).at[receiver].add(passed)
    items = jnp.searchsorted(jnp.cumsum(tallies), jnp.arange(rows * top), side="right").astype(jnp.int32)
    table = items.reshape(top, rows).T
    table = table[jax.random.permutation(jax.random.fold_in(own, 1), rows)]
    rotation = jax.random.randint(jax.random.fold_in(own, 2), (rows, 1), 0, top)
    return jnp.take_along_axis(table, (jnp.arange(top)[None, :] + rotation) % top, axis=1)


def portions_of(number_of, total, most, skew, full):
    portions = [(1 << 20) // math.isqrt(rank ** skew) + 1 for rank in range(1, number_of + 1)]
    largest = most if full else min(most, max(-(-total // number_of), total * portions[0] // sum(portions)))
    least = 1 if total - largest >= number_of - 1 else 0
    given, spare = [largest] + [least] * (number_of - 1), total - largest - least * (number_of - 1)
    while spare > 0:
        free = [i for i in range(1, number_of) if given[i] < largest] or [i for i in range(1, number_of) if given[i] < most]
        mass, remaining = sum([portions[i] for i in free]), spare
        for i in free:
            more = min(most - given[i], max(1, remaining * portions[i] // mass), spare)
            given[i] = given[i] + more
            spare = spare - more
    return np.array(given)


def centred(stream_key, extent, width, reach, cuts=(), kind=jnp.bfloat16):
    entries = width * jax.random.normal(stream_key, extent, jnp.float32)
    if cuts:
        entries = entries * levels(stream_key, extent, cuts, -0.22, 0.18)
    return jnp.clip(entries, -reach, reach).astype(kind)


def setup_inputs(seed: int = 0) -> dict:
    streams_of = jax.random.split(jax.random.key(seed), 17)
    inputs = centred(streams_of[0], (LEN, SEQS, D), 1.0, 6.0, ((0, 8), (2, 4)))
    lengths = draw_lengths(jax.random.fold_in(streams_of[16], 71), 0)
    routes_keys = jax.random.split(jax.random.fold_in(streams_of[2], 1), LEN * SEQS // (L_DEV * SEQS))
    routes_turns = jax.random.permutation(jax.random.fold_in(streams_of[2], 3), LEN * SEQS // (L_DEV * SEQS))
    routes = jax.vmap(lambda own, number: assign_block(jax.random.fold_in(streams_of[2], 2), own, number, L_DEV * SEQS, EXPERTS, TOP, CAP, 1))(routes_keys, routes_turns).reshape((LEN, SEQS, TOP))
    attn_gain = jnp.clip(1.0 + 0.1 * jax.random.normal(streams_of[3], (D,), jnp.float32), 0.5, 1.5)
    w_query = centred(streams_of[4], (D, HEADS * HD), D ** -0.5, 0.125, ((1, 4),))
    w_key = centred(streams_of[5], (D, HEADS * HD), D ** -0.5, 0.125, ((1, 4),))
    w_value = centred(streams_of[6], (D, HEADS * HD), D ** -0.5, 0.125, ((1, 4),))
    query_gain = jnp.clip(1.0 + 0.18 * jax.random.normal(streams_of[7], (HEADS * HD,), jnp.float32), 0.1, 1.9)
    key_gain = jnp.clip(1.0 + 0.18 * jax.random.normal(streams_of[8], (HEADS * HD,), jnp.float32), 0.1, 1.9)
    w_out = centred(streams_of[9], (HEADS * HD, D), (max(1, HEADS * HD // 256)) ** -0.5, 2.0, ((0, 4),))
    ffn_gain = jnp.clip(1.0 + 0.1 * jax.random.normal(streams_of[10], (D,), jnp.float32), 0.5, 1.5)
    router = centred(streams_of[11], (D, EXPERTS), (4 * D) ** -0.5, 0.0625)
    w_gate = centred(streams_of[12], (EXPERTS, D, FF), D ** -0.5, 0.125, ((0, 4),))
    w_up = centred(streams_of[13], (EXPERTS, D, FF), D ** -0.5, 0.125, ((0, 4),))
    w_down = centred(streams_of[14], (EXPERTS, FF, D), (1.5 * EXPERTS * (TOP * FF) ** -0.5), 1.5859375, ((0, 4),))
    cotangent = centred(streams_of[15], (LEN, SEQS, D), 1.0, 6.0, ((0, 8), (2, 4)))
    return {"inputs": inputs, "lengths": lengths, "routes": routes, "attn_gain": attn_gain, "w_query": w_query, "w_key": w_key, "w_value": w_value, "query_gain": query_gain, "key_gain": key_gain, "w_out": w_out, "ffn_gain": ffn_gain, "router": router, "w_gate": w_gate, "w_up": w_up, "w_down": w_down, "cotangent": cotangent}


EPSILON = 1e-05
ROTARY_BASE = 10000.0
NEGATIVE = -1e+30
HIGHEST = lax.Precision.HIGHEST

@jax.custom_vjp
def low(v):
    return lax.optimization_barrier(v.astype(jnp.bfloat16)).astype(jnp.float32)

@jax.custom_vjp
def low_back(v):
    return v

def low_keep(v):
    return (low(v), None)

def low_pass(kept, grad):
    return (grad,)

def back_keep(v):
    return (v, None)

def back_low(kept, grad):
    return (low(grad),)
low.defvjp(low_keep, low_pass)
low_back.defvjp(back_keep, back_low)

def rms_norm(values, gain):
    return values * lax.rsqrt(lax.optimization_barrier(jnp.mean(values * values, axis=-1, keepdims=True)) + EPSILON) * gain

def rotary_tables(positions, head_size):
    exponent = jnp.arange(head_size // 2, dtype=jnp.float32) * 2.0 / head_size
    frequency = ROTARY_BASE ** (-exponent)
    angles = positions.astype(jnp.float32)[:, None] * frequency[None, :]
    cosine = jnp.concatenate([jnp.cos(angles), jnp.cos(angles)], axis=-1)
    sine_table = jnp.concatenate([jnp.sin(angles), jnp.sin(angles)], axis=-1)
    return (cosine, sine_table)

def rotate_forward(values, cosine, sine_table):
    half_width = values.shape[-1] // 2
    turned = jnp.concatenate([-values[..., half_width:], values[..., :half_width]], axis=-1)
    return values * cosine[:, None, None, :] + turned * sine_table[:, None, None, :]

def project(left, right):
    return jnp.einsum('psd,de->pse', left, right, precision=HIGHEST)

def attend_sequence(packed):
    queries, keys, values, length = packed
    positions = jnp.arange(queries.shape[0], dtype=jnp.int32)
    scores = low_back(jnp.einsum('qhd,khd->hqk', queries, keys, precision=HIGHEST) * HD ** (-0.5))
    allowed = (positions[None, :] <= positions[:, None]) & (positions[None, :] < length)
    weights = jax.nn.softmax(jnp.where(allowed[None], scores, NEGATIVE), axis=-1)
    return jnp.einsum('hqk,khd->qhd', low(weights), values, precision=HIGHEST)

def layer(params, lengths, routes):
    rows, attn_gain, w_query, w_key, w_value, query_gain, key_gain, w_out, ffn_gain, router, w_gate, w_up, w_down = params
    length_all, seq_count, model_width = rows.shape
    attn_in = low(rms_norm(rows, attn_gain))
    query_raw = low_back(project(attn_in, w_query))
    key_raw = low_back(project(attn_in, w_key))
    value_low = low_back(low(project(attn_in, w_value)))
    head_shape = (length_all, seq_count, HEADS, HD)
    cosine, sine_table = rotary_tables(jnp.arange(length_all, dtype=jnp.int32), HD)
    query_low = low_back(low(rotate_forward(rms_norm(query_raw, query_gain).reshape(head_shape), cosine, sine_table)))
    key_low = low_back(low(rotate_forward(rms_norm(key_raw, key_gain).reshape(head_shape), cosine, sine_table)))
    value_heads = value_low.reshape(head_shape)
    attended = lax.map(jax.checkpoint(attend_sequence), (jnp.transpose(query_low, (1, 0, 2, 3)), jnp.transpose(key_low, (1, 0, 2, 3)), jnp.transpose(value_heads, (1, 0, 2, 3)), lengths))
    attn_low = low_back(low(jnp.transpose(attended, (1, 0, 2, 3)).reshape(length_all, seq_count, HEADS * HD)))
    middle = rows + low_back(project(attn_low, w_out))
    ffn_in = low(rms_norm(middle, ffn_gain))
    token_count = length_all * seq_count
    flat_in = ffn_in.reshape(token_count, model_width)
    probabilities = jax.nn.softmax(jnp.dot(flat_in, router, precision=HIGHEST), axis=-1)
    flat_routes = routes.reshape(token_count, TOP)
    chosen = jnp.take_along_axis(probabilities, flat_routes, axis=1)
    token_ids = jnp.arange(token_count, dtype=jnp.int32)
    slot_count = CAP * N_SQ

    def expert_step(mixture, packed):
        expert_id, gate_w, up_w, down_w = packed
        matched = flat_routes == expert_id
        present = jnp.any(matched, axis=1)
        gate_value = lax.optimization_barrier(jnp.sum(jnp.where(matched, chosen, 0.0), axis=1))
        ordinal = jnp.cumsum(present.astype(jnp.int32), dtype=jnp.int32) - 1
        target = jnp.where(present, ordinal, slot_count)
        slot_rows = jnp.zeros((slot_count,), jnp.int32).at[target].set(token_ids, mode='drop')
        slot_gate = jnp.zeros((slot_count,), jnp.float32).at[target].set(gate_value, mode='drop')
        expert_in = flat_in[slot_rows]
        gate_pre = low_back(jnp.dot(expert_in, gate_w, precision=HIGHEST))
        up_pre = low_back(jnp.dot(expert_in, up_w, precision=HIGHEST))
        hidden_low = low_back(low(jax.nn.silu(gate_pre) * up_pre))
        expert_out = low_back(jnp.dot(hidden_low, down_w, precision=HIGHEST))
        return (mixture.at[slot_rows].add(slot_gate[:, None] * expert_out), None)
    mixture, _ = lax.scan(jax.checkpoint(expert_step), jnp.zeros((token_count, model_width), jnp.float32), (jnp.arange(EXPERTS, dtype=jnp.int32), w_gate, w_up, w_down))
    return middle + mixture.reshape(length_all, seq_count, model_width)

def reference(inputs, lengths, routes, attn_gain, w_query, w_key, w_value, query_gain, key_gain, w_out, ffn_gain, router, w_gate, w_up, w_down, cotangent):
    params = tuple((array_in.astype(jnp.float32) for array_in in (inputs, attn_gain, w_query, w_key, w_value, query_gain, key_gain, w_out, ffn_gain, router, w_gate, w_up, w_down)))

    def forward(packed):
        return layer(packed, lengths, routes)
    result, pullback = jax.vjp(forward, params)
    gradients = pullback(cotangent.astype(jnp.float32))[0]
    return (result.astype(jnp.bfloat16), gradients[0], gradients[1], gradients[2], gradients[3], gradients[4], gradients[5], gradients[6], gradients[7], gradients[8], gradients[9], gradients[10], gradients[11], gradients[12])
```

```python
import functools

import jax
import jax.numpy as jnp
from jax import lax
from jax.experimental import pallas as pl
from jax.experimental.pallas import tpu as pltpu
from jax.sharding import PartitionSpec as P

HD = 128
EPSILON = 1e-05
ROTARY_BASE = 10000.0
NEGATIVE = -1e30
F32 = jnp.float32
BF16 = jnp.bfloat16
VMEM_LIMIT = 56 * 1024 * 1024
CHUNKS = 2
NT = (((1,), (1,)), ((), ()))
TN = (((0,), (0,)), ((), ()))
NN = (((1,), (0,)), ((), ()))


def dot(left, right, dims=NN):
    return lax.dot_general(left, right, dims, preferred_element_type=F32)


def pick(which, cases):
    return lax.select_n(which, *cases) if len(cases) > 1 else cases[0]


def shift(block, axis, distance):
    count = lax.axis_size(axis)
    return lax.ppermute(block, axis, [(i, (i + distance) % count) for i in range(count)])


def swap(block, axis, mask):
    return lax.ppermute(block, axis, [(i, i ^ mask) for i in range(lax.axis_size(axis))])


def gather_chain(block, axis):
    count, place = lax.axis_size(axis), lax.axis_index(axis)
    right, left = [block], [block]
    for t in range(1, count):
        right.append(lax.ppermute(right[-1], axis, [(i, i + 1) for i in range(t - 1, count - 1)]))
        left.append(lax.ppermute(left[-1], axis, [(i + 1, i) for i in range(count - t)]))
    return [
        pick(place, [right[p - f] if p >= f else left[f - p] for p in range(count)])
        for f in range(count)
    ]


def exchange(part_of, axis):
    count, place = lax.axis_size(axis), lax.axis_index(axis)
    got = [part_of(place)]
    for k in range(1, count):
        got.append(shift(part_of((place + k) % count), axis, k))
    return got


def exchange_sum(part_of, axis):
    total = None
    for part in exchange(part_of, axis):
        total = part.astype(F32) if total is None else total + part.astype(F32)
    return total


def exchange_ordered(part_of, axis):
    count, place = lax.axis_size(axis), lax.axis_index(axis)
    got = exchange(part_of, axis)
    return [pick(place, [got[(p - f) % count] for p in range(count)]) for f in range(count)]


def butterfly(value, axis):
    mask = 1
    while mask < lax.axis_size(axis):
        value = value + swap(value, axis, mask)
        mask *= 2
    return value


def block_of(array, index, size, axis):
    return lax.dynamic_slice_in_dim(array, index * size, size, axis)


def relative(array, axis_name, width):
    count, place = lax.axis_size(axis_name), lax.axis_index(axis_name)
    return [block_of(array, place ^ m, width, 1) for m in range(count)]


def reduce_blocks(rel, right):
    count = len(rel)
    width = rel[0].shape[1]
    if count == 1:
        return dot(rel[0], right, TN)
    odd = jnp.concatenate([rel[m] for m in range(1, count, 2)], axis=1)
    even = jnp.concatenate([rel[m] for m in range(0, count, 2)], axis=1)
    received = swap(dot(odd, right, TN).astype(BF16), "sq", 1)
    own = (dot(even, right, TN) + received.astype(F32)).astype(BF16)
    columns = right.shape[1]
    own = own.reshape(count // 2, width, columns)
    half = columns // 2
    results = []
    for part in range(2):
        blocks = own[:, :, part * half : (part + 1) * half]
        steps = [1 << b for b in range((count // 2).bit_length() - 1)]
        if part:
            steps = steps[::-1]
        kept = {m: blocks[m] for m in range(count // 2)}
        for number, step in enumerate(steps):
            give = sorted(m for m in kept if m & step)
            keep = sorted(m for m in kept if not m & step)
            got = swap(jnp.stack([kept[m] for m in give]), "sq", 2 * step)
            last = number == len(steps) - 1
            kept = {
                m: (kept[m].astype(F32) + got[i].astype(F32)).astype(F32 if last else BF16)
                for i, m in enumerate(keep)
            }
        results.append(kept[0])
    return jnp.concatenate(results, axis=1).astype(F32)


def attn_forward_kernel(slots, info, q_ref, *refs):
    kv_refs, (low_ref, full_ref, lse_ref), (top, total, accum) = (
        refs[:slots],
        refs[slots : slots + 3],
        refs[slots + 3 :],
    )
    rank = info[0]
    length = info[1 + pl.program_id(0)]
    queries = q_ref[0]
    size = queries.shape[0]
    top[...] = jnp.full(top.shape, NEGATIVE, F32)
    total[...] = jnp.zeros(total.shape, F32)
    accum[...] = jnp.zeros(accum.shape, F32)
    key_row = lax.broadcasted_iota(jnp.int32, (size, size), 0)
    query_col = lax.broadcasted_iota(jnp.int32, (size, size), 1)
    for slot in range(slots):
        block = rank ^ slot
        start = block * size

        @pl.when((block <= rank) & (start < length))
        def _(slot=slot, start=start):
            scores = dot(kv_refs[slot][0, 0], queries, NT) * HD**-0.5
            allowed = key_row + start < length
            if slot == 0:
                allowed = allowed & (key_row <= query_col)
            scores = jnp.where(allowed, scores, NEGATIVE)
            newest = jnp.maximum(top[...], jnp.max(scores, axis=0, keepdims=True))
            weights = jnp.exp(scores - newest)
            factor = jnp.exp(top[...] - newest)
            top[...] = newest
            total[...] = total[...] * factor + jnp.sum(weights, axis=0, keepdims=True)
            accum[...] = accum[...] * factor + dot(
                kv_refs[slot][1, 0], weights.astype(BF16), TN
            )

    result = (accum[...] / total[...]).T
    full_ref[0] = result
    low_ref[0] = result.astype(BF16)
    lse_ref[0, 0] = top[...] + jnp.log(total[...])


def attn_forward(info, queries, kv_slots):
    seqs, size, columns = queries.shape
    heads = columns // HD
    slots = len(kv_slots)
    row_spec = pl.BlockSpec((1, size, HD), lambda s, h, info: (s, 0, h))
    kv_spec = pl.BlockSpec((2, 1, size, HD), lambda s, h, info: (0, s, 0, h))
    lse_spec = pl.BlockSpec((1, 1, 1, size), lambda s, h, info: (s, h, 0, 0))
    return pl.pallas_call(
        functools.partial(attn_forward_kernel, slots),
        grid_spec=pltpu.PrefetchScalarGridSpec(
            num_scalar_prefetch=1,
            grid=(seqs, heads),
            in_specs=[row_spec] + [kv_spec] * slots,
            out_specs=[row_spec, row_spec, lse_spec],
            scratch_shapes=[
                pltpu.VMEM((1, size), F32),
                pltpu.VMEM((1, size), F32),
                pltpu.VMEM((HD, size), F32),
            ],
        ),
        out_shape=[
            jax.ShapeDtypeStruct(queries.shape, BF16),
            jax.ShapeDtypeStruct(queries.shape, F32),
            jax.ShapeDtypeStruct((seqs, heads, 1, size), F32),
        ],
        compiler_params=pltpu.CompilerParams(vmem_limit_bytes=VMEM_LIMIT),
        cost_estimate=pl.CostEstimate(
            flops=4 * seqs * heads * slots * size * size * HD,
            bytes_accessed=4 * seqs * size * columns * (slots + 2),
            transcendentals=seqs * heads * slots * size * size,
        ),
        name="attn_forward",
    )(info, queries, *kv_slots)


def attn_backward_kernel(slots, info, q_ref, grad_ref, full_ref, lse_ref, *refs):
    kv_refs, (dq_ref, even_ref, odd_ref), (accum,) = (
        refs[:slots],
        refs[slots : slots + 3],
        refs[slots + 3 :],
    )
    rank = info[0]
    length = info[1 + pl.program_id(0)]
    queries, grads = q_ref[0], grad_ref[0]
    size = queries.shape[0]
    lse = lse_ref[0, 0]
    delta = jnp.sum((grads.astype(F32) * full_ref[0]).T, axis=0, keepdims=True)
    accum[...] = jnp.zeros(accum.shape, F32)
    key_row = lax.broadcasted_iota(jnp.int32, (size, size), 0)
    query_col = lax.broadcasted_iota(jnp.int32, (size, size), 1)
    for slot in range(slots):
        block = rank ^ slot
        start = block * size
        out_ref = odd_ref if slot % 2 else even_ref
        live = (block <= rank) & (start < length)

        @pl.when(live)
        def _(slot=slot, start=start, out_ref=out_ref):
            keys, values = kv_refs[slot][0, 0], kv_refs[slot][1, 0]
            scores = dot(keys, queries, NT) * HD**-0.5
            allowed = key_row + start < length
            if slot == 0:
                allowed = allowed & (key_row <= query_col)
            weights = jnp.where(allowed, jnp.exp(scores - lse), 0.0)
            back = dot(values, grads, NT)
            score_grad = (weights * (back - delta)).astype(BF16)
            out_ref[slot // 2, 1, 0] = dot(weights.astype(BF16), grads).astype(BF16)
            out_ref[slot // 2, 0, 0] = (dot(score_grad, queries) * HD**-0.5).astype(BF16)
            accum[...] += dot(score_grad, keys, TN)

        @pl.when(jnp.logical_not(live))
        def _(slot=slot, out_ref=out_ref):
            out_ref[slot // 2, :, 0] = jnp.zeros((2,) + queries.shape, BF16)

    dq_ref[0] = (accum[...] * HD**-0.5).astype(BF16)


def attn_backward(info, queries, grads, full, lse, kv_slots):
    seqs, size, columns = queries.shape
    heads = columns // HD
    slots = len(kv_slots)
    row_spec = pl.BlockSpec((1, size, HD), lambda s, h, info: (s, 0, h))
    kv_spec = pl.BlockSpec((2, 1, size, HD), lambda s, h, info: (0, s, 0, h))
    lse_spec = pl.BlockSpec((1, 1, 1, size), lambda s, h, info: (s, h, 0, 0))
    out_spec = pl.BlockSpec((slots // 2, 2, 1, size, HD), lambda s, h, info: (0, 0, s, 0, h))
    out_shape = jax.ShapeDtypeStruct((slots // 2, 2, seqs, size, columns), BF16)
    return pl.pallas_call(
        functools.partial(attn_backward_kernel, slots),
        grid_spec=pltpu.PrefetchScalarGridSpec(
            num_scalar_prefetch=1,
            grid=(seqs, heads),
            in_specs=[row_spec, row_spec, row_spec, lse_spec] + [kv_spec] * slots,
            out_specs=[row_spec, out_spec, out_spec],
            scratch_shapes=[pltpu.VMEM((size, HD), F32)],
        ),
        out_shape=[jax.ShapeDtypeStruct(queries.shape, BF16), out_shape, out_shape],
        compiler_params=pltpu.CompilerParams(vmem_limit_bytes=VMEM_LIMIT),
        cost_estimate=pl.CostEstimate(
            flops=10 * seqs * heads * slots * size * size * HD,
            bytes_accessed=8 * seqs * size * columns * (slots + 2),
            transcendentals=seqs * heads * slots * size * size,
        ),
        name="attn_backward",
    )(info, queries, grads, full, lse, *kv_slots)


def expert_hidden_kernel(
    tile, x_ref, g_ref, gate_ref, wg_ref, wu_ref, wd_ref, gh_ref, gp_ref, up_ref, gg_ref
):
    expert, block = pl.program_id(0), pl.program_id(1)
    rows = x_ref.shape[0]

    @pl.when((expert == 0) & (block == 0))
    def _():
        gg_ref[...] = jnp.zeros(gg_ref.shape, F32)

    @pl.loop(0, rows // tile)
    def _(i):
        span = pl.ds(pl.multiple_of(i * tile, tile), tile)
        tokens = x_ref[span, :]
        gate_pre = dot(tokens, wg_ref[0])
        up_pre = dot(tokens, wu_ref[0])
        back = dot(g_ref[span, :], wd_ref[0], NT)
        gates = gate_ref[span, :]
        lane = lax.broadcasted_iota(jnp.int32, gates.shape, 1)
        gate = jnp.sum(jnp.where(lane == expert, gates, 0.0), axis=1, keepdims=True)
        sigmoid = 1.0 / (1.0 + jnp.exp(-gate_pre))
        silu = gate_pre * sigmoid
        hidden = silu * up_pre
        inner = jnp.sum(hidden * back, axis=1, keepdims=True)
        gg_ref[span, :] += jnp.where(lane == expert, inner, 0.0)
        gh_ref[span, :] = (gate * hidden).astype(BF16)
        hidden_grad = gate * back
        gp_ref[span, :] = (
            hidden_grad * up_pre * (sigmoid + silu * (1.0 - sigmoid))
        ).astype(BF16)
        up_ref[span, :] = (hidden_grad * silu).astype(BF16)


def expert_hidden(tokens, grads, gates, w_gate, w_up, w_down):
    rows, width = tokens.shape
    experts, _, units = w_gate.shape
    cols = min(256, units)
    tile = min(512, rows)
    whole = pl.BlockSpec((rows, width), lambda e, f: (0, 0), pipeline_mode=pl.Buffered(1))
    small = pl.BlockSpec((rows, experts), lambda e, f: (0, 0))
    wide = pl.BlockSpec((1, width, cols), lambda e, f: (e, 0, f))
    tall = pl.BlockSpec((1, cols, width), lambda e, f: (e, f, 0))
    result = pl.BlockSpec((rows, cols), lambda e, f: (0, e * (units // cols) + f))
    out = jax.ShapeDtypeStruct((rows, experts * units), BF16)
    return pl.pallas_call(
        functools.partial(expert_hidden_kernel, tile),
        grid=(experts, units // cols),
        in_specs=[whole, whole, small, wide, wide, tall],
        out_specs=[result, result, result, small],
        out_shape=[out, out, out, jax.ShapeDtypeStruct((rows, experts), F32)],
        compiler_params=pltpu.CompilerParams(vmem_limit_bytes=VMEM_LIMIT),
        cost_estimate=pl.CostEstimate(
            flops=6 * rows * width * experts * units,
            bytes_accessed=6 * width * experts * units + 6 * rows * experts * units,
            transcendentals=rows * experts * units,
        ),
        name="expert_hidden",
    )(tokens, grads, gates, w_gate, w_up, w_down)


def expert_back_kernel(gp_ref, up_ref, lg_ref, router_ref, wg_ref, wu_ref, out_ref, accum):
    expert = pl.program_id(1)

    @pl.when(expert == 0)
    def _():
        accum[...] = lax.dot_general(
            lg_ref[...],
            router_ref[...].astype(F32),
            NT,
            precision=lax.Precision.HIGHEST,
            preferred_element_type=F32,
        )

    accum[...] += dot(gp_ref[...], wg_ref[0], NT) + dot(up_ref[...], wu_ref[0], NT)

    @pl.when(expert == pl.num_programs(1) - 1)
    def _():
        out_ref[...] = accum[...].astype(BF16)


def expert_back(gate_grads, up_grads, logit_grads, router, w_gate, w_up):
    rows = gate_grads.shape[0]
    experts, width, units = w_gate.shape
    total = router.shape[1]
    cols = min(512, width)
    left = pl.BlockSpec((rows, units), lambda d, e: (0, e))
    weight = pl.BlockSpec((1, cols, units), lambda d, e: (e, d, 0))
    return pl.pallas_call(
        expert_back_kernel,
        grid=(width // cols, experts),
        in_specs=[
            left,
            left,
            pl.BlockSpec((rows, total), lambda d, e: (0, 0)),
            pl.BlockSpec((cols, total), lambda d, e: (d, 0)),
            weight,
            weight,
        ],
        out_specs=pl.BlockSpec((rows, cols), lambda d, e: (0, d)),
        out_shape=jax.ShapeDtypeStruct((rows, width), BF16),
        scratch_shapes=[pltpu.VMEM((rows, cols), F32)],
        compiler_params=pltpu.CompilerParams(vmem_limit_bytes=VMEM_LIMIT),
        cost_estimate=pl.CostEstimate(
            flops=4 * rows * width * experts * units,
            bytes_accessed=4 * width * experts * units + 20 * rows * experts * units,
            transcendentals=0,
        ),
        name="expert_back",
    )(gate_grads, up_grads, logit_grads, router, w_gate, w_up)


def rotary_tables(positions):
    exponent = jnp.arange(HD // 2, dtype=F32) * 2.0 / HD
    frequency = ROTARY_BASE ** (-exponent)
    angles = positions.astype(F32)[:, None] * frequency[None, :]
    cosine = jnp.concatenate([jnp.cos(angles), jnp.cos(angles)], axis=-1)
    sine = jnp.concatenate([jnp.sin(angles), jnp.sin(angles)], axis=-1)
    return cosine, sine


def rotate_forward(values, cosine, sine):
    half = HD // 2
    turned = jnp.concatenate([-values[..., half:], values[..., :half]], axis=-1)
    return values * cosine[None, :, None, :] + turned * sine[None, :, None, :]


def rotate_backward(grads, cosine, sine):
    half = HD // 2
    scaled = grads * sine[None, :, None, :]
    turned = jnp.concatenate([scaled[..., half:], -scaled[..., :half]], axis=-1)
    return grads * cosine[None, :, None, :] + turned


def gather_sq(block):
    count = lax.axis_size("sq")
    slots = [None] * count
    for m in range(0, count, 2):
        slots[m] = block if m == 0 else swap(block, "sq", m)
    for m in range(0, count, 2):
        if count > 1:
            slots[m + 1] = swap(slots[m], "sq", 1)
    return slots


def scatter_sq(even, odd):
    received = swap(odd, "sq", 1)
    total = None
    for k in range(even.shape[0]):
        part = (even[k].astype(F32) + received[k].astype(F32)).astype(BF16)
        part = part if k == 0 else swap(part, "sq", 2 * k)
        total = part.astype(F32) if total is None else total + part.astype(F32)
    return total


def shards(
    inputs,
    lengths,
    routes,
    attn_gain,
    w_query,
    w_key,
    w_value,
    query_gain,
    key_gain,
    w_out,
    ffn_gain,
    router,
    w_gate,
    w_up,
    w_down,
    cotangent,
):
    size, seqs, feat = inputs.shape
    width, head_cols = w_query.shape
    heads = head_cols // HD
    tp_rank, tp_count = lax.axis_index("tp"), lax.axis_size("tp")
    sq_rank, sq_count = lax.axis_index("sq"), lax.axis_size("sq")
    experts = w_gate.shape[0]
    experts_total = router.shape[1]
    all_cols = head_cols * tp_count
    block = width // sq_count
    chunks = CHUNKS
    per = seqs // chunks
    rows_n = per * size
    quarter = rows_n // tp_count
    positions = sq_rank * size + jnp.arange(size, dtype=jnp.int32)
    cosine, sine = rotary_tables(positions)
    group = lambda array: [
        array[:, c * per : (c + 1) * per].transpose(1, 0, 2) for c in range(chunks)
    ]
    inputs_c, cotangent_c, routes_c = group(inputs), group(cotangent), group(routes)
    info_c = [
        jnp.concatenate([sq_rank[None], lengths[c * per : (c + 1) * per]]).astype(jnp.int32)
        for c in range(chunks)
    ]

    slab = w_out.shape[0] // sq_count
    w_out_all = lax.all_gather(
        block_of(w_out, sq_rank, slab, 0), ("tp", "sq"), axis=0, tiled=True
    )

    w_qkv = jnp.concatenate([w_query, w_key, w_value], axis=1)

    def attention_in(c):
        pieces = gather_chain(inputs_c[c].reshape(rows_n, feat), "tp")
        low = jnp.concatenate(pieces, axis=1)
        rows = low.astype(F32)
        inv = lax.rsqrt(jnp.mean(rows * rows, axis=1, keepdims=True) + EPSILON)
        normed = (rows * inv * attn_gain).astype(BF16)
        qkv = dot(normed, w_qkv)
        query_raw, key_raw = qkv[:, :head_cols], qkv[:, head_cols : 2 * head_cols]
        value = qkv[:, 2 * head_cols :].astype(BF16)
        squares = jnp.stack(
            [jnp.sum(query_raw * query_raw, axis=1), jnp.sum(key_raw * key_raw, axis=1)]
        )
        squares = butterfly(squares, "tp")
        inv_qk = lax.rsqrt(squares / all_cols + EPSILON)
        query_hat = query_raw * inv_qk[0][:, None]
        key_hat = key_raw * inv_qk[1][:, None]
        shape = (per, size, heads, HD)
        turn = lambda hat, gain: (
            rotate_forward((hat * gain).reshape(shape), cosine, sine)
            .astype(BF16)
            .reshape(per, size, head_cols)
        )
        queries = turn(query_hat, query_gain)
        keys = turn(key_hat, key_gain)
        pair = jnp.stack([keys, value.reshape(per, size, head_cols)])
        return low, inv, normed, query_raw, key_raw, inv_qk, queries, pair

    ins = [attention_in(c) for c in range(chunks)]
    slots_c = [gather_sq(ins[c][7]) for c in range(chunks)]
    attn_c = [attn_forward(info_c[c], ins[c][6], slots_c[c]) for c in range(chunks)]

    grad_c = [
        jnp.concatenate(gather_chain(cotangent_c[c].reshape(rows_n, feat), "tp"), axis=1)
        for c in range(chunks)
    ]

    def middle_of(c):
        low = ins[c][0]
        attn_all = jnp.concatenate(
            gather_chain(attn_c[c][0].reshape(rows_n, head_cols), "tp"), axis=1
        )
        middle = low.astype(F32) + dot(attn_all, w_out_all)
        inv = lax.rsqrt(jnp.mean(middle * middle, axis=1, keepdims=True) + EPSILON)
        ffn_in = (middle * inv * ffn_gain).astype(BF16)
        probs = jax.nn.softmax(dot(ffn_in, router), axis=1)
        flat_routes = routes_c[c].reshape(rows_n, -1)
        ids = jnp.arange(experts_total, dtype=jnp.int32)
        routed = functools.reduce(
            jnp.logical_or,
            [flat_routes[:, r : r + 1] == ids[None, :] for r in range(flat_routes.shape[1])],
        )
        gates = jnp.where(routed, probs, 0.0)
        own = block_of(gates, tp_rank, experts, 1)
        return attn_all, middle, inv, ffn_in, probs, routed, own

    mids = [middle_of(c) for c in range(chunks)]

    def expert_part(c):
        _, _, _, ffn_in, probs, routed, own = mids[c]
        hidden, gate_grads, up_grads, inner = expert_hidden(
            ffn_in, grad_c[c], own, w_gate, w_up, w_down
        )
        inner = lax.dynamic_update_slice_in_dim(
            jnp.zeros(probs.shape, F32), inner, tp_rank * experts, 1
        )
        prob_grad = jnp.where(routed, inner, 0.0)
        logit_grad = probs * (prob_grad - jnp.sum(probs * prob_grad, axis=1, keepdims=True))
        back = expert_back(gate_grads, up_grads, logit_grad, router, w_gate, w_up)
        return hidden, gate_grads, up_grads, logit_grad, back

    exps = [expert_part(c) for c in range(chunks)]

    def middle_back(c):
        attn_all, middle, inv, _, _, _, _ = mids[c]
        back = exps[c][4]
        ffn_grad = exchange_sum(lambda d: block_of(back, d, quarter, 0), "tp")
        own_middle = block_of(middle, tp_rank, quarter, 0)
        own_inv = block_of(inv, tp_rank, quarter, 0)
        own_grad = block_of(grad_c[c], tp_rank, quarter, 0).astype(F32)
        hat = own_middle * own_inv
        gained = ffn_grad * ffn_gain
        gain_part = jnp.sum(ffn_grad * hat, axis=0)
        middle_grad = own_grad + own_inv * (
            gained - hat * jnp.mean(gained * hat, axis=1, keepdims=True)
        )
        low = middle_grad.astype(BF16)
        attn_grad = dot(low, w_out_all, NT).astype(BF16)
        parts = exchange_ordered(lambda d: block_of(attn_grad, d, head_cols, 1), "tp")
        attn_grad = jnp.concatenate(parts, axis=0).reshape(per, size, head_cols)
        parts = exchange_ordered(lambda d: block_of(low, d, feat, 1), "tp")
        middle_own = jnp.concatenate(parts, axis=0)
        return gain_part, low, attn_grad, middle_own, block_of(attn_all, tp_rank, quarter, 0)

    backs = [middle_back(c) for c in range(chunks)]

    def output_of(c):
        hidden = exps[c][0]
        mixture = dot(hidden, w_down.reshape(-1, width)).astype(BF16)
        total = exchange_sum(lambda d: block_of(mixture, d, feat, 1), "tp")
        own = block_of(mids[c][1], tp_rank, feat, 1)
        return (own + total).astype(BF16).reshape(per, size, feat).transpose(1, 0, 2)

    outputs = [output_of(c) for c in range(chunks)]

    join = lambda parts: parts[0] if len(parts) == 1 else jnp.concatenate(parts, axis=0)
    ffn_all = join([mids[c][3] for c in range(chunks)])
    grad_all = join(grad_c)
    ffn_rel = relative(ffn_all, "sq", block)
    grad_rel = relative(grad_all, "sq", block)
    w_gate_grad = reduce_blocks(ffn_rel, join([exps[c][1] for c in range(chunks)]))
    w_up_grad = reduce_blocks(ffn_rel, join([exps[c][2] for c in range(chunks)]))
    w_down_grad = reduce_blocks(grad_rel, join([exps[c][0] for c in range(chunks)]))
    spread = lambda g: g.reshape(block, experts, -1).transpose(1, 0, 2)
    w_gate_grad, w_up_grad = spread(w_gate_grad), spread(w_up_grad)
    w_down_grad = w_down_grad.T.reshape(experts, -1, block)

    logit_all = join([exps[c][3] for c in range(chunks)])
    router_grad = lax.dot_general(
        logit_all,
        ffn_all.astype(F32),
        TN,
        precision=lax.Precision.HIGHEST,
        preferred_element_type=F32,
    )

    low_rel = relative(join([b[1] for b in backs]), "sq", block)
    out_grad = reduce_blocks(low_rel, join([b[4] for b in backs])).astype(BF16)
    w_out_grad = exchange_sum(lambda d: block_of(out_grad, d, head_cols, 1), "tp").T

    def attention_back(c):
        low, inv, normed, query_raw, key_raw, inv_qk, queries, _ = ins[c]
        _, full, lse = attn_c[c]
        dq, even, odd = attn_backward(info_c[c], queries, backs[c][2], full, lse, slots_c[c])
        dkv = scatter_sq(even, odd).astype(BF16)
        shape = (per, size, heads, HD)
        turn = lambda grad: rotate_backward(
            grad.astype(F32).reshape(shape), cosine, sine
        ).reshape(rows_n, head_cols)
        query_grad, key_grad = turn(dq), turn(dkv[0])
        value_grad = dkv[1].reshape(rows_n, head_cols)
        query_hat = query_raw * inv_qk[0][:, None]
        key_hat = key_raw * inv_qk[1][:, None]
        gained_q, gained_k = query_grad * query_gain, key_grad * key_gain
        stats = jnp.stack(
            [jnp.sum(gained_q * query_hat, axis=1), jnp.sum(gained_k * key_hat, axis=1)]
        )
        stats = butterfly(stats, "tp") / all_cols
        raw_q = (inv_qk[0][:, None] * (gained_q - query_hat * stats[0][:, None])).astype(BF16)
        raw_k = (inv_qk[1][:, None] * (gained_k - key_hat * stats[1][:, None])).astype(BF16)
        gain_q = jnp.sum(query_grad * query_hat, axis=0)
        gain_k = jnp.sum(key_grad * key_hat, axis=0)
        raw = jnp.concatenate([raw_q, raw_k, value_grad], axis=1)
        first = dot(raw, w_qkv, NT)
        hat = low.astype(F32) * inv
        gain_part = jnp.sum(first * hat, axis=0)
        inner = jnp.sum(first * attn_gain * hat, axis=1)
        inner = butterfly(inner, "tp")
        first_low = first.astype(BF16)
        first_own = exchange_sum(lambda d: block_of(first_low, d, feat, 1), "tp")
        hat_own = inputs_c[c].reshape(rows_n, feat).astype(F32) * inv
        gain_own = block_of(attn_gain, tp_rank, feat, 0)
        result = backs[c][3].astype(F32) + inv * (
            gain_own * first_own - hat_own * inner[:, None] / width
        )
        result = result.reshape(per, size, feat).transpose(1, 0, 2)
        return result, raw, gain_q, gain_k, gain_part

    fronts = [attention_back(c) for c in range(chunks)]
    normed_rel = relative(join([ins[c][2] for c in range(chunks)]), "sq", block)
    qkv_grad = reduce_blocks(normed_rel, join([f[1] for f in fronts]))

    tally = lambda parts: functools.reduce(lambda a, b: a + b, parts)
    place = lambda part: lax.dynamic_update_slice_in_dim(
        jnp.zeros((all_cols,), F32), part, tp_rank * head_cols, 0
    )
    early = jnp.concatenate(
        [router_grad, tally([b[0] for b in backs])[None, :]], axis=0
    )
    early = butterfly(butterfly(early, "sq"), "tp")
    late = jnp.stack(
        [
            tally([f[4] for f in fronts]),
            place(tally([f[2] for f in fronts])),
            place(tally([f[3] for f in fronts])),
        ]
    )
    late = butterfly(butterfly(late, "sq"), "tp")
    joined = lambda parts: parts[0] if len(parts) == 1 else jnp.concatenate(parts, axis=1)
    return (
        joined(outputs),
        joined([f[0] for f in fronts]),
        late[0],
        qkv_grad[:, :head_cols],
        qkv_grad[:, head_cols : 2 * head_cols],
        qkv_grad[:, 2 * head_cols :],
        late[1],
        late[2],
        w_out_grad,
        early[experts_total],
        early[:experts_total].T,
        w_gate_grad,
        w_up_grad,
        w_down_grad,
    )


def solution(mesh):
    placed = (
        P("sq", None, "tp"),
        P(),
        P("sq", None, None),
        P(),
        P(None, "tp"),
        P(None, "tp"),
        P(None, "tp"),
        P("tp"),
        P("tp"),
        P("tp", None),
        P(),
        P(),
        P("tp", None, None),
        P("tp", None, None),
        P("tp", None, None),
        P("sq", None, "tp"),
    )
    return jax.shard_map(
        shards,
        mesh=mesh,
        in_specs=placed,
        out_specs=(
            P("sq", None, "tp"),
            P("sq", None, "tp"),
            P(),
            P("sq", "tp"),
            P("sq", "tp"),
            P("sq", "tp"),
            P(),
            P(),
            P("tp", "sq"),
            P(),
            P(),
            P("tp", "sq", None),
            P("tp", "sq", None),
            P("tp", None, "sq"),
        ),
        check_vma=False,
    )
```

```python
import functools

import jax
import jax.numpy as jnp
from jax import lax
from jax.experimental import pallas as pl
from jax.experimental.pallas import tpu as pltpu
from jax.sharding import PartitionSpec as P

HD = 128
EPSILON = 1e-05
ROTARY_BASE = 10000.0
NEGATIVE = -1e30
F32 = jnp.float32
BF16 = jnp.bfloat16
VMEM_LIMIT = 56 * 1024 * 1024
CHUNKS = 2
NT = (((1,), (1,)), ((), ()))
TN = (((0,), (0,)), ((), ()))
NN = (((1,), (0,)), ((), ()))


def dot(left, right, dims=NN):
    return lax.dot_general(left, right, dims, preferred_element_type=F32)


def after(value, *others):
    return lax.optimization_barrier((value, *others))[0]


def shift(block, axis, distance):
    count = lax.axis_size(axis)
    return lax.ppermute(block, axis, [(i, (i + distance) % count) for i in range(count)])


def swap(block, axis, mask):
    return lax.ppermute(block, axis, [(i, i ^ mask) for i in range(lax.axis_size(axis))])


OUTER, INNER = [(0, 1), (1, 0), (2, 3), (3, 2)], [(0, 0), (1, 2), (2, 1), (3, 3)]


def first_step(block):
    count = lax.axis_size("tp")
    if count == 4:
        return [block, lax.ppermute(block, "tp", OUTER), lax.ppermute(block, "tp", INNER)]
    return [block] + [shift(block, "tp", k) for k in range(1, count)]


def second_step(first, *others):
    if lax.axis_size("tp") != 4:
        return []
    _, a1, b1 = first
    return [
        lax.ppermute(after(b1, a1, *others), "tp", OUTER),
        lax.ppermute(after(a1, b1, *others), "tp", INNER),
    ]


def third_step(first, second, *others):
    count = lax.axis_size("tp")
    if count != 4:
        return first, by_distance(count)
    (block, a1, b1), (a2, b2) = first, second
    a3 = lax.ppermute(after(b2, a2, *others), "tp", OUTER)
    return [block, a1, a2, a3, b1, b2], ((0, 1, 2, 3), (1, 0, 4, 5), (5, 4, 0, 1), (3, 2, 1, 0))


def gather_tp(block, second=(), third=()):
    first = first_step(block)
    return third_step(first, second_step(first, *second), *third)


def by_distance(count):
    return tuple(tuple((z - f) % count for f in range(count)) for z in range(count))


def exchange(pieces):
    return [p if k == 0 else shift(p, "tp", k) for k, p in enumerate(pieces)]


def butterfly(value, axis):
    return butterfly_steps(value, axis)[0]


def butterfly_steps(value, axis):
    mask, received = 1, None
    while mask < lax.axis_size(axis):
        received = swap(value, axis, mask)
        value = value + received
        mask *= 2
    return value, received


def block_of(array, index, size, axis):
    return lax.dynamic_slice_in_dim(array, index * size, size, axis)


def gather_sides(pair):
    if lax.axis_size("sq") == 8:
        return swap(pair, "sq", 2), swap(pair, "sq", 4)
    return [swap(pair, "sq", m) for m in range(2, lax.axis_size("sq"), 2)]


def gather_diagonal(pair, sides):
    trio = swap(jnp.stack([pair, *sides]), "sq", 1)
    if lax.axis_size("sq") == 8:
        near, far = sides
        return trio, swap(far[:1], "sq", 2), swap(near[1:], "sq", 4)
    return (trio,)


def gather_slots(pair, sides, trio, *diagonal):
    slots = []
    for k, side in enumerate([pair, *sides]):
        slots += [side, trio[k]]
    if diagonal:
        slots += [diagonal, swap(jnp.concatenate(diagonal), "sq", 1)]
    return slots


def scatter_cores(odd):
    return swap(odd, "sq", 1)


def scatter_diagonal(even, received):
    return add_blocks([[(even, (3, half)), (received, (3, half))] for half in range(2)])


def send_halves(diagonal):
    return [swap(diagonal[half], "sq", 2 + 2 * half) for half in range(2)]


def scatter_sides(even, received, halves):
    sums = []
    for k in range(1, 3 if halves else even.shape[0]):
        terms = [[(even, (k, half)), (received, (k, half))] for half in range(2)]
        if halves:
            terms[2 - k].append((halves[2 - k], ()))
        sums.append(add_blocks(terms))
    return sums, [swap(array, "sq", 2 * k + 2) for k, array in enumerate(sums)]


def scatter_total(even, received, blocks):
    return add_blocks(
        [
            [(even, (0, half)), (received, (0, half))] + [(block, (half,)) for block in blocks]
            for half in range(2)
        ]
    )


def reduce_cores(info, pairs):
    received = swap(relative_grads(info, 1, pairs, None), "sq", 1)
    own = relative_grads(info, 0, pairs, received)
    return own.reshape(lax.axis_size("sq") // 2, -1, own.shape[1])


def reduce_chips(own):
    half = own.shape[2] // 2
    results = []
    for part in range(2):
        blocks = own[:, :, part * half : (part + 1) * half]
        steps = [1 << b for b in range(own.shape[0].bit_length() - 1)]
        if part:
            steps = steps[::-1]
        kept = {m: blocks[m] for m in range(own.shape[0])}
        for number, step in enumerate(steps):
            give = sorted(m for m in kept if m & step)
            keep = sorted(m for m in kept if not m & step)
            got = swap(jnp.stack([kept[m] for m in give]), "sq", 2 * step)
            last = number == len(steps) - 1
            kept = {
                m: (kept[m].astype(F32) + got[i].astype(F32)).astype(F32 if last else BF16)
                for i, m in enumerate(keep)
            }
        results.append(kept[0])
    return jnp.concatenate(results, axis=1).astype(F32)


COST = 100


def cost(flops, bytes_accessed, transcendentals):
    return pl.CostEstimate(
        flops=flops // COST,
        bytes_accessed=bytes_accessed // COST,
        transcendentals=transcendentals // COST,
    )


def add_kernel(counts, *refs):
    first = 0
    for half, count in enumerate(counts):
        total = None
        for ref in refs[first : first + count]:
            part = ref[(0,) * (len(ref.shape) - 2)].astype(F32)
            total = part if total is None else total + part
        refs[-1][half, 0] = total.astype(BF16)
        first += count


def add_blocks(halves):
    shape = halves[0][0][0].shape[-3:]

    def spec(lead):
        return pl.BlockSpec((1,) * (len(lead) + 1) + shape[1:], lambda s: (*lead, s, 0, 0))

    terms = [term for half in halves for term in half]
    return pl.pallas_call(
        functools.partial(add_kernel, [len(half) for half in halves]),
        grid=(shape[0],),
        in_specs=[spec(lead) for _, lead in terms],
        out_specs=pl.BlockSpec((2, 1) + shape[1:], lambda s: (0, s, 0, 0)),
        out_shape=jax.ShapeDtypeStruct((2, *shape), BF16),
        compiler_params=params(),
        name="add_blocks",
    )(*[array for array, _ in terms])


def params():
    return pltpu.CompilerParams(vmem_limit_bytes=VMEM_LIMIT)


def place_columns(rank, table, sources, out_ref):
    width = sources[0].shape[-1]
    for z in range(len(table)):

        @pl.when(rank == z)
        def _(z=z):
            for f, index in enumerate(table[z]):
                out_ref[:, f * width : (f + 1) * width] = sources[index][...]


def row_sums(values):
    cols = values.shape[1]
    total = values[:, :HD]
    for k in range(1, cols // HD):
        total = total + values[:, k * HD : (k + 1) * HD]
    return jnp.sum(total.T, axis=0, keepdims=True)


def as_columns(row):
    return jnp.broadcast_to(row, (HD, row.shape[1])).T


def front_kernel(table, count, info, *refs):
    sources, refs = refs[:count], refs[count:]
    gain_ref, wq_ref, wk_ref, wv_ref = refs[:4]
    low_ref, normed_ref, inv_ref, query_ref, key_ref, value_ref, square_ref = refs[4:]
    place_columns(info[0], table, sources, low_ref)
    rows = low_ref[...].astype(F32)
    inv = lax.rsqrt(jnp.mean(rows * rows, axis=1, keepdims=True) + EPSILON)
    inv_ref[...] = inv
    normed = (rows * inv * gain_ref[...]).astype(BF16)
    normed_ref[...] = normed
    query, key = dot(normed, wq_ref[...]), dot(normed, wk_ref[...])
    query_ref[...] = query
    key_ref[...] = key
    value_ref[...] = dot(normed, wv_ref[...]).astype(BF16)
    square_ref[0:1, :] = row_sums(query * query)
    square_ref[1:2, :] = row_sums(key * key)


def front(rank, gathered, gain, w_query, w_key, w_value):
    sources, table = gathered
    rows, width = sources[0].shape
    total = width * len(table)
    cols = w_query.shape[1]
    tile = min(256, rows)
    spec = lambda cols: pl.BlockSpec((tile, cols), lambda i, info: (i, 0))
    whole = lambda array: pl.BlockSpec(
        array.shape, lambda i, info: (0, 0), pipeline_mode=pl.Buffered(1)
    )
    out = lambda cols, dtype: jax.ShapeDtypeStruct((rows, cols), dtype)
    return pl.pallas_call(
        functools.partial(front_kernel, table, len(sources)),
        grid_spec=pltpu.PrefetchScalarGridSpec(
            num_scalar_prefetch=1,
            grid=(rows // tile,),
            in_specs=[spec(width)] * len(sources)
            + [pl.BlockSpec((1, total), lambda i, info: (0, 0))]
            + [whole(w_query), whole(w_key), whole(w_value)],
            out_specs=[spec(total), spec(total), spec(1), spec(cols), spec(cols), spec(cols)]
            + [pl.BlockSpec((2, tile), lambda i, info: (0, i))],
        ),
        out_shape=[
            out(total, BF16),
            out(total, BF16),
            out(1, F32),
            out(cols, F32),
            out(cols, F32),
            out(cols, BF16),
            jax.ShapeDtypeStruct((2, rows), F32),
        ],
        compiler_params=params(),
        cost_estimate=cost(
            flops=6 * rows * total * cols,
            bytes_accessed=6 * total * cols + 8 * rows * total,
            transcendentals=0,
        ),
        name="front",
    )(rank, *sources, gain[None, :], w_query, w_key, w_value)


def halves(count):
    lane = lax.broadcasted_iota(jnp.int32, (1, HD), 1)
    return jnp.where(lane < HD // 2, 1.0, -1.0)


def rotate_kernel(
    all_cols, q_ref, k_ref, v_ref, square_ref, qg_ref, kg_ref, cos_ref, sin_ref, out_ref, pair_ref
):
    inv = lax.rsqrt(square_ref[...] / all_cols + EPSILON)
    cosine, sine = cos_ref[...], -halves(HD) * sin_ref[...]
    for number, (raw_ref, gain_ref) in enumerate(((q_ref, qg_ref), (k_ref, kg_ref))):
        scale = as_columns(inv[number : number + 1, :])
        for h in range(raw_ref.shape[1] // HD):
            span = slice(h * HD, (h + 1) * HD)
            normed = raw_ref[:, span] * scale * gain_ref[:, span]
            turned = (normed * cosine + pltpu.roll(normed, HD // 2, 1) * sine).astype(BF16)
            if number == 0:
                out_ref[0, :, span] = turned
            else:
                pair_ref[0, 0, :, span] = turned
    pair_ref[1, 0] = v_ref[...]


def rotate(query, key, value, squares, query_gain, key_gain, cosine, sine, all_cols):
    rows, cols = query.shape
    size = cosine.shape[0]
    spec = pl.BlockSpec((size, cols), lambda s: (s, 0))
    one = pl.BlockSpec((1, cols), lambda s: (0, 0))
    turn = pl.BlockSpec((size, HD), lambda s: (0, 0))
    return pl.pallas_call(
        functools.partial(rotate_kernel, all_cols),
        grid=(rows // size,),
        in_specs=[spec, spec, spec, pl.BlockSpec((2, size), lambda s: (0, s))]
        + [one, one, turn, turn],
        out_specs=[
            pl.BlockSpec((1, size, cols), lambda s: (s, 0, 0)),
            pl.BlockSpec((2, 1, size, cols), lambda s: (0, s, 0, 0)),
        ],
        out_shape=[
            jax.ShapeDtypeStruct((rows // size, size, cols), BF16),
            jax.ShapeDtypeStruct((2, rows // size, size, cols), BF16),
        ],
        compiler_params=params(),
        name="rotate",
    )(query, key, value, squares, query_gain[None, :], key_gain[None, :], cosine, sine)


def back_parts(all_cols, refs):
    dq_ref, dkv_ref, q_ref, k_ref, square_ref, qg_ref, kg_ref, cos_ref, sin_ref = refs
    inv = lax.rsqrt(square_ref[...] / all_cols + EPSILON)
    cosine, sine = cos_ref[...], sin_ref[...]
    sign = halves(HD)
    for number, (raw_ref, gain_ref) in enumerate(((q_ref, qg_ref), (k_ref, kg_ref))):
        scale = as_columns(inv[number : number + 1, :])
        for h in range(raw_ref.shape[1] // HD):
            span = slice(h * HD, (h + 1) * HD)
            grad = (dkv_ref[0, 0, :, span] if number else dq_ref[0, :, span]).astype(F32)
            back = grad * cosine + pltpu.roll(grad * sine, HD // 2, 1) * sign
            yield number, span, back, raw_ref[:, span] * scale, scale, gain_ref[:, span]


def back_stats_kernel(all_cols, *refs):
    stat_ref, gain_ref = refs[9:]

    @pl.when(pl.program_id(0) == 0)
    def _():
        gain_ref[...] = jnp.zeros(gain_ref.shape, F32)

    totals = [None, None]
    for number, span, back, hat, _, gain in back_parts(all_cols, refs[:9]):
        product = back * hat
        gain_ref[number : number + 1, span] += jnp.sum(product, axis=0, keepdims=True)
        product = product * gain
        totals[number] = product if totals[number] is None else totals[number] + product
    for number in range(2):
        stat_ref[number : number + 1, :] = row_sums(totals[number])


def back_specs(size, cols):
    spec = pl.BlockSpec((size, cols), lambda s: (s, 0))
    one = pl.BlockSpec((1, cols), lambda s: (0, 0))
    turn = pl.BlockSpec((size, HD), lambda s: (0, 0))
    row = pl.BlockSpec((2, size), lambda s: (0, s))
    return [
        pl.BlockSpec((1, size, cols), lambda s: (s, 0, 0)),
        pl.BlockSpec((2, 1, size, cols), lambda s: (0, s, 0, 0)),
        spec,
        spec,
        row,
        one,
        one,
        turn,
        turn,
    ]


def back_stats(operands, all_cols):
    rows, cols = operands[2].shape
    size = operands[0].shape[1]
    return pl.pallas_call(
        functools.partial(back_stats_kernel, all_cols),
        grid=(rows // size,),
        in_specs=back_specs(size, cols),
        out_specs=[
            pl.BlockSpec((2, size), lambda s: (0, s)),
            pl.BlockSpec((2, cols), lambda s: (0, 0)),
        ],
        out_shape=[
            jax.ShapeDtypeStruct((2, rows), F32),
            jax.ShapeDtypeStruct((2, cols), F32),
        ],
        compiler_params=params(),
        name="back_stats",
    )(*operands)


def back_first_kernel(all_cols, count, info, *refs):
    stat_ref, low_ref, inv_ref, gain_ref, wq_ref, wk_ref, wv_ref = refs[9:16]
    raw_ref, part_ref = refs[16:18]
    first_refs, buffer = refs[18 : 18 + count], refs[18 + count]
    size = buffer.shape[0]
    rows = pl.ds(pl.multiple_of(pl.program_id(0) * size, size), size)
    cols = wq_ref.shape[1]
    stats = stat_ref[...] / all_cols
    for number, span, back, hat, scale, gain in back_parts(all_cols, refs[:9]):
        mean = as_columns(stats[number : number + 1, :])
        raw = scale * (back * gain - hat * mean)
        raw_ref[:, number * cols + span.start : number * cols + span.stop] = raw.astype(BF16)
    raw_ref[:, 2 * cols :] = refs[1][1, 0]
    first = (
        dot(raw_ref[:, :cols], wq_ref[...], NT)
        + dot(raw_ref[:, cols : 2 * cols], wk_ref[...], NT)
        + dot(raw_ref[:, 2 * cols :], wv_ref[...], NT)
    )
    buffer[...] = first.astype(BF16)
    feat = first_refs[0].shape[1]
    for k in range(count):
        target = lax.rem(info[1] + k, count)
        span = pl.ds(pl.multiple_of(target * feat, feat), feat)
        first_refs[k][rows, :] = buffer[:, span]

    @pl.when(pl.program_id(0) == 0)
    def _():
        part_ref[...] = jnp.zeros(part_ref.shape, F32)

    product = first * (low_ref[...].astype(F32) * inv_ref[...])
    part_ref[...] += jnp.sum(product, axis=0, keepdims=True)
    rest = row_sums(product * gain_ref[...])
    line = lax.broadcasted_iota(jnp.int32, (EXTRA, size), 0)
    terms = jnp.zeros((EXTRA, size), F32)
    for term in range(2):
        part = rest.astype(BF16).astype(F32)
        rest = rest - part
        terms = jnp.where(line == 2 * pl.program_id(0) + term, part, terms)
    for ref in first_refs:
        place = ref.shape[0] - EXTRA

        @pl.when(pl.program_id(0) == 0)
        def _(ref=ref, place=place):
            ref[place:, :] = jnp.zeros((EXTRA, feat), BF16)

        ref[place:, :size] += terms.astype(BF16)


EXTRA = 16


def back_first(info, operands, stats, low, inv, gain, w_query, w_key, w_value, all_cols, count):
    rows, cols = operands[2].shape
    size = operands[0].shape[1]
    total = low.shape[1]
    lift = lambda spec: pl.BlockSpec(spec.block_shape, lambda s, info: spec.index_map(s))
    spec = lambda cols: pl.BlockSpec((size, cols), lambda s, info: (s, 0))
    row = lambda count: pl.BlockSpec((count, size), lambda s, info: (0, s))
    whole = lambda array: pl.BlockSpec(
        array.shape, lambda s, info: (0, 0), pipeline_mode=pl.Buffered(1)
    )
    one = pl.BlockSpec((1, total), lambda s, info: (0, 0))
    height = rows + EXTRA
    raw, part, *pieces = pl.pallas_call(
        functools.partial(back_first_kernel, all_cols, count),
        grid_spec=pltpu.PrefetchScalarGridSpec(
            num_scalar_prefetch=1,
            grid=(rows // size,),
            in_specs=[lift(s) for s in back_specs(size, cols)]
            + [row(2), spec(total), spec(1), one]
            + [whole(w_query), whole(w_key), whole(w_value)],
            out_specs=[spec(3 * cols), one]
            + [pl.BlockSpec((height, total // count), lambda s, info: (0, 0))] * count,
            scratch_shapes=[pltpu.VMEM((size, total), BF16)],
        ),
        out_shape=[
            jax.ShapeDtypeStruct((rows, 3 * cols), BF16),
            jax.ShapeDtypeStruct((1, total), F32),
        ]
        + [jax.ShapeDtypeStruct((height, total // count), BF16)] * count,
        compiler_params=params(),
        cost_estimate=cost(
            flops=6 * rows * total * cols,
            bytes_accessed=6 * total * cols + 8 * rows * total,
            transcendentals=0,
        ),
        name="back_first",
    )(info, *operands, stats, low, inv, gain[None, :], w_query, w_key, w_value)
    return raw, pieces, part[0]


def joined_kernel(table, count, info, *refs):
    place_columns(info[0], table, refs[:count], refs[count])


def joined_rows(rank, gathered):
    sources, table = gathered
    rows, width = sources[0].shape
    total = width * len(table)
    tile = min(256, rows)
    spec = lambda cols: pl.BlockSpec((tile, cols), lambda i, info: (i, 0))
    return pl.pallas_call(
        functools.partial(joined_kernel, table, len(sources)),
        grid_spec=pltpu.PrefetchScalarGridSpec(
            num_scalar_prefetch=1,
            grid=(rows // tile,),
            in_specs=[spec(width)] * len(sources),
            out_specs=spec(total),
        ),
        out_shape=jax.ShapeDtypeStruct((rows, total), BF16),
        compiler_params=params(),
        name="joined_rows",
    )(rank, *sources)


def relative_grads_kernel(counts, info, *refs):
    more = refs[2 * sum(counts) : -1]
    first, start = 0, 0
    for count in counts:
        lefts, rights = refs[first : first + count], refs[first + count : first + 2 * count]
        first += 2 * count
        total = dot(lefts[0][...], rights[0][...], TN)
        for left, right in zip(lefts[1:], rights[1:]):
            total += dot(left[...], right[...], TN)
        span = slice(start, start + total.shape[1])
        start = span.stop
        for ref in more:
            total += ref[:, span].astype(F32)
        refs[-1][:, span] = total.astype(BF16)


def relative_grads(info, parity, pairs, more):
    blocks = lax.axis_size("sq")
    height = pairs[0][0][0][0].shape[1] // blocks
    specs, operands, width = [], [], 0
    for lefts, rights in pairs:
        width += rights[0].shape[1]
        for (_, chunk), right in zip(lefts, rights):
            specs.append(
                pl.BlockSpec(
                    (right.shape[0], height),
                    lambda m, info, chunk=chunk: (
                        chunk,
                        jnp.bitwise_xor(info[0], 2 * m + parity),
                    ),
                )
            )
        specs += [
            pl.BlockSpec(right.shape, lambda m, info: (0, 0), pipeline_mode=pl.Buffered(1))
            for right in rights
        ]
        operands += [left for left, _ in lefts] + list(rights)
    out = pl.BlockSpec((height, width), lambda m, info: (m, 0))
    if more is not None:
        specs.append(out)
        operands.append(more)
    return pl.pallas_call(
        functools.partial(relative_grads_kernel, [len(lefts) for lefts, _ in pairs]),
        grid_spec=pltpu.PrefetchScalarGridSpec(
            num_scalar_prefetch=1, grid=(blocks // 2,), in_specs=specs, out_specs=out
        ),
        out_shape=jax.ShapeDtypeStruct((height * blocks // 2, width), BF16),
        compiler_params=params(),
        name="relative_grads",
    )(info, *operands)


def middle_kernel(table, count, info, *refs):
    sources = refs[:count]
    low_ref, w_ref, gain_ref, router_ref, routes_ref = refs[count : count + 5]
    attn_ref, middle_ref, inv_ref, ffn_ref, prob_ref, routed_ref = refs[count + 5 :]
    place_columns(info[0], table, sources, attn_ref)
    middle = low_ref[...].astype(F32) + dot(attn_ref[...], w_ref[...])
    middle_ref[...] = middle
    inv = lax.rsqrt(jnp.mean(middle * middle, axis=1, keepdims=True) + EPSILON)
    inv_ref[...] = inv
    ffn_in = (middle * inv * gain_ref[...]).astype(BF16)
    ffn_ref[...] = ffn_in
    logits = dot(ffn_in, router_ref[...])
    powers = jnp.exp(logits - jnp.max(logits, axis=1, keepdims=True))
    prob_ref[...] = powers / jnp.sum(powers, axis=1, keepdims=True)
    routes = routes_ref[...]
    ids = lax.broadcasted_iota(jnp.int32, logits.shape, 1)
    routed = jnp.zeros(logits.shape, F32)
    for r in range(routes.shape[1]):
        routed = jnp.where(routes[:, r : r + 1] == ids, 1.0, routed)
    routed_ref[...] = routed


def middle_rows(rank, gathered, low, w_out, gain, router, routes):
    sources, table = gathered
    rows, width = sources[0].shape
    total = low.shape[1]
    experts = router.shape[1]
    tile = min(256, rows)
    spec = lambda cols: pl.BlockSpec((tile, cols), lambda i, info: (i, 0))
    whole = lambda array: pl.BlockSpec(
        array.shape, lambda i, info: (0, 0), pipeline_mode=pl.Buffered(1)
    )
    out = lambda cols, dtype: jax.ShapeDtypeStruct((rows, cols), dtype)
    return pl.pallas_call(
        functools.partial(middle_kernel, table, len(sources)),
        grid_spec=pltpu.PrefetchScalarGridSpec(
            num_scalar_prefetch=1,
            grid=(rows // tile,),
            in_specs=[spec(width)] * len(sources)
            + [spec(total), whole(w_out), pl.BlockSpec((1, total), lambda i, info: (0, 0))]
            + [whole(router), spec(routes.shape[1])],
            out_specs=[
                spec(width * len(table)),
                spec(total),
                spec(1),
                spec(total),
                spec(experts),
                spec(experts),
            ],
        ),
        out_shape=[
            out(width * len(table), BF16),
            out(total, F32),
            out(1, F32),
            out(total, BF16),
            out(experts, F32),
            out(experts, F32),
        ],
        compiler_params=params(),
        cost_estimate=cost(
            flops=2 * rows * total * total,
            bytes_accessed=2 * total * total + 12 * rows * total,
            transcendentals=0,
        ),
        name="middle_rows",
    )(rank, *sources, low, w_out, gain[None, :], router, routes)


def weight_grad_kernel(count, parts, *refs):
    height = refs[count].shape[0]
    left = lambda i: refs[i][...] if parts == 1 else refs[0][i * height : (i + 1) * height, :]
    total = dot(left(0), refs[count][...], TN)
    for i in range(1, len(refs) - 1 - count):
        total += dot(left(i), refs[count + i][...], TN)
    refs[-1][...] = total.astype(BF16)


def weight_grad(lefts, rights):
    rows, height = rights[0].shape[0], lefts[0].shape[1]
    width = rights[0].shape[1]
    parts = lefts[0].shape[0] // rows
    tall = min(2048, height)
    cols = min(512, width)
    return pl.pallas_call(
        functools.partial(weight_grad_kernel, len(lefts), parts),
        grid=(width // cols, height // tall),
        in_specs=[pl.BlockSpec((rows * parts, tall), lambda j, i: (0, i))] * len(lefts)
        + [pl.BlockSpec((rows, cols), lambda j, i: (0, j))] * len(rights),
        out_specs=pl.BlockSpec((tall, cols), lambda j, i: (i, j)),
        out_shape=jax.ShapeDtypeStruct((height, width), BF16),
        compiler_params=params(),
        cost_estimate=cost(
            flops=2 * rows * len(rights) * height * width,
            bytes_accessed=2 * (rows * len(rights) * (height + width) + height * width),
            transcendentals=0,
        ),
        name="weight_grad",
    )(*lefts, *rights)


def slot_operands(kv_slots):
    arrays, places = [], []
    for slot in kv_slots:
        if isinstance(slot, tuple):
            places.append(((len(arrays), 0), (len(arrays) + 1, 0)))
            arrays += list(slot)
        else:
            places.append(((len(arrays), 0), (len(arrays), 1)))
            arrays.append(slot)
    size = arrays[0].shape[2]
    specs = [
        pl.BlockSpec((a.shape[0], 1, size, HD), lambda s, h, info: (0, s, 0, h)) for a in arrays
    ]
    return arrays, specs, places


def attn_forward_kernel(places, count, info, q_ref, *refs):
    kv_refs, (low_ref, full_ref, lse_ref, top, total, accum) = refs[:count], refs[count:]
    rank = info[0]
    length = info[2 + pl.program_id(0)]
    queries = q_ref[0]
    size = queries.shape[0]
    top[...] = jnp.full(top.shape, NEGATIVE, F32)
    total[...] = jnp.zeros(total.shape, F32)
    accum[...] = jnp.zeros(accum.shape, F32)
    key_row = lax.broadcasted_iota(jnp.int32, (size, size), 0)
    query_col = lax.broadcasted_iota(jnp.int32, (size, size), 1)
    for slot, ((ka, ki), (va, vi)) in enumerate(places):
        block = rank ^ slot
        start = block * size

        @pl.when((block <= rank) & (start < length))
        def _(slot=slot, start=start, ka=ka, ki=ki, va=va, vi=vi):
            scores = dot(kv_refs[ka][ki, 0], queries, NT) * HD**-0.5
            allowed = key_row + start < length
            if slot == 0:
                allowed = allowed & (key_row <= query_col)
            scores = jnp.where(allowed, scores, NEGATIVE)
            newest = jnp.maximum(top[...], jnp.max(scores, axis=0, keepdims=True))
            weights = jnp.exp(scores - newest)
            factor = jnp.exp(top[...] - newest)
            top[...] = newest
            total[...] = total[...] * factor + jnp.sum(weights, axis=0, keepdims=True)
            accum[...] = accum[...] * factor + dot(kv_refs[va][vi, 0], weights.astype(BF16), TN)

    result = (accum[...] / total[...]).T
    full_ref[0] = result
    low_ref[0] = result.astype(BF16)
    lse_ref[0, 0] = top[...] + jnp.log(total[...])


def attn_forward(info, queries, kv_slots):
    seqs, size, columns = queries.shape
    heads = columns // HD
    slots = len(kv_slots)
    arrays, specs, places = slot_operands(kv_slots)
    row_spec = pl.BlockSpec((1, size, HD), lambda s, h, info: (s, 0, h))
    lse_spec = pl.BlockSpec((1, 1, 1, size), lambda s, h, info: (s, h, 0, 0))
    return pl.pallas_call(
        functools.partial(attn_forward_kernel, places, len(arrays)),
        grid_spec=pltpu.PrefetchScalarGridSpec(
            num_scalar_prefetch=1,
            grid=(seqs, heads),
            in_specs=[row_spec] + specs,
            out_specs=[row_spec, row_spec, lse_spec],
            scratch_shapes=[
                pltpu.VMEM((1, size), F32),
                pltpu.VMEM((1, size), F32),
                pltpu.VMEM((HD, size), F32),
            ],
        ),
        out_shape=[
            jax.ShapeDtypeStruct(queries.shape, BF16),
            jax.ShapeDtypeStruct(queries.shape, F32),
            jax.ShapeDtypeStruct((seqs, heads, 1, size), F32),
        ],
        compiler_params=params(),
        cost_estimate=cost(
            flops=8 * seqs * heads * slots * size * size * HD,
            bytes_accessed=4 * seqs * size * columns * (slots + 2),
            transcendentals=seqs * heads * slots * size * size,
        ),
        name="attn_forward",
    )(info, queries, *arrays)


def attn_backward_kernel(places, count, tp_count, info, q_ref, full_ref, lse_ref, *refs):
    grad_refs, refs = refs[:tp_count], refs[tp_count:]
    kv_refs, (dq_ref, even_ref, odd_ref, accum, grad_buf) = refs[:count], refs[count:]
    rank = info[0]
    length = info[2 + pl.program_id(0)]
    queries = q_ref[0]
    size = queries.shape[0]
    piece = size * pl.num_programs(0) // tp_count
    for i in range(size // piece):
        sender = pl.program_id(0) * (size // piece) + i
        distance = lax.rem(info[1] - sender + tp_count, tp_count)
        for k in range(tp_count):

            @pl.when(distance == k)
            def _(i=i, k=k):
                grad_buf[i * piece : (i + 1) * piece, :] = grad_refs[k][...]

    grads = grad_buf[...]
    lse = lse_ref[0, 0]
    delta = jnp.sum((grads.astype(F32) * full_ref[0]).T, axis=0, keepdims=True)
    accum[...] = jnp.zeros(accum.shape, F32)
    key_row = lax.broadcasted_iota(jnp.int32, (size, size), 0)
    query_col = lax.broadcasted_iota(jnp.int32, (size, size), 1)
    for slot, ((ka, ki), (va, vi)) in enumerate(places):
        block = rank ^ slot
        start = block * size
        out_ref = odd_ref if slot % 2 else even_ref
        live = (block <= rank) & (start < length)

        @pl.when(live)
        def _(slot=slot, start=start, out_ref=out_ref, ka=ka, ki=ki, va=va, vi=vi):
            keys, values = kv_refs[ka][ki, 0], kv_refs[va][vi, 0]
            scores = dot(keys, queries, NT) * HD**-0.5
            allowed = key_row + start < length
            if slot == 0:
                allowed = allowed & (key_row <= query_col)
            weights = jnp.where(allowed, jnp.exp(scores - lse), 0.0)
            back = dot(values, grads, NT)
            score_grad = (weights * (back - delta)).astype(BF16)
            out_ref[slot // 2, 1, 0] = dot(weights.astype(BF16), grads).astype(BF16)
            out_ref[slot // 2, 0, 0] = (dot(score_grad, queries) * HD**-0.5).astype(BF16)
            accum[...] += dot(score_grad, keys, TN)

        @pl.when(jnp.logical_not(live))
        def _(slot=slot, out_ref=out_ref):
            out_ref[slot // 2, :, 0] = jnp.zeros((2,) + queries.shape, BF16)

    dq_ref[0] = (accum[...] * HD**-0.5).astype(BF16)


def attn_backward(info, queries, grad_pieces, full, lse, kv_slots):
    seqs, size, columns = queries.shape
    heads = columns // HD
    slots = len(kv_slots)
    arrays, specs, places = slot_operands(kv_slots)
    piece = size * seqs // len(grad_pieces)
    last = grad_pieces[0].shape[0] // piece - 1
    row_spec = pl.BlockSpec((1, size, HD), lambda s, h, info: (s, 0, h))
    piece_spec = pl.BlockSpec((piece, HD), lambda s, h, info: (last, h))
    lse_spec = pl.BlockSpec((1, 1, 1, size), lambda s, h, info: (s, h, 0, 0))
    out_spec = pl.BlockSpec((slots // 2, 2, 1, size, HD), lambda s, h, info: (0, 0, s, 0, h))
    out_shape = jax.ShapeDtypeStruct((slots // 2, 2, seqs, size, columns), BF16)
    return pl.pallas_call(
        functools.partial(attn_backward_kernel, places, len(arrays), len(grad_pieces)),
        grid_spec=pltpu.PrefetchScalarGridSpec(
            num_scalar_prefetch=1,
            grid=(seqs, heads),
            in_specs=[row_spec, row_spec, lse_spec] + [piece_spec] * len(grad_pieces) + specs,
            out_specs=[row_spec, out_spec, out_spec],
            scratch_shapes=[pltpu.VMEM((size, HD), F32), pltpu.VMEM((size, HD), BF16)],
        ),
        out_shape=[jax.ShapeDtypeStruct(queries.shape, BF16), out_shape, out_shape],
        compiler_params=params(),
        cost_estimate=cost(
            flops=20 * seqs * heads * slots * size * size * HD,
            bytes_accessed=8 * seqs * size * columns * (slots + 2),
            transcendentals=seqs * heads * slots * size * size,
        ),
        name="attn_backward",
    )(info, queries, full, lse, *grad_pieces, *arrays)


def expert_hidden_kernel(
    tile,
    info,
    x_ref,
    g_ref,
    prob_ref,
    routed_ref,
    wg_ref,
    wu_ref,
    wd_ref,
    gh_ref,
    gp_ref,
    up_ref,
    gg_ref,
):
    expert, block = pl.program_id(0), pl.program_id(1)
    rows = x_ref.shape[0]

    @pl.when((expert == 0) & (block == 0))
    def _():
        gg_ref[...] = jnp.zeros(gg_ref.shape, F32)

    for i in range(rows // tile):
        span = slice(i * tile, (i + 1) * tile)
        tokens = x_ref[span, :]
        gate_pre = dot(tokens, wg_ref[0])
        up_pre = dot(tokens, wu_ref[0])
        back = dot(g_ref[span, :], wd_ref[0], NT)
        probs = prob_ref[span, :]
        lane = lax.broadcasted_iota(jnp.int32, probs.shape, 1)
        chosen = (lane == info[1] * pl.num_programs(0) + expert) & (routed_ref[span, :] > 0.5)
        gate = jnp.sum(jnp.where(chosen, probs, 0.0), axis=1, keepdims=True)
        sigmoid = 1.0 / (1.0 + jnp.exp(-gate_pre))
        silu = gate_pre * sigmoid
        hidden = silu * up_pre
        inner = jnp.sum(hidden * back, axis=1, keepdims=True)
        gg_ref[span, :] += jnp.where(chosen, inner, 0.0)
        gh_ref[span, :] = (gate * hidden).astype(BF16)
        hidden_grad = gate * back
        gp_ref[span, :] = (
            hidden_grad * up_pre * (sigmoid + silu * (1.0 - sigmoid))
        ).astype(BF16)
        up_ref[span, :] = (hidden_grad * silu).astype(BF16)


def expert_hidden(info, tokens, grads, probs, routed, w_gate, w_up, w_down, chunk):
    rows, width = tokens.shape
    experts, _, units = w_gate.shape
    cols = min(512, units)
    tile = min(512, rows)
    whole = pl.BlockSpec((rows, width), lambda e, f, info: (0, 0), pipeline_mode=pl.Buffered(1))
    part = pl.BlockSpec((rows, width), lambda e, f, info: (chunk, 0), pipeline_mode=pl.Buffered(1))
    small = pl.BlockSpec(probs.shape, lambda e, f, info: (0, 0))
    wide = pl.BlockSpec((1, width, cols), lambda e, f, info: (e, 0, f))
    tall = pl.BlockSpec((1, cols, width), lambda e, f, info: (e, f, 0))
    result = pl.BlockSpec((rows, cols), lambda e, f, info: (0, e * (units // cols) + f))
    out = jax.ShapeDtypeStruct((rows, experts * units), BF16)
    return pl.pallas_call(
        functools.partial(expert_hidden_kernel, tile),
        grid_spec=pltpu.PrefetchScalarGridSpec(
            num_scalar_prefetch=1,
            grid=(experts, units // cols),
            in_specs=[whole, part, small, small, wide, wide, tall],
            out_specs=[result, result, result, small],
        ),
        out_shape=[out, out, out, jax.ShapeDtypeStruct(probs.shape, F32)],
        compiler_params=params(),
        cost_estimate=cost(
            flops=6 * rows * width * experts * units,
            bytes_accessed=6 * width * experts * units + 6 * rows * experts * units,
            transcendentals=rows * experts * units,
        ),
        name="expert_hidden",
    )(info, tokens, grads, probs, routed, w_gate, w_up, w_down)


def expert_back_kernel(
    count, info, gp_ref, up_ref, gg_ref, prob_ref, router_ref, x_ref, wg_ref, wu_ref, *refs
):
    out_refs, lg_ref, rg_ref, accum = refs[:count], refs[count], refs[count + 1], refs[count + 2]
    expert, block = pl.program_id(0), pl.program_id(1)
    cols = wg_ref.shape[1]
    span = pl.ds(pl.multiple_of(block * cols, cols), cols)

    @pl.when((expert == 0) & (block == 0))
    def _():
        probs, inner = prob_ref[...], gg_ref[...]
        lg_ref[...] = probs * (inner - jnp.sum(probs * inner, axis=1, keepdims=True))

    @pl.when(expert == 0)
    def _():
        accum[:, span] = lax.dot_general(
            lg_ref[...],
            router_ref[...].astype(F32),
            NT,
            precision=lax.Precision.HIGHEST,
            preferred_element_type=F32,
        )

    accum[:, span] += dot(gp_ref[...], wg_ref[0], NT) + dot(up_ref[...], wu_ref[0], NT)

    @pl.when(expert == 0)
    def _():
        rest = lg_ref[...]
        total = jnp.zeros((rest.shape[1], cols), F32)
        for _ in range(3):
            part = rest.astype(BF16)
            rest = rest - part.astype(F32)
            total += dot(part, x_ref[...], TN)
        rg_ref[...] = total

    @pl.when(expert == pl.num_programs(0) - 1)
    def _():
        height = out_refs[0].shape[0]
        for k in range(count):
            target = lax.rem(info[1] + k, count)
            rows = pl.ds(pl.multiple_of(target * height, height), height)
            out_refs[k][:, span] = accum[rows, span].astype(BF16)


def expert_back(info, gate_grads, up_grads, inner, probs, router, tokens, w_gate, w_up, count):
    rows = gate_grads.shape[0]
    experts, width, units = w_gate.shape
    total = router.shape[1]
    cols = min(1024, width)
    left = pl.BlockSpec((rows, units), lambda e, d, info: (0, e))
    small = pl.BlockSpec((rows, total), lambda e, d, info: (0, 0))
    weight = pl.BlockSpec((1, cols, units), lambda e, d, info: (e, d, 0))
    piece = pl.BlockSpec((rows // count, width), lambda e, d, info: (0, 0))
    last = width // cols - 1
    *pieces, _, router_grad = pl.pallas_call(
        functools.partial(expert_back_kernel, count),
        grid_spec=pltpu.PrefetchScalarGridSpec(
            num_scalar_prefetch=1,
            grid=(experts, width // cols),
            in_specs=[
                left,
                left,
                small,
                small,
                pl.BlockSpec((cols, total), lambda e, d, info: (d, 0)),
                pl.BlockSpec((rows, cols), lambda e, d, info: (0, jnp.where(e == 0, d, last))),
                weight,
                weight,
            ],
            out_specs=[piece] * count
            + [
                small,
                pl.BlockSpec((total, cols), lambda e, d, info: (0, jnp.where(e == 0, d, last))),
            ],
            scratch_shapes=[pltpu.VMEM((rows, width), F32)],
        ),
        out_shape=[jax.ShapeDtypeStruct((rows // count, width), BF16)] * count
        + [jax.ShapeDtypeStruct((rows, total), F32), jax.ShapeDtypeStruct((total, width), F32)],
        compiler_params=params(),
        cost_estimate=cost(
            flops=4 * rows * width * experts * units,
            bytes_accessed=4 * width * experts * units + 6 * rows * experts * units,
            transcendentals=0,
        ),
        name="expert_back",
    )(info, gate_grads, up_grads, inner, probs, router, tokens, w_gate, w_up)
    return pieces, router_grad


def mixture_kernel(count, info, hidden_ref, w_ref, *refs):
    head_refs, out_refs = refs[:count], refs[count:]
    rows = hidden_ref.shape[0]
    result = dot(hidden_ref[...], w_ref[...]).astype(BF16)
    for k in range(count):

        @pl.when(pl.program_id(0) == k)
        def _(k=k):
            out_refs[k][:rows] = result
            out_refs[k][rows:] = head_refs[k][...]


def mixture(info, hidden, w_down, heads, count):
    rows, units = hidden.shape
    width = w_down.shape[-1]
    feat = width // count
    height = heads[0].shape[0]
    piece = pl.BlockSpec((rows + height, feat), lambda k, info: (0, 0))
    row = pl.BlockSpec((height, feat), lambda k, info: (0, 0))
    return pl.pallas_call(
        functools.partial(mixture_kernel, count),
        grid_spec=pltpu.PrefetchScalarGridSpec(
            num_scalar_prefetch=1,
            grid=(count,),
            in_specs=[
                pl.BlockSpec((rows, units), lambda k, info: (0, 0), pipeline_mode=pl.Buffered(1)),
                pl.BlockSpec((units, feat), lambda k, info: (0, lax.rem(info[1] + k, count))),
            ]
            + [row] * count,
            out_specs=[piece] * count,
        ),
        out_shape=[jax.ShapeDtypeStruct((rows + height, feat), BF16)] * count,
        compiler_params=params(),
        cost_estimate=cost(
            flops=2 * rows * units * width,
            bytes_accessed=2 * (rows * units + units * width + rows * width),
            transcendentals=0,
        ),
        name="mixture",
    )(info, hidden, w_down.reshape(units, width), *heads)


def middle_back_kernel(count, info, *refs):
    piece_refs, refs = refs[:count], refs[count:]
    middle_ref, inv_ref, grad_ref, gain_ref, w_ref = refs[:5]
    part_ref, low_ref, *out_refs = refs[5:]
    ffn_grad = piece_refs[0][...].astype(F32)
    for k in range(1, count):
        ffn_grad = ffn_grad + piece_refs[k][...].astype(F32)
    inv = inv_ref[...]
    hat = middle_ref[...] * inv
    part_ref[...] = jnp.sum(ffn_grad * hat, axis=0, keepdims=True)
    gained = ffn_grad * gain_ref[...]
    mean = jnp.mean(gained * hat, axis=1, keepdims=True)
    low = (grad_ref[...].astype(F32) + inv * (gained - hat * mean)).astype(BF16)
    low_ref[...] = low
    cols = out_refs[0].shape[1]
    for k in range(count):
        target = lax.rem(info[1] + k, count)
        rows = pl.ds(pl.multiple_of(target * cols, cols), cols)
        out_refs[k][...] = dot(low, w_ref[rows, :], NT).astype(BF16)


def middle_back(info, pieces, middle, inv, grads, gain, w_out, chunk):
    count = len(pieces)
    height, width = pieces[0].shape
    cols = w_out.shape[0] // count
    whole = lambda array: pl.BlockSpec(array.shape, lambda i, info: (0, 0))
    own = lambda cols: pl.BlockSpec((height, cols), lambda i, info: (info[1], 0))
    part = pl.BlockSpec((height, width), lambda i, info: (chunk * count + info[1], 0))
    first = lambda rows, cols: pl.BlockSpec((rows, cols), lambda i, info: (0, 0))
    out = lambda rows, cols, dtype: jax.ShapeDtypeStruct((rows, cols), dtype)
    part, low, *rest = pl.pallas_call(
        functools.partial(middle_back_kernel, count),
        grid_spec=pltpu.PrefetchScalarGridSpec(
            num_scalar_prefetch=1,
            grid=(1,),
            in_specs=[first(height, width)] * count
            + [own(width), own(1), part, first(1, width), whole(w_out)],
            out_specs=[first(1, width), first(height, width)] + [first(height, cols)] * count,
        ),
        out_shape=[out(1, width, F32), out(height, width, BF16)]
        + [out(height, cols, BF16)] * count,
        compiler_params=params(),
        cost_estimate=cost(
            flops=2 * height * width * width, bytes_accessed=2 * width * width, transcendentals=0
        ),
        name="middle_back",
    )(info, *pieces, middle, inv, grads, gain[None, :], w_out)
    return part[0], low, rest


def finish_kernel(count, info, *refs):
    row_ref, first_refs = refs[0], refs[1 : 1 + count]
    x_ref, inv_ref, gain_ref, out_ref = refs[1 + count :]
    size, width = out_ref.shape[0], count * x_ref.shape[1]
    rows = pl.ds(pl.multiple_of(pl.program_id(0) * size, size), size)
    place = first_refs[0].shape[0] - EXTRA
    first, terms = None, None
    for ref in first_refs:
        part, extra = ref[rows, :].astype(F32), ref[place:, :size].astype(F32)
        first = part if first is None else first + part
        terms = extra if terms is None else terms + extra
    line = lax.broadcasted_iota(jnp.int32, terms.shape, 0)
    own = jnp.where(line // 2 == pl.program_id(0), terms, 0.0)
    inner = as_columns(jnp.sum(own, axis=0, keepdims=True) / width)[:, :1]
    inv = inv_ref[...]
    hat = x_ref[...].astype(F32) * inv
    out_ref[...] = row_ref[...].astype(F32) + inv * (gain_ref[...] * first - hat * inner)


def finish(info, all_rows, first_pieces, x, inv, gain, chunk, seqs):
    count = len(first_pieces)
    rows, feat = x.shape
    size = rows // seqs
    one = lambda array: pl.BlockSpec(array.shape, lambda i, info: (0, 0))
    own = lambda cols: pl.BlockSpec((size, cols), lambda i, info: (i, 0))
    return pl.pallas_call(
        functools.partial(finish_kernel, count),
        grid_spec=pltpu.PrefetchScalarGridSpec(
            num_scalar_prefetch=1,
            grid=(seqs,),
            in_specs=[
                pl.BlockSpec((size, feat), lambda i, info: (chunk * seqs + i, info[1]))
            ]
            + [one(a) for a in first_pieces]
            + [own(feat), own(1), pl.BlockSpec((1, feat), lambda i, info: (0, info[1]))],
            out_specs=own(feat),
        ),
        out_shape=jax.ShapeDtypeStruct((rows, feat), F32),
        compiler_params=params(),
        name="finish",
    )(info, all_rows, *first_pieces, x, inv, gain[None, :])


def ordered_kernel(count, info, *refs):
    height = refs[0].shape[0]
    for z in range(count):

        @pl.when(info[0] == z)
        def _(z=z):
            for c in range(len(refs) // count):
                for f in range(count):
                    row = (c * count + f) * height
                    refs[-1][row : row + height, :] = refs[c * count + (z - f) % count][...]


def ordered_rows(rank, chunks):
    pieces = [piece for chunk in chunks for piece in chunk]
    height, width = pieces[0].shape
    cols = min(512, width)
    spec = lambda rows: pl.BlockSpec((rows, cols), lambda i, info: (0, i))
    return pl.pallas_call(
        functools.partial(ordered_kernel, len(chunks[0])),
        grid_spec=pltpu.PrefetchScalarGridSpec(
            num_scalar_prefetch=1,
            grid=(width // cols,),
            in_specs=[spec(height)] * len(pieces),
            out_specs=spec(height * len(pieces)),
        ),
        out_shape=jax.ShapeDtypeStruct((height * len(pieces), width), BF16),
        compiler_params=params(),
        name="ordered_rows",
    )(rank, *pieces)


def rotary_tables(positions):
    exponent = jnp.arange(HD // 2, dtype=F32) * 2.0 / HD
    frequency = ROTARY_BASE ** (-exponent)
    angles = positions.astype(F32)[:, None] * frequency[None, :]
    cosine = jnp.concatenate([jnp.cos(angles), jnp.cos(angles)], axis=-1)
    sine = jnp.concatenate([jnp.sin(angles), jnp.sin(angles)], axis=-1)
    return cosine, sine


def shards(
    inputs,
    lengths,
    routes,
    attn_gain,
    w_query,
    w_key,
    w_value,
    query_gain,
    key_gain,
    w_out,
    ffn_gain,
    router,
    w_gate,
    w_up,
    w_down,
    cotangent,
):
    size, seqs, feat = inputs.shape
    width, head_cols = w_query.shape
    heads = head_cols // HD
    tp_rank, tp_count = lax.axis_index("tp"), lax.axis_size("tp")
    sq_rank, sq_count = lax.axis_index("sq"), lax.axis_size("sq")
    experts = w_gate.shape[0]
    experts_total = router.shape[1]
    all_cols = head_cols * tp_count
    block = width // sq_count
    chunks = CHUNKS
    per = seqs // chunks
    rows_n = per * size
    quarter = rows_n // tp_count
    positions = sq_rank * size + jnp.arange(size, dtype=jnp.int32)
    cosine, sine = rotary_tables(positions)
    group = lambda array: [
        array[:, c * per : (c + 1) * per].transpose(1, 0, 2).reshape(rows_n, -1)
        for c in range(chunks)
    ]
    inputs_c, routes_c = group(inputs), group(routes)
    cotangent_rows = cotangent.transpose(1, 0, 2).reshape(seqs * size, feat)
    info_c = [
        jnp.concatenate(
            [sq_rank[None], tp_rank[None], lengths[c * per : (c + 1) * per]]
        ).astype(jnp.int32)
        for c in range(chunks)
    ]
    rank = tp_rank[None].astype(jnp.int32)
    def attention_in(c, gathered, *others):
        low, normed, inv, query_raw, key_raw, value, squares = front(
            after(rank, *others) if others else rank, gathered, attn_gain, w_query, w_key, w_value
        )
        with jax.named_scope(f"squares{c}"):
            got = exchange([squares] * tp_count)
        return low, normed, inv, query_raw, key_raw, sum(got), value, got[1:]

    def rotated(c, *others):
        query_raw, key_raw, squares, value = ins[c][3:7]
        squares = after(squares, *others) if others else squares
        return rotate(
            query_raw, key_raw, value, squares, query_gain, key_gain, cosine, sine, all_cols
        )

    def gather_heads(c, ready, *others):
        with jax.named_scope(f"heads{c}"):
            own = attn_c[c][0].reshape(rows_n, head_cols)
            return gather_tp(after(own, *ready) if ready else own, *others)

    early_parts = lambda gathered: (gathered[0][1], gathered[0][-2])

    ins, turned, slots_c, attn_c, heads_c, mids, exps = [], [], [], [], [], [], []
    with jax.named_scope("inputs0"):
        x0 = gather_tp(inputs_c[0])
    with jax.named_scope("inputs1"):
        x1_first = first_step(after(inputs_c[1], x0[0][3]))
    ins.append(attention_in(0, x0))
    turned.append(rotated(0, *x1_first[1:]))
    with jax.named_scope("inputs1"):
        x1_second = second_step(x1_first, ins[0][1])
        x1 = third_step(x1_first, x1_second, turned[0][1])
    with jax.named_scope("pairs0"):
        near0 = gather_sides(turned[0][1])
    ins.append(attention_in(1, x1))
    slab = w_out.shape[0] // sq_count
    w_slab = after(block_of(w_out, sq_rank, slab, 0), *ins[1][7])
    w_out_all = lax.all_gather(w_slab, ("tp", "sq"), axis=0, tiled=True)
    with jax.named_scope("cotangent"):
        grads_first = first_step(after(cotangent_rows, *ins[1][7]))
    with jax.named_scope("pairs0"):
        diag0 = gather_diagonal(turned[0][1], [after(side, x1[0][3]) for side in near0])
    turned.append(rotated(1, *diag0, *grads_first[1:]))
    with jax.named_scope("cotangent"):
        grads_second = second_step(grads_first, turned[1][1])
    with jax.named_scope("pairs0"):
        slots_c.append(gather_slots(turned[0][1], near0, *diag0))
    with jax.named_scope("pairs1"):
        near1 = gather_sides(turned[1][1])
    attn_c.append(attn_forward(after(info_c[0], turned[1][1]), turned[0][0], slots_c[0]))
    heads_c.append(gather_heads(0, grads_second))
    with jax.named_scope("pairs1"):
        near1 = [after(side, attn_c[0][2]) for side in near1]
        diag1 = gather_diagonal(turned[1][1], near1)
        slots_c.append(gather_slots(turned[1][1], near1, *diag1))
    with jax.named_scope("cotangent"):
        grads_third = third_step(grads_first, grads_second)
    attn_c.append(
        attn_forward(
            after(info_c[1], *early_parts(heads_c[0])), turned[1][0], slots_c[1]
        )
    )
    grad_all = joined_rows(rank, grads_third)

    def middle_of(c, *others):
        return middle_rows(
            after(rank, *others), heads_c[c], ins[c][0], w_out_all, ffn_gain, router, routes_c[c]
        )

    def hidden_of(c, *others):
        _, _, _, ffn_in, probs, routed = mids[c]
        return expert_hidden(
            after(info_c[c], *others), ffn_in, grad_all, probs, routed, w_gate, w_up, w_down, c
        )

    def back_of(c, *others):
        _, gate_grads, up_grads, inner = exps[c]
        return expert_back(
            after(info_c[c], *others),
            gate_grads,
            up_grads,
            inner,
            mids[c][4],
            router,
            mids[c][3],
            w_gate,
            w_up,
            tp_count,
        )

    def ffn_exchange(c, pieces):
        with jax.named_scope(f"ffn_grad{c}"):
            return exchange(pieces)

    def middle_grad_of(c, pieces, *others):
        return middle_back(
            after(info_c[c], *others), pieces, mids[c][1], mids[c][2], grad_all, ffn_gain, w_out_all, c
        )

    def mixture_of(c, *others):
        pieces = mixture(
            after(info_c[c], *others), exps[c][0], w_down, backs[c][2], tp_count
        )
        with jax.named_scope(f"mixture{c}"):
            return exchange(pieces)

    def output_of(c, pieces):
        total = block_of(mids[c][1], tp_rank, feat, 1)
        for piece in pieces:
            total = total + piece[:rows_n].astype(F32)
        return total.astype(BF16).reshape(per, size, feat).transpose(1, 0, 2)

    def attention_back(c, *others):
        return attn_backward(
            after(info_c[c], *others), turned[c][0], sent[c], *attn_c[c][1:], slots_c[c]
        )

    def cores_of(c):
        with jax.named_scope(f"pair_cores{c}"):
            return scatter_cores(dqs[c][2])

    def diagonal_of(c, received):
        if sq_count != 8:
            return None, []
        with jax.named_scope(f"pair_diagonal{c}"):
            diagonal = scatter_diagonal(dqs[c][1], received)
            return diagonal, send_halves(diagonal)

    def sides_of(c, received, diagonal):
        with jax.named_scope(f"pair_sides{c}"):
            return scatter_sides(dqs[c][1], received, diagonal)

    def stats_of(c, received, blocks):
        query_raw, key_raw, squares = ins[c][3:6]
        operands = (
            dqs[c][0],
            scatter_total(dqs[c][1], received, blocks),
            query_raw,
            key_raw,
            squares,
            query_gain[None, :],
            key_gain[None, :],
            cosine,
            sine,
        )
        stats, gain_qk = back_stats(operands, all_cols)
        with jax.named_scope(f"stats{c}"):
            stats = sum(exchange([stats] * tp_count))
        return operands, stats, gain_qk

    def first_of(c, operands, stats, *others):
        low, _, inv = ins[c][:3]
        raw, pieces, part = back_first(
            after(info_c[c], *others),
            operands,
            stats,
            low,
            inv,
            attn_gain,
            w_query,
            w_key,
            w_value,
            all_cols,
            tp_count,
        )
        with jax.named_scope(f"first{c}"):
            pieces = exchange(pieces)
        return raw, pieces, part

    scatter = lambda g: lax.psum_scatter(g, "sq", scatter_dimension=0, tiled=True)
    spread = lambda g: g.astype(F32).reshape(block, experts, -1).transpose(1, 0, 2)

    backs, dqs = [], []
    mids.append(middle_of(0, attn_c[1][2], *grads_second))
    exps.append(hidden_of(0))
    heads_c.append(gather_heads(1, (), (mids[0][3],), (exps[0][3],)))
    back0, router0 = back_of(0)
    sent0 = ffn_exchange(0, back0)
    mids.append(middle_of(1, back0[0]))
    exps.append(hidden_of(1))
    ffn_list = [m[3] for m in mids]
    w_down_part = weight_grad([grad_all], [e[0] for e in exps])
    backs.append(middle_grad_of(0, sent0, w_down_part))
    sent = [mixture_of(0, backs[0][1])]
    back1, router1 = back_of(1, sent[0][0])
    sent1 = ffn_exchange(1, back1)
    w_up_part = weight_grad(ffn_list, [exps[0][2], after(exps[1][2], back1[0])])
    w_gate_part = weight_grad(
        ffn_list, [exps[0][1], after(exps[1][1], w_up_part, *sent[0][1:])]
    )
    backs.append(middle_grad_of(1, sent1, w_gate_part))
    sent.append(mixture_of(1, backs[1][1]))
    dqs.append(attention_back(0, sent[1][0]))
    cores0 = cores_of(0)
    summed0, diagonal0 = diagonal_of(0, cores0)
    sums0, sides0 = sides_of(0, cores0, diagonal0)
    with jax.named_scope("low_rows0"):
        low0 = exchange([after(backs[0][1], *sent[1][1:])] * tp_count)
    dqs.append(attention_back(1, *sums0))
    cores1 = cores_of(1)
    operands0, stats0, gain0 = stats_of(0, after(cores0, dqs[1][0]), sides0)
    with jax.named_scope("low_rows1"):
        low1 = exchange([after(backs[1][1], *low0[1:])] * tp_count)
    low_all = ordered_rows(rank, [low0, low1])
    raw0, first0, part0 = first_of(0, operands0, stats0, cores1, *low0[1:])
    summed1, diagonal1 = diagonal_of(1, cores1)
    sums1, sides1 = sides_of(1, cores1, diagonal1)

    outputs = [output_of(c, sent[c]) for c in range(2)]
    operands1, stats1, gain1 = stats_of(1, cores1, sides1)
    raw1, first1, part1 = first_of(1, operands1, stats1, low_all, *first0[1:])
    w_down_rows = scatter(after(w_down_part, backs[0][1]))
    w_up_rows = scatter(after(w_up_part, backs[1][1]))
    w_gate_rows = scatter(after(w_gate_part, backs[1][1]))
    w_down_grad = w_down_rows.astype(F32).T.reshape(experts, -1, block)
    w_up_grad, w_gate_grad = spread(w_up_rows), spread(w_gate_rows)
    heads_own = [attn_c[c][0].reshape(rows_n, head_cols) for c in range(2)]
    with jax.named_scope("weights"):
        own = reduce_cores(
            info_c[0],
            [
                ([(i[1], 0) for i in ins], [raw0, raw1]),
                ([(low_all, 0), (low_all, 1)], heads_own),
            ],
        )
        qkv_grad = reduce_chips(own)
    finals = [
        finish(after(info_c[c], own), low_all, pieces, inputs_c[c], ins[c][2], attn_gain, c, per)
        for c, pieces in enumerate((first0, first1))
    ]
    w_out_grad = qkv_grad[:, 3 * head_cols :].T
    small = jnp.concatenate(
        [
            router0 + router1,
            (backs[0][0] + backs[1][0])[None, :],
            (part0 + after(part1, finals[1]))[None, :],
            lax.dynamic_update_slice_in_dim(
                jnp.zeros((2, all_cols), F32), gain0 + gain1, tp_rank * head_cols, 1
            ),
        ],
        axis=0,
    )
    with jax.named_scope("small"):
        small = butterfly(butterfly(small, "sq"), "tp")
    early, late = small[: experts_total + 1], small[experts_total + 1 :]
    return (
        jnp.concatenate(outputs, axis=1),
        jnp.concatenate(finals, axis=0).reshape(seqs, size, feat).transpose(1, 0, 2),
        late[0],
        qkv_grad[:, :head_cols],
        qkv_grad[:, head_cols : 2 * head_cols],
        qkv_grad[:, 2 * head_cols : 3 * head_cols],
        late[1],
        late[2],
        w_out_grad,
        early[experts_total],
        early[:experts_total].T,
        w_gate_grad,
        w_up_grad,
        w_down_grad,
    )


def solution(mesh):
    placed = (
        P("sq", None, "tp"),
        P(),
        P("sq", None, None),
        P(),
        P(None, "tp"),
        P(None, "tp"),
        P(None, "tp"),
        P("tp"),
        P("tp"),
        P("tp", None),
        P(),
        P(),
        P("tp", None, None),
        P("tp", None, None),
        P("tp", None, None),
        P("sq", None, "tp"),
    )
    return jax.shard_map(
        shards,
        mesh=mesh,
        in_specs=placed,
        out_specs=(
            P("sq", None, "tp"),
            P("sq", None, "tp"),
            P(),
            P("sq", "tp"),
            P("sq", "tp"),
            P("sq", "tp"),
            P(),
            P(),
            P("tp", "sq"),
            P(),
            P(),
            P("tp", "sq", None),
            P("tp", "sq", None),
            P("tp", None, "sq"),
        ),
        check_vma=False,
    )
```

```python
import functools

import jax
import jax.numpy as jnp
from jax import lax
from jax.experimental import pallas as pl
from jax.experimental.pallas import tpu as pltpu
from jax.sharding import PartitionSpec as P

HD = 128
EPSILON = 1e-05
ROTARY_BASE = 10000.0
NEGATIVE = -1e30
F32 = jnp.float32
BF16 = jnp.bfloat16
VMEM_LIMIT = 56 * 1024 * 1024
CHUNKS = 2
NT = (((1,), (1,)), ((), ()))
TN = (((0,), (0,)), ((), ()))
NN = (((1,), (0,)), ((), ()))


def dot(left, right, dims=NN):
    return lax.dot_general(left, right, dims, preferred_element_type=F32)


def after(value, *others):
    return lax.optimization_barrier((value, *others))[0]


def shift(block, axis, distance):
    count = lax.axis_size(axis)
    return lax.ppermute(block, axis, [(i, (i + distance) % count) for i in range(count)])


def swap(block, axis, mask):
    return lax.ppermute(block, axis, [(i, i ^ mask) for i in range(lax.axis_size(axis))])


OUTER, INNER = [(0, 1), (1, 0), (2, 3), (3, 2)], [(0, 0), (1, 2), (2, 1), (3, 3)]


def first_step(block):
    count = lax.axis_size("tp")
    if count == 4:
        return [block, lax.ppermute(block, "tp", OUTER), lax.ppermute(block, "tp", INNER)]
    return [block] + [shift(block, "tp", k) for k in range(1, count)]


def second_step(first, *others):
    if lax.axis_size("tp") != 4:
        return []
    _, a1, b1 = first
    return [
        lax.ppermute(after(b1, a1, *others), "tp", OUTER),
        lax.ppermute(after(a1, b1, *others), "tp", INNER),
    ]


def third_step(first, second, *others):
    count = lax.axis_size("tp")
    if count != 4:
        return first, by_distance(count)
    (block, a1, b1), (a2, b2) = first, second
    a3 = lax.ppermute(after(b2, a2, *others), "tp", OUTER)
    return [block, a1, a2, a3, b1, b2], ((0, 1, 2, 3), (1, 0, 4, 5), (5, 4, 0, 1), (3, 2, 1, 0))


def gather_tp(block, second=(), third=()):
    first = first_step(block)
    return third_step(first, second_step(first, *second), *third)


def by_distance(count):
    return tuple(tuple((z - f) % count for f in range(count)) for z in range(count))


def exchange(pieces):
    return [p if k == 0 else shift(p, "tp", k) for k, p in enumerate(pieces)]


def butterfly(value, axis):
    return butterfly_steps(value, axis)[0]


def butterfly_steps(value, axis):
    mask, received = 1, None
    while mask < lax.axis_size(axis):
        received = swap(value, axis, mask)
        value = value + received
        mask *= 2
    return value, received


def block_of(array, index, size, axis):
    return lax.dynamic_slice_in_dim(array, index * size, size, axis)


def gather_sides(pair):
    if lax.axis_size("sq") == 8:
        return swap(pair, "sq", 2), swap(pair, "sq", 4)
    return [swap(pair, "sq", m) for m in range(2, lax.axis_size("sq"), 2)]


def gather_diagonal(pair, sides):
    trio = swap(jnp.stack([pair, *sides]), "sq", 1)
    if lax.axis_size("sq") == 8:
        near, far = sides
        return trio, swap(far[:1], "sq", 2), swap(near[1:], "sq", 4)
    return (trio,)


def gather_slots(pair, sides, trio, *diagonal):
    slots = []
    for k, side in enumerate([pair, *sides]):
        slots += [side, trio[k]]
    if diagonal:
        slots += [diagonal, swap(jnp.concatenate(diagonal), "sq", 1)]
    return slots


def scatter_cores(odd):
    return swap(odd, "sq", 1)


def scatter_diagonal(even, received):
    return add_blocks([[(even, (3, half)), (received, (3, half))] for half in range(2)])


def send_halves(diagonal):
    return [swap(diagonal[half], "sq", 2 + 2 * half) for half in range(2)]


def scatter_sides(even, received, halves):
    sums = []
    for k in range(1, 3 if halves else even.shape[0]):
        terms = [[(even, (k, half)), (received, (k, half))] for half in range(2)]
        if halves:
            terms[2 - k].append((halves[2 - k], ()))
        sums.append(add_blocks(terms))
    return sums, [swap(array, "sq", 2 * k + 2) for k, array in enumerate(sums)]


def scatter_total(even, received, blocks):
    return add_blocks(
        [
            [(even, (0, half)), (received, (0, half))] + [(block, (half,)) for block in blocks]
            for half in range(2)
        ]
    )


def reduce_cores(info, pairs):
    received = swap(relative_grads(info, 1, pairs, None), "sq", 1)
    own = relative_grads(info, 0, pairs, received)
    return own.reshape(lax.axis_size("sq") // 2, -1, own.shape[1])


def reduce_chips(own):
    half = own.shape[2] // 2
    results, came = [], []
    for part in range(2):
        blocks = own[:, :, part * half : (part + 1) * half]
        steps = [1 << b for b in range(own.shape[0].bit_length() - 1)]
        if part:
            steps = steps[::-1]
        kept = {m: blocks[m] for m in range(own.shape[0])}
        for number, step in enumerate(steps):
            give = sorted(m for m in kept if m & step)
            keep = sorted(m for m in kept if not m & step)
            got = swap(jnp.stack([kept[m] for m in give]), "sq", 2 * step)
            if number == 0:
                came.append(got)
            last = number == len(steps) - 1
            kept = {
                m: (kept[m].astype(F32) + got[i].astype(F32)).astype(F32 if last else BF16)
                for i, m in enumerate(keep)
            }
        results.append(kept[0])
    return jnp.concatenate(results, axis=1).astype(F32), came


COST = 100


def cost(flops, bytes_accessed, transcendentals):
    return pl.CostEstimate(
        flops=flops // COST,
        bytes_accessed=bytes_accessed // COST,
        transcendentals=transcendentals // COST,
    )


def add_kernel(counts, *refs):
    first = 0
    for half, count in enumerate(counts):
        total = None
        for ref in refs[first : first + count]:
            part = ref[(0,) * (len(ref.shape) - 2)].astype(F32)
            total = part if total is None else total + part
        refs[-1][half, 0] = total.astype(BF16)
        first += count


def add_blocks(halves):
    shape = halves[0][0][0].shape[-3:]

    def spec(lead):
        return pl.BlockSpec((1,) * (len(lead) + 1) + shape[1:], lambda s: (*lead, s, 0, 0))

    terms = [term for half in halves for term in half]
    return pl.pallas_call(
        functools.partial(add_kernel, [len(half) for half in halves]),
        grid=(shape[0],),
        in_specs=[spec(lead) for _, lead in terms],
        out_specs=pl.BlockSpec((2, 1) + shape[1:], lambda s: (0, s, 0, 0)),
        out_shape=jax.ShapeDtypeStruct((2, *shape), BF16),
        compiler_params=params(),
        name="add_blocks",
    )(*[array for array, _ in terms])


def params():
    return pltpu.CompilerParams(vmem_limit_bytes=VMEM_LIMIT)


def place_columns(rank, table, sources, out_ref):
    width = sources[0].shape[-1]
    for z in range(len(table)):

        @pl.when(rank == z)
        def _(z=z):
            for f, index in enumerate(table[z]):
                out_ref[:, f * width : (f + 1) * width] = sources[index][...]


def row_sums(values):
    cols = values.shape[1]
    total = values[:, :HD]
    for k in range(1, cols // HD):
        total = total + values[:, k * HD : (k + 1) * HD]
    return jnp.sum(total.T, axis=0, keepdims=True)


def as_columns(row):
    return jnp.broadcast_to(row, (HD, row.shape[1])).T


def front_kernel(table, count, info, *refs):
    sources, refs = refs[:count], refs[count:]
    gain_ref, wq_ref, wk_ref, wv_ref = refs[:4]
    low_ref, normed_ref, inv_ref, query_ref, key_ref, value_ref, square_ref = refs[4:]
    place_columns(info[0], table, sources, low_ref)
    rows = low_ref[...].astype(F32)
    inv = lax.rsqrt(jnp.mean(rows * rows, axis=1, keepdims=True) + EPSILON)
    inv_ref[...] = inv
    normed = (rows * inv * gain_ref[...]).astype(BF16)
    normed_ref[...] = normed
    query, key = dot(normed, wq_ref[...]), dot(normed, wk_ref[...])
    query_ref[...] = query
    key_ref[...] = key
    value_ref[...] = dot(normed, wv_ref[...]).astype(BF16)
    square_ref[0:1, :] = row_sums(query * query)
    square_ref[1:2, :] = row_sums(key * key)


def front(rank, gathered, gain, w_query, w_key, w_value):
    sources, table = gathered
    rows, width = sources[0].shape
    total = width * len(table)
    cols = w_query.shape[1]
    tile = min(256, rows)
    spec = lambda cols: pl.BlockSpec((tile, cols), lambda i, info: (i, 0))
    whole = lambda array: pl.BlockSpec(
        array.shape, lambda i, info: (0, 0), pipeline_mode=pl.Buffered(1)
    )
    out = lambda cols, dtype: jax.ShapeDtypeStruct((rows, cols), dtype)
    return pl.pallas_call(
        functools.partial(front_kernel, table, len(sources)),
        grid_spec=pltpu.PrefetchScalarGridSpec(
            num_scalar_prefetch=1,
            grid=(rows // tile,),
            in_specs=[spec(width)] * len(sources)
            + [pl.BlockSpec((1, total), lambda i, info: (0, 0))]
            + [whole(w_query), whole(w_key), whole(w_value)],
            out_specs=[spec(total), spec(total), spec(1), spec(cols), spec(cols), spec(cols)]
            + [pl.BlockSpec((2, tile), lambda i, info: (0, i))],
        ),
        out_shape=[
            out(total, BF16),
            out(total, BF16),
            out(1, F32),
            out(cols, F32),
            out(cols, F32),
            out(cols, BF16),
            jax.ShapeDtypeStruct((2, rows), F32),
        ],
        compiler_params=params(),
        cost_estimate=cost(
            flops=6 * rows * total * cols,
            bytes_accessed=6 * total * cols + 8 * rows * total,
            transcendentals=0,
        ),
        name="front",
    )(rank, *sources, gain[None, :], w_query, w_key, w_value)


def halves(count):
    lane = lax.broadcasted_iota(jnp.int32, (1, HD), 1)
    return jnp.where(lane < HD // 2, 1.0, -1.0)


def rotate_kernel(
    all_cols, q_ref, k_ref, v_ref, square_ref, qg_ref, kg_ref, cos_ref, sin_ref, out_ref, pair_ref
):
    inv = lax.rsqrt(square_ref[...] / all_cols + EPSILON)
    cosine, sine = cos_ref[...], -halves(HD) * sin_ref[...]
    for number, (raw_ref, gain_ref) in enumerate(((q_ref, qg_ref), (k_ref, kg_ref))):
        scale = as_columns(inv[number : number + 1, :])
        for h in range(raw_ref.shape[1] // HD):
            span = slice(h * HD, (h + 1) * HD)
            normed = raw_ref[:, span] * scale * gain_ref[:, span]
            turned = (normed * cosine + pltpu.roll(normed, HD // 2, 1) * sine).astype(BF16)
            if number == 0:
                out_ref[0, :, span] = turned
            else:
                pair_ref[0, 0, :, span] = turned
    pair_ref[1, 0] = v_ref[...]


def rotate(query, key, value, squares, query_gain, key_gain, cosine, sine, all_cols):
    rows, cols = query.shape
    size = cosine.shape[0]
    spec = pl.BlockSpec((size, cols), lambda s: (s, 0))
    one = pl.BlockSpec((1, cols), lambda s: (0, 0))
    turn = pl.BlockSpec((size, HD), lambda s: (0, 0))
    return pl.pallas_call(
        functools.partial(rotate_kernel, all_cols),
        grid=(rows // size,),
        in_specs=[spec, spec, spec, pl.BlockSpec((2, size), lambda s: (0, s))]
        + [one, one, turn, turn],
        out_specs=[
            pl.BlockSpec((1, size, cols), lambda s: (s, 0, 0)),
            pl.BlockSpec((2, 1, size, cols), lambda s: (0, s, 0, 0)),
        ],
        out_shape=[
            jax.ShapeDtypeStruct((rows // size, size, cols), BF16),
            jax.ShapeDtypeStruct((2, rows // size, size, cols), BF16),
        ],
        compiler_params=params(),
        name="rotate",
    )(query, key, value, squares, query_gain[None, :], key_gain[None, :], cosine, sine)


def back_parts(all_cols, refs):
    dq_ref, dkv_ref, q_ref, k_ref, square_ref, qg_ref, kg_ref, cos_ref, sin_ref = refs
    inv = lax.rsqrt(square_ref[...] / all_cols + EPSILON)
    cosine, sine = cos_ref[...], sin_ref[...]
    sign = halves(HD)
    for number, (raw_ref, gain_ref) in enumerate(((q_ref, qg_ref), (k_ref, kg_ref))):
        scale = as_columns(inv[number : number + 1, :])
        for h in range(raw_ref.shape[1] // HD):
            span = slice(h * HD, (h + 1) * HD)
            grad = (dkv_ref[0, 0, :, span] if number else dq_ref[0, :, span]).astype(F32)
            back = grad * cosine + pltpu.roll(grad * sine, HD // 2, 1) * sign
            yield number, span, back, raw_ref[:, span] * scale, scale, gain_ref[:, span]


def back_stats_kernel(all_cols, *refs):
    stat_ref, gain_ref = refs[9:]

    @pl.when(pl.program_id(0) == 0)
    def _():
        gain_ref[...] = jnp.zeros(gain_ref.shape, F32)

    totals = [None, None]
    for number, span, back, hat, _, gain in back_parts(all_cols, refs[:9]):
        product = back * hat
        gain_ref[number : number + 1, span] += jnp.sum(product, axis=0, keepdims=True)
        product = product * gain
        totals[number] = product if totals[number] is None else totals[number] + product
    for number in range(2):
        stat_ref[number : number + 1, :] = row_sums(totals[number])


def back_specs(size, cols):
    spec = pl.BlockSpec((size, cols), lambda s: (s, 0))
    one = pl.BlockSpec((1, cols), lambda s: (0, 0))
    turn = pl.BlockSpec((size, HD), lambda s: (0, 0))
    row = pl.BlockSpec((2, size), lambda s: (0, s))
    return [
        pl.BlockSpec((1, size, cols), lambda s: (s, 0, 0)),
        pl.BlockSpec((2, 1, size, cols), lambda s: (0, s, 0, 0)),
        spec,
        spec,
        row,
        one,
        one,
        turn,
        turn,
    ]


def back_stats(operands, all_cols):
    rows, cols = operands[2].shape
    size = operands[0].shape[1]
    return pl.pallas_call(
        functools.partial(back_stats_kernel, all_cols),
        grid=(rows // size,),
        in_specs=back_specs(size, cols),
        out_specs=[
            pl.BlockSpec((2, size), lambda s: (0, s)),
            pl.BlockSpec((2, cols), lambda s: (0, 0)),
        ],
        out_shape=[
            jax.ShapeDtypeStruct((2, rows), F32),
            jax.ShapeDtypeStruct((2, cols), F32),
        ],
        compiler_params=params(),
        name="back_stats",
    )(*operands)


def back_first_kernel(all_cols, count, info, *refs):
    stat_ref, low_ref, inv_ref, gain_ref, wq_ref, wk_ref, wv_ref = refs[9:16]
    raw_ref, part_ref = refs[16:18]
    first_refs, buffer = refs[18 : 18 + count], refs[18 + count]
    size = buffer.shape[0]
    rows = pl.ds(pl.multiple_of(pl.program_id(0) * size, size), size)
    cols = wq_ref.shape[1]
    stats = stat_ref[...] / all_cols
    for number, span, back, hat, scale, gain in back_parts(all_cols, refs[:9]):
        mean = as_columns(stats[number : number + 1, :])
        raw = scale * (back * gain - hat * mean)
        raw_ref[:, number * cols + span.start : number * cols + span.stop] = raw.astype(BF16)
    raw_ref[:, 2 * cols :] = refs[1][1, 0]
    first = (
        dot(raw_ref[:, :cols], wq_ref[...], NT)
        + dot(raw_ref[:, cols : 2 * cols], wk_ref[...], NT)
        + dot(raw_ref[:, 2 * cols :], wv_ref[...], NT)
    )
    buffer[...] = first.astype(BF16)
    feat = first_refs[0].shape[1]
    for k in range(count):
        target = lax.rem(info[1] + k, count)
        span = pl.ds(pl.multiple_of(target * feat, feat), feat)
        first_refs[k][rows, :] = buffer[:, span]

    @pl.when(pl.program_id(0) == 0)
    def _():
        part_ref[...] = jnp.zeros(part_ref.shape, F32)

    product = first * (low_ref[...].astype(F32) * inv_ref[...])
    part_ref[...] += jnp.sum(product, axis=0, keepdims=True)
    rest = row_sums(product * gain_ref[...])
    line = lax.broadcasted_iota(jnp.int32, (EXTRA, size), 0)
    terms = jnp.zeros((EXTRA, size), F32)
    for term in range(2):
        part = rest.astype(BF16).astype(F32)
        rest = rest - part
        terms = jnp.where(line == 2 * pl.program_id(0) + term, part, terms)
    for ref in first_refs:
        place = ref.shape[0] - EXTRA

        @pl.when(pl.program_id(0) == 0)
        def _(ref=ref, place=place):
            ref[place:, :] = jnp.zeros((EXTRA, feat), BF16)

        ref[place:, :size] += terms.astype(BF16)


EXTRA = 16


def back_first(info, operands, stats, low, inv, gain, w_query, w_key, w_value, all_cols, count):
    rows, cols = operands[2].shape
    size = operands[0].shape[1]
    total = low.shape[1]
    lift = lambda spec: pl.BlockSpec(spec.block_shape, lambda s, info: spec.index_map(s))
    spec = lambda cols: pl.BlockSpec((size, cols), lambda s, info: (s, 0))
    row = lambda count: pl.BlockSpec((count, size), lambda s, info: (0, s))
    whole = lambda array: pl.BlockSpec(
        array.shape, lambda s, info: (0, 0), pipeline_mode=pl.Buffered(1)
    )
    one = pl.BlockSpec((1, total), lambda s, info: (0, 0))
    height = rows + EXTRA
    raw, part, *pieces = pl.pallas_call(
        functools.partial(back_first_kernel, all_cols, count),
        grid_spec=pltpu.PrefetchScalarGridSpec(
            num_scalar_prefetch=1,
            grid=(rows // size,),
            in_specs=[lift(s) for s in back_specs(size, cols)]
            + [row(2), spec(total), spec(1), one]
            + [whole(w_query), whole(w_key), whole(w_value)],
            out_specs=[spec(3 * cols), one]
            + [pl.BlockSpec((height, total // count), lambda s, info: (0, 0))] * count,
            scratch_shapes=[pltpu.VMEM((size, total), BF16)],
        ),
        out_shape=[
            jax.ShapeDtypeStruct((rows, 3 * cols), BF16),
            jax.ShapeDtypeStruct((1, total), F32),
        ]
        + [jax.ShapeDtypeStruct((height, total // count), BF16)] * count,
        compiler_params=params(),
        cost_estimate=cost(
            flops=6 * rows * total * cols,
            bytes_accessed=6 * total * cols + 8 * rows * total,
            transcendentals=0,
        ),
        name="back_first",
    )(info, *operands, stats, low, inv, gain[None, :], w_query, w_key, w_value)
    return raw, pieces, part[0]


def joined_kernel(table, count, info, *refs):
    place_columns(info[0], table, refs[:count], refs[count])


def joined_rows(rank, gathered):
    sources, table = gathered
    rows, width = sources[0].shape
    total = width * len(table)
    tile = min(256, rows)
    spec = lambda cols: pl.BlockSpec((tile, cols), lambda i, info: (i, 0))
    return pl.pallas_call(
        functools.partial(joined_kernel, table, len(sources)),
        grid_spec=pltpu.PrefetchScalarGridSpec(
            num_scalar_prefetch=1,
            grid=(rows // tile,),
            in_specs=[spec(width)] * len(sources),
            out_specs=spec(total),
        ),
        out_shape=jax.ShapeDtypeStruct((rows, total), BF16),
        compiler_params=params(),
        name="joined_rows",
    )(rank, *sources)


def relative_grads_kernel(counts, info, *refs):
    more = refs[2 * sum(counts) : -1]
    first, start = 0, 0
    for count in counts:
        lefts, rights = refs[first : first + count], refs[first + count : first + 2 * count]
        first += 2 * count
        total = dot(lefts[0][...], rights[0][...], TN)
        for left, right in zip(lefts[1:], rights[1:]):
            total += dot(left[...], right[...], TN)
        span = slice(start, start + total.shape[1])
        start = span.stop
        for ref in more:
            total += ref[:, span].astype(F32)
        refs[-1][:, span] = total.astype(BF16)


def relative_grads(info, parity, pairs, more):
    blocks = lax.axis_size("sq")
    height = pairs[0][0][0][0].shape[1] // blocks
    specs, operands, width = [], [], 0
    for lefts, rights in pairs:
        width += rights[0].shape[1]
        for (_, chunk), right in zip(lefts, rights):
            specs.append(
                pl.BlockSpec(
                    (right.shape[0], height),
                    lambda m, info, chunk=chunk: (
                        chunk,
                        jnp.bitwise_xor(info[0], 2 * m + parity),
                    ),
                )
            )
        specs += [
            pl.BlockSpec(right.shape, lambda m, info: (0, 0), pipeline_mode=pl.Buffered(1))
            for right in rights
        ]
        operands += [left for left, _ in lefts] + list(rights)
    out = pl.BlockSpec((height, width), lambda m, info: (m, 0))
    if more is not None:
        specs.append(out)
        operands.append(more)
    return pl.pallas_call(
        functools.partial(relative_grads_kernel, [len(lefts) for lefts, _ in pairs]),
        grid_spec=pltpu.PrefetchScalarGridSpec(
            num_scalar_prefetch=1, grid=(blocks // 2,), in_specs=specs, out_specs=out
        ),
        out_shape=jax.ShapeDtypeStruct((height * blocks // 2, width), BF16),
        compiler_params=params(),
        name="relative_grads",
    )(info, *operands)


def middle_kernel(table, count, info, *refs):
    sources = refs[:count]
    low_ref, w_ref, gain_ref, router_ref, routes_ref = refs[count : count + 5]
    attn_ref, middle_ref, inv_ref, ffn_ref, prob_ref, routed_ref = refs[count + 5 :]
    place_columns(info[0], table, sources, attn_ref)
    middle = low_ref[...].astype(F32) + dot(attn_ref[...], w_ref[...])
    middle_ref[...] = middle
    inv = lax.rsqrt(jnp.mean(middle * middle, axis=1, keepdims=True) + EPSILON)
    inv_ref[...] = inv
    ffn_in = (middle * inv * gain_ref[...]).astype(BF16)
    ffn_ref[...] = ffn_in
    logits = dot(ffn_in, router_ref[...])
    powers = jnp.exp(logits - jnp.max(logits, axis=1, keepdims=True))
    prob_ref[...] = powers / jnp.sum(powers, axis=1, keepdims=True)
    routes = routes_ref[...]
    ids = lax.broadcasted_iota(jnp.int32, logits.shape, 1)
    routed = jnp.zeros(logits.shape, F32)
    for r in range(routes.shape[1]):
        routed = jnp.where(routes[:, r : r + 1] == ids, 1.0, routed)
    routed_ref[...] = routed


def middle_rows(rank, gathered, low, w_out, gain, router, routes):
    sources, table = gathered
    rows, width = sources[0].shape
    total = low.shape[1]
    experts = router.shape[1]
    tile = min(256, rows)
    spec = lambda cols: pl.BlockSpec((tile, cols), lambda i, info: (i, 0))
    whole = lambda array: pl.BlockSpec(
        array.shape, lambda i, info: (0, 0), pipeline_mode=pl.Buffered(1)
    )
    out = lambda cols, dtype: jax.ShapeDtypeStruct((rows, cols), dtype)
    return pl.pallas_call(
        functools.partial(middle_kernel, table, len(sources)),
        grid_spec=pltpu.PrefetchScalarGridSpec(
            num_scalar_prefetch=1,
            grid=(rows // tile,),
            in_specs=[spec(width)] * len(sources)
            + [spec(total), whole(w_out), pl.BlockSpec((1, total), lambda i, info: (0, 0))]
            + [whole(router), spec(routes.shape[1])],
            out_specs=[
                spec(width * len(table)),
                spec(total),
                spec(1),
                spec(total),
                spec(experts),
                spec(experts),
            ],
        ),
        out_shape=[
            out(width * len(table), BF16),
            out(total, F32),
            out(1, F32),
            out(total, BF16),
            out(experts, F32),
            out(experts, F32),
        ],
        compiler_params=params(),
        cost_estimate=cost(
            flops=2 * rows * total * total,
            bytes_accessed=2 * total * total + 12 * rows * total,
            transcendentals=0,
        ),
        name="middle_rows",
    )(rank, *sources, low, w_out, gain[None, :], router, routes)


def weight_grad_kernel(count, parts, *refs):
    height = refs[count].shape[0]
    left = lambda i: refs[i][...] if parts == 1 else refs[0][i * height : (i + 1) * height, :]
    total = dot(left(0), refs[count][...], TN)
    for i in range(1, len(refs) - 1 - count):
        total += dot(left(i), refs[count + i][...], TN)
    refs[-1][...] = total.astype(BF16)


def weight_grad(lefts, rights):
    rows, height = rights[0].shape[0], lefts[0].shape[1]
    width = rights[0].shape[1]
    parts = lefts[0].shape[0] // rows
    tall = min(2048, height)
    cols = min(512, width)
    return pl.pallas_call(
        functools.partial(weight_grad_kernel, len(lefts), parts),
        grid=(width // cols, height // tall),
        in_specs=[pl.BlockSpec((rows * parts, tall), lambda j, i: (0, i))] * len(lefts)
        + [pl.BlockSpec((rows, cols), lambda j, i: (0, j))] * len(rights),
        out_specs=pl.BlockSpec((tall, cols), lambda j, i: (i, j)),
        out_shape=jax.ShapeDtypeStruct((height, width), BF16),
        compiler_params=params(),
        cost_estimate=cost(
            flops=2 * rows * len(rights) * height * width,
            bytes_accessed=2 * (rows * len(rights) * (height + width) + height * width),
            transcendentals=0,
        ),
        name="weight_grad",
    )(*lefts, *rights)


def slot_operands(kv_slots):
    arrays, places = [], []
    for slot in kv_slots:
        if isinstance(slot, tuple):
            places.append(((len(arrays), 0), (len(arrays) + 1, 0)))
            arrays += list(slot)
        else:
            places.append(((len(arrays), 0), (len(arrays), 1)))
            arrays.append(slot)
    size = arrays[0].shape[2]
    specs = [
        pl.BlockSpec((a.shape[0], 1, size, HD), lambda s, h, info: (0, s, 0, h)) for a in arrays
    ]
    return arrays, specs, places


def attn_forward_kernel(places, count, info, q_ref, *refs):
    kv_refs, (low_ref, full_ref, lse_ref, top, total, accum) = refs[:count], refs[count:]
    rank = info[0]
    length = info[2 + pl.program_id(0)]
    queries = q_ref[0]
    size = queries.shape[0]
    top[...] = jnp.full(top.shape, NEGATIVE, F32)
    total[...] = jnp.zeros(total.shape, F32)
    accum[...] = jnp.zeros(accum.shape, F32)
    key_row = lax.broadcasted_iota(jnp.int32, (size, size), 0)
    query_col = lax.broadcasted_iota(jnp.int32, (size, size), 1)
    for slot, ((ka, ki), (va, vi)) in enumerate(places):
        block = rank ^ slot
        start = block * size

        @pl.when((block <= rank) & (start < length))
        def _(slot=slot, start=start, ka=ka, ki=ki, va=va, vi=vi):
            scores = dot(kv_refs[ka][ki, 0], queries, NT) * HD**-0.5
            allowed = key_row + start < length
            if slot == 0:
                allowed = allowed & (key_row <= query_col)
            scores = jnp.where(allowed, scores, NEGATIVE)
            newest = jnp.maximum(top[...], jnp.max(scores, axis=0, keepdims=True))
            weights = jnp.exp(scores - newest)
            factor = jnp.exp(top[...] - newest)
            top[...] = newest
            total[...] = total[...] * factor + jnp.sum(weights, axis=0, keepdims=True)
            accum[...] = accum[...] * factor + dot(kv_refs[va][vi, 0], weights.astype(BF16), TN)

    result = (accum[...] / total[...]).T
    full_ref[0] = result
    low_ref[0] = result.astype(BF16)
    lse_ref[0, 0] = top[...] + jnp.log(total[...])


def attn_forward(info, queries, kv_slots):
    seqs, size, columns = queries.shape
    heads = columns // HD
    slots = len(kv_slots)
    arrays, specs, places = slot_operands(kv_slots)
    row_spec = pl.BlockSpec((1, size, HD), lambda s, h, info: (s, 0, h))
    lse_spec = pl.BlockSpec((1, 1, 1, size), lambda s, h, info: (s, h, 0, 0))
    return pl.pallas_call(
        functools.partial(attn_forward_kernel, places, len(arrays)),
        grid_spec=pltpu.PrefetchScalarGridSpec(
            num_scalar_prefetch=1,
            grid=(seqs, heads),
            in_specs=[row_spec] + specs,
            out_specs=[row_spec, row_spec, lse_spec],
            scratch_shapes=[
                pltpu.VMEM((1, size), F32),
                pltpu.VMEM((1, size), F32),
                pltpu.VMEM((HD, size), F32),
            ],
        ),
        out_shape=[
            jax.ShapeDtypeStruct(queries.shape, BF16),
            jax.ShapeDtypeStruct(queries.shape, F32),
            jax.ShapeDtypeStruct((seqs, heads, 1, size), F32),
        ],
        compiler_params=params(),
        cost_estimate=cost(
            flops=8 * seqs * heads * slots * size * size * HD,
            bytes_accessed=4 * seqs * size * columns * (slots + 2),
            transcendentals=seqs * heads * slots * size * size,
        ),
        name="attn_forward",
    )(info, queries, *arrays)


def attn_backward_kernel(places, count, tp_count, info, q_ref, full_ref, lse_ref, *refs):
    grad_refs, refs = refs[:tp_count], refs[tp_count:]
    kv_refs, (dq_ref, even_ref, odd_ref, accum, grad_buf) = refs[:count], refs[count:]
    rank = info[0]
    length = info[2 + pl.program_id(0)]
    queries = q_ref[0]
    size = queries.shape[0]
    piece = size * pl.num_programs(0) // tp_count
    for i in range(size // piece):
        sender = pl.program_id(0) * (size // piece) + i
        distance = lax.rem(info[1] - sender + tp_count, tp_count)
        for k in range(tp_count):

            @pl.when(distance == k)
            def _(i=i, k=k):
                grad_buf[i * piece : (i + 1) * piece, :] = grad_refs[k][...]

    grads = grad_buf[...]
    lse = lse_ref[0, 0]
    delta = jnp.sum((grads.astype(F32) * full_ref[0]).T, axis=0, keepdims=True)
    accum[...] = jnp.zeros(accum.shape, F32)
    key_row = lax.broadcasted_iota(jnp.int32, (size, size), 0)
    query_col = lax.broadcasted_iota(jnp.int32, (size, size), 1)
    for slot, ((ka, ki), (va, vi)) in enumerate(places):
        block = rank ^ slot
        start = block * size
        out_ref = odd_ref if slot % 2 else even_ref
        live = (block <= rank) & (start < length)

        @pl.when(live)
        def _(slot=slot, start=start, out_ref=out_ref, ka=ka, ki=ki, va=va, vi=vi):
            keys, values = kv_refs[ka][ki, 0], kv_refs[va][vi, 0]
            scores = dot(keys, queries, NT) * HD**-0.5
            allowed = key_row + start < length
            if slot == 0:
                allowed = allowed & (key_row <= query_col)
            weights = jnp.where(allowed, jnp.exp(scores - lse), 0.0)
            back = dot(values, grads, NT)
            score_grad = (weights * (back - delta)).astype(BF16)
            out_ref[slot // 2, 1, 0] = dot(weights.astype(BF16), grads).astype(BF16)
            out_ref[slot // 2, 0, 0] = (dot(score_grad, queries) * HD**-0.5).astype(BF16)
            accum[...] += dot(score_grad, keys, TN)

        @pl.when(jnp.logical_not(live))
        def _(slot=slot, out_ref=out_ref):
            out_ref[slot // 2, :, 0] = jnp.zeros((2,) + queries.shape, BF16)

    dq_ref[0] = (accum[...] * HD**-0.5).astype(BF16)


def attn_backward(info, queries, grad_pieces, full, lse, kv_slots):
    seqs, size, columns = queries.shape
    heads = columns // HD
    slots = len(kv_slots)
    arrays, specs, places = slot_operands(kv_slots)
    piece = size * seqs // len(grad_pieces)
    last = grad_pieces[0].shape[0] // piece - 1
    row_spec = pl.BlockSpec((1, size, HD), lambda s, h, info: (s, 0, h))
    piece_spec = pl.BlockSpec((piece, HD), lambda s, h, info: (last, h))
    lse_spec = pl.BlockSpec((1, 1, 1, size), lambda s, h, info: (s, h, 0, 0))
    out_spec = pl.BlockSpec((slots // 2, 2, 1, size, HD), lambda s, h, info: (0, 0, s, 0, h))
    out_shape = jax.ShapeDtypeStruct((slots // 2, 2, seqs, size, columns), BF16)
    return pl.pallas_call(
        functools.partial(attn_backward_kernel, places, len(arrays), len(grad_pieces)),
        grid_spec=pltpu.PrefetchScalarGridSpec(
            num_scalar_prefetch=1,
            grid=(seqs, heads),
            in_specs=[row_spec, row_spec, lse_spec] + [piece_spec] * len(grad_pieces) + specs,
            out_specs=[row_spec, out_spec, out_spec],
            scratch_shapes=[pltpu.VMEM((size, HD), F32), pltpu.VMEM((size, HD), BF16)],
        ),
        out_shape=[jax.ShapeDtypeStruct(queries.shape, BF16), out_shape, out_shape],
        compiler_params=params(),
        cost_estimate=cost(
            flops=20 * seqs * heads * slots * size * size * HD,
            bytes_accessed=8 * seqs * size * columns * (slots + 2),
            transcendentals=seqs * heads * slots * size * size,
        ),
        name="attn_backward",
    )(info, queries, full, lse, *grad_pieces, *arrays)


def expert_hidden_kernel(
    tile,
    info,
    x_ref,
    g_ref,
    prob_ref,
    routed_ref,
    wg_ref,
    wu_ref,
    wd_ref,
    gh_ref,
    gp_ref,
    up_ref,
    gg_ref,
):
    expert, block = pl.program_id(0), pl.program_id(1)
    rows = x_ref.shape[0]

    @pl.when((expert == 0) & (block == 0))
    def _():
        gg_ref[...] = jnp.zeros(gg_ref.shape, F32)

    for i in range(rows // tile):
        span = slice(i * tile, (i + 1) * tile)
        tokens = x_ref[span, :]
        gate_pre = dot(tokens, wg_ref[0])
        up_pre = dot(tokens, wu_ref[0])
        back = dot(g_ref[span, :], wd_ref[0], NT)
        probs = prob_ref[span, :]
        lane = lax.broadcasted_iota(jnp.int32, probs.shape, 1)
        chosen = (lane == info[1] * pl.num_programs(0) + expert) & (routed_ref[span, :] > 0.5)
        gate = jnp.sum(jnp.where(chosen, probs, 0.0), axis=1, keepdims=True)
        sigmoid = 1.0 / (1.0 + jnp.exp(-gate_pre))
        silu = gate_pre * sigmoid
        hidden = silu * up_pre
        inner = jnp.sum(hidden * back, axis=1, keepdims=True)
        gg_ref[span, :] += jnp.where(chosen, inner, 0.0)
        gh_ref[span, :] = (gate * hidden).astype(BF16)
        hidden_grad = gate * back
        gp_ref[span, :] = (
            hidden_grad * up_pre * (sigmoid + silu * (1.0 - sigmoid))
        ).astype(BF16)
        up_ref[span, :] = (hidden_grad * silu).astype(BF16)


def expert_hidden(info, tokens, grads, probs, routed, w_gate, w_up, w_down, chunk):
    rows, width = tokens.shape
    experts, _, units = w_gate.shape
    cols = min(512, units)
    tile = min(512, rows)
    whole = pl.BlockSpec((rows, width), lambda e, f, info: (0, 0), pipeline_mode=pl.Buffered(1))
    part = pl.BlockSpec((rows, width), lambda e, f, info: (chunk, 0), pipeline_mode=pl.Buffered(1))
    small = pl.BlockSpec(probs.shape, lambda e, f, info: (0, 0))
    wide = pl.BlockSpec((1, width, cols), lambda e, f, info: (e, 0, f))
    tall = pl.BlockSpec((1, cols, width), lambda e, f, info: (e, f, 0))
    result = pl.BlockSpec((rows, cols), lambda e, f, info: (0, e * (units // cols) + f))
    out = jax.ShapeDtypeStruct((rows, experts * units), BF16)
    return pl.pallas_call(
        functools.partial(expert_hidden_kernel, tile),
        grid_spec=pltpu.PrefetchScalarGridSpec(
            num_scalar_prefetch=1,
            grid=(experts, units // cols),
            in_specs=[whole, part, small, small, wide, wide, tall],
            out_specs=[result, result, result, small],
        ),
        out_shape=[out, out, out, jax.ShapeDtypeStruct(probs.shape, F32)],
        compiler_params=params(),
        cost_estimate=cost(
            flops=6 * rows * width * experts * units,
            bytes_accessed=6 * width * experts * units + 6 * rows * experts * units,
            transcendentals=rows * experts * units,
        ),
        name="expert_hidden",
    )(info, tokens, grads, probs, routed, w_gate, w_up, w_down)


def expert_back_kernel(
    count, info, gp_ref, up_ref, gg_ref, prob_ref, router_ref, x_ref, wg_ref, wu_ref, *refs
):
    out_refs, lg_ref, rg_ref, accum = refs[:count], refs[count], refs[count + 1], refs[count + 2]
    expert, block = pl.program_id(0), pl.program_id(1)
    cols = wg_ref.shape[1]
    span = pl.ds(pl.multiple_of(block * cols, cols), cols)

    @pl.when((expert == 0) & (block == 0))
    def _():
        probs, inner = prob_ref[...], gg_ref[...]
        lg_ref[...] = probs * (inner - jnp.sum(probs * inner, axis=1, keepdims=True))

    @pl.when(expert == 0)
    def _():
        accum[:, span] = lax.dot_general(
            lg_ref[...],
            router_ref[...].astype(F32),
            NT,
            precision=lax.Precision.HIGHEST,
            preferred_element_type=F32,
        )

    accum[:, span] += dot(gp_ref[...], wg_ref[0], NT) + dot(up_ref[...], wu_ref[0], NT)

    @pl.when(expert == 0)
    def _():
        rest = lg_ref[...]
        total = jnp.zeros((rest.shape[1], cols), F32)
        for _ in range(3):
            part = rest.astype(BF16)
            rest = rest - part.astype(F32)
            total += dot(part, x_ref[...], TN)
        rg_ref[...] = total

    @pl.when(expert == pl.num_programs(0) - 1)
    def _():
        height = out_refs[0].shape[0]
        for k in range(count):
            target = lax.rem(info[1] + k, count)
            rows = pl.ds(pl.multiple_of(target * height, height), height)
            out_refs[k][:, span] = accum[rows, span].astype(BF16)


def expert_back(info, gate_grads, up_grads, inner, probs, router, tokens, w_gate, w_up, count):
    rows = gate_grads.shape[0]
    experts, width, units = w_gate.shape
    total = router.shape[1]
    cols = min(1024, width)
    left = pl.BlockSpec((rows, units), lambda e, d, info: (0, e))
    small = pl.BlockSpec((rows, total), lambda e, d, info: (0, 0))
    weight = pl.BlockSpec((1, cols, units), lambda e, d, info: (e, d, 0))
    piece = pl.BlockSpec((rows // count, width), lambda e, d, info: (0, 0))
    last = width // cols - 1
    *pieces, _, router_grad = pl.pallas_call(
        functools.partial(expert_back_kernel, count),
        grid_spec=pltpu.PrefetchScalarGridSpec(
            num_scalar_prefetch=1,
            grid=(experts, width // cols),
            in_specs=[
                left,
                left,
                small,
                small,
                pl.BlockSpec((cols, total), lambda e, d, info: (d, 0)),
                pl.BlockSpec((rows, cols), lambda e, d, info: (0, jnp.where(e == 0, d, last))),
                weight,
                weight,
            ],
            out_specs=[piece] * count
            + [
                small,
                pl.BlockSpec((total, cols), lambda e, d, info: (0, jnp.where(e == 0, d, last))),
            ],
            scratch_shapes=[pltpu.VMEM((rows, width), F32)],
        ),
        out_shape=[jax.ShapeDtypeStruct((rows // count, width), BF16)] * count
        + [jax.ShapeDtypeStruct((rows, total), F32), jax.ShapeDtypeStruct((total, width), F32)],
        compiler_params=params(),
        cost_estimate=cost(
            flops=4 * rows * width * experts * units,
            bytes_accessed=4 * width * experts * units + 6 * rows * experts * units,
            transcendentals=0,
        ),
        name="expert_back",
    )(info, gate_grads, up_grads, inner, probs, router, tokens, w_gate, w_up)
    return pieces, router_grad


def mixture_kernel(count, info, hidden_ref, w_ref, *refs):
    head_refs, own_refs, out_refs = refs[:count], refs[count : 2 * count], refs[2 * count :]
    rows, height = hidden_ref.shape[0], own_refs[0].shape[0]
    result = dot(hidden_ref[...], w_ref[...]).astype(BF16)
    for k in range(count):

        @pl.when(pl.program_id(0) == k)
        def _(k=k):
            out_refs[k][:rows] = result
            out_refs[k][rows : rows + height] = own_refs[k][...]
            out_refs[k][rows + height :] = head_refs[k][...]


def mixture(info, hidden, w_down, heads, own, count):
    rows, units = hidden.shape
    width = w_down.shape[-1]
    feat = width // count
    height = heads[0].shape[0]
    piece = pl.BlockSpec((rows + 2 * height, feat), lambda k, info: (0, 0))
    row = pl.BlockSpec((height, feat), lambda k, info: (0, 0))
    return pl.pallas_call(
        functools.partial(mixture_kernel, count),
        grid_spec=pltpu.PrefetchScalarGridSpec(
            num_scalar_prefetch=1,
            grid=(count,),
            in_specs=[
                pl.BlockSpec((rows, units), lambda k, info: (0, 0), pipeline_mode=pl.Buffered(1)),
                pl.BlockSpec((units, feat), lambda k, info: (0, lax.rem(info[1] + k, count))),
            ]
            + [row] * (2 * count),
            out_specs=[piece] * count,
        ),
        out_shape=[jax.ShapeDtypeStruct((rows + 2 * height, feat), BF16)] * count,
        compiler_params=params(),
        cost_estimate=cost(
            flops=2 * rows * units * width,
            bytes_accessed=2 * (rows * units + units * width + rows * width),
            transcendentals=0,
        ),
        name="mixture",
    )(info, hidden, w_down.reshape(units, width), *heads, *own)


def middle_back_kernel(count, info, *refs):
    piece_refs, refs = refs[:count], refs[count:]
    middle_ref, inv_ref, grad_ref, gain_ref, w_ref = refs[:5]
    part_ref, low_ref, out_refs, own_refs = refs[5], refs[6], refs[7 : 7 + count], refs[7 + count :]
    ffn_grad = piece_refs[0][...].astype(F32)
    for k in range(1, count):
        ffn_grad = ffn_grad + piece_refs[k][...].astype(F32)
    inv = inv_ref[...]
    hat = middle_ref[...] * inv
    part_ref[...] = jnp.sum(ffn_grad * hat, axis=0, keepdims=True)
    gained = ffn_grad * gain_ref[...]
    mean = jnp.mean(gained * hat, axis=1, keepdims=True)
    low = (grad_ref[...].astype(F32) + inv * (gained - hat * mean)).astype(BF16)
    low_ref[...] = low
    cols, feat = out_refs[0].shape[1], own_refs[0].shape[1]
    for k in range(count):
        target = lax.rem(info[1] + k, count)
        own_refs[k][...] = low_ref[:, pl.ds(pl.multiple_of(target * feat, feat), feat)]
        rows = pl.ds(pl.multiple_of(target * cols, cols), cols)
        out_refs[k][...] = dot(low, w_ref[rows, :], NT).astype(BF16)


def middle_back(info, pieces, middle, inv, grads, gain, w_out, chunk):
    count = len(pieces)
    height, width = pieces[0].shape
    cols = w_out.shape[0] // count
    whole = lambda array: pl.BlockSpec(array.shape, lambda i, info: (0, 0))
    own = lambda cols: pl.BlockSpec((height, cols), lambda i, info: (info[1], 0))
    part = pl.BlockSpec((height, width), lambda i, info: (chunk * count + info[1], 0))
    first = lambda rows, cols: pl.BlockSpec((rows, cols), lambda i, info: (0, 0))
    out = lambda rows, cols, dtype: jax.ShapeDtypeStruct((rows, cols), dtype)
    part, low, *rest = pl.pallas_call(
        functools.partial(middle_back_kernel, count),
        grid_spec=pltpu.PrefetchScalarGridSpec(
            num_scalar_prefetch=1,
            grid=(1,),
            in_specs=[first(height, width)] * count
            + [own(width), own(1), part, first(1, width), whole(w_out)],
            out_specs=[first(1, width), first(height, width)]
            + [first(height, cols)] * count
            + [first(height, width // count)] * count,
        ),
        out_shape=[out(1, width, F32), out(height, width, BF16)]
        + [out(height, cols, BF16)] * count
        + [out(height, width // count, BF16)] * count,
        compiler_params=params(),
        cost_estimate=cost(
            flops=2 * height * width * width, bytes_accessed=2 * width * width, transcendentals=0
        ),
        name="middle_back",
    )(info, *pieces, middle, inv, grads, gain[None, :], w_out)
    return part[0], low, rest[:count], rest[count:]


def finish_kernel(count, info, *refs):
    sent_refs, first_refs = refs[:count], refs[count : 2 * count]
    x_ref, inv_ref, gain_ref, out_ref = refs[2 * count :]
    height = sent_refs[0].shape[0]
    pieces = out_ref.shape[0] // height
    for i in range(pieces):
        distance = lax.rem(info[1] - pl.program_id(0) * pieces - i + 2 * count, count)
        for k in range(count):

            @pl.when(distance == k)
            def _(i=i, k=k):
                out_ref[i * height : (i + 1) * height, :] = sent_refs[k][...].astype(F32)

    size, width = out_ref.shape[0], count * x_ref.shape[1]
    rows = pl.ds(pl.multiple_of(pl.program_id(0) * size, size), size)
    place = first_refs[0].shape[0] - EXTRA
    first, terms = None, None
    for ref in first_refs:
        part, extra = ref[rows, :].astype(F32), ref[place:, :size].astype(F32)
        first = part if first is None else first + part
        terms = extra if terms is None else terms + extra
    line = lax.broadcasted_iota(jnp.int32, terms.shape, 0)
    own = jnp.where(line // 2 == pl.program_id(0), terms, 0.0)
    inner = as_columns(jnp.sum(own, axis=0, keepdims=True) / width)[:, :1]
    inv = inv_ref[...]
    hat = x_ref[...].astype(F32) * inv
    out_ref[...] += inv * (gain_ref[...] * first - hat * inner)


def finish(info, sent_pieces, first_pieces, x, inv, gain, seqs):
    count = len(first_pieces)
    rows, feat = x.shape
    size = rows // seqs
    one = lambda array: pl.BlockSpec(array.shape, lambda i, info: (0, 0))
    own = lambda cols: pl.BlockSpec((size, cols), lambda i, info: (i, 0))
    return pl.pallas_call(
        functools.partial(finish_kernel, count),
        grid_spec=pltpu.PrefetchScalarGridSpec(
            num_scalar_prefetch=1,
            grid=(seqs,),
            in_specs=[pl.BlockSpec((rows // count, feat), lambda i, info: (count, 0))] * count
            + [one(a) for a in first_pieces]
            + [own(feat), own(1), pl.BlockSpec((1, feat), lambda i, info: (0, info[1]))],
            out_specs=own(feat),
        ),
        out_shape=jax.ShapeDtypeStruct((rows, feat), F32),
        compiler_params=params(),
        name="finish",
    )(info, *sent_pieces, *first_pieces, x, inv, gain[None, :])


def spread_kernel(turned, in_ref, out_ref):
    block = in_ref[...].astype(F32)
    out_ref[0] = block.T if turned else block


def spread(rows, experts, turned):
    height, width = rows.shape
    units = width // experts
    shape = (units, height) if turned else (height, units)
    return pl.pallas_call(
        functools.partial(spread_kernel, turned),
        grid=(experts,),
        in_specs=[pl.BlockSpec((height, units), lambda e: (0, e))],
        out_specs=pl.BlockSpec((1, *shape), lambda e: (e, 0, 0)),
        out_shape=jax.ShapeDtypeStruct((experts, *shape), F32),
        compiler_params=params(),
        name="spread",
    )(rows)


def rotary_tables(positions):
    exponent = jnp.arange(HD // 2, dtype=F32) * 2.0 / HD
    frequency = ROTARY_BASE ** (-exponent)
    angles = positions.astype(F32)[:, None] * frequency[None, :]
    cosine = jnp.concatenate([jnp.cos(angles), jnp.cos(angles)], axis=-1)
    sine = jnp.concatenate([jnp.sin(angles), jnp.sin(angles)], axis=-1)
    return cosine, sine


def shards(
    inputs,
    lengths,
    routes,
    attn_gain,
    w_query,
    w_key,
    w_value,
    query_gain,
    key_gain,
    w_out,
    ffn_gain,
    router,
    w_gate,
    w_up,
    w_down,
    cotangent,
):
    size, seqs, feat = inputs.shape
    width, head_cols = w_query.shape
    heads = head_cols // HD
    tp_rank, tp_count = lax.axis_index("tp"), lax.axis_size("tp")
    sq_rank, sq_count = lax.axis_index("sq"), lax.axis_size("sq")
    experts = w_gate.shape[0]
    experts_total = router.shape[1]
    all_cols = head_cols * tp_count
    block = width // sq_count
    chunks = CHUNKS
    per = seqs // chunks
    rows_n = per * size
    quarter = rows_n // tp_count
    positions = sq_rank * size + jnp.arange(size, dtype=jnp.int32)
    cosine, sine = rotary_tables(positions)
    group = lambda array: [
        array[:, c * per : (c + 1) * per].transpose(1, 0, 2).reshape(rows_n, -1)
        for c in range(chunks)
    ]
    inputs_c, routes_c = group(inputs), group(routes)
    cotangent_rows = cotangent.transpose(1, 0, 2).reshape(seqs * size, feat)
    info_c = [
        jnp.concatenate(
            [sq_rank[None], tp_rank[None], lengths[c * per : (c + 1) * per]]
        ).astype(jnp.int32)
        for c in range(chunks)
    ]
    rank = tp_rank[None].astype(jnp.int32)
    def attention_in(c, gathered, *others):
        low, normed, inv, query_raw, key_raw, value, squares = front(
            after(rank, *others) if others else rank, gathered, attn_gain, w_query, w_key, w_value
        )
        with jax.named_scope(f"squares{c}"):
            got = exchange([squares] * tp_count)
        return low, normed, inv, query_raw, key_raw, sum(got), value, got[1:]

    def rotated(c, *others):
        query_raw, key_raw, squares, value = ins[c][3:7]
        squares = after(squares, *others) if others else squares
        return rotate(
            query_raw, key_raw, value, squares, query_gain, key_gain, cosine, sine, all_cols
        )

    def gather_heads(c, ready, *others):
        with jax.named_scope(f"heads{c}"):
            own = attn_c[c][0].reshape(rows_n, head_cols)
            return gather_tp(after(own, *ready) if ready else own, *others)

    early_parts = lambda gathered: (gathered[0][1], gathered[0][-2])

    ins, turned, slots_c, attn_c, heads_c, mids, exps = [], [], [], [], [], [], []
    with jax.named_scope("inputs0"):
        x0 = gather_tp(inputs_c[0])
    with jax.named_scope("inputs1"):
        x1_first = first_step(after(inputs_c[1], x0[0][3]))
    ins.append(attention_in(0, x0))
    turned.append(rotated(0, *x1_first[1:]))
    with jax.named_scope("inputs1"):
        x1_second = second_step(x1_first, ins[0][1])
        x1 = third_step(x1_first, x1_second, turned[0][1])
    with jax.named_scope("pairs0"):
        near0 = gather_sides(turned[0][1])
    ins.append(attention_in(1, x1))
    slab = w_out.shape[0] // sq_count
    w_slab = after(block_of(w_out, sq_rank, slab, 0), *ins[1][7])
    w_out_all = lax.all_gather(w_slab, ("tp", "sq"), axis=0, tiled=True)
    with jax.named_scope("cotangent"):
        grads_first = first_step(after(cotangent_rows, *ins[1][7]))
    with jax.named_scope("pairs0"):
        diag0 = gather_diagonal(turned[0][1], [after(side, x1[0][3]) for side in near0])
    turned.append(rotated(1, *diag0, *grads_first[1:]))
    with jax.named_scope("cotangent"):
        grads_second = second_step(grads_first, turned[1][1])
    with jax.named_scope("pairs0"):
        slots_c.append(gather_slots(turned[0][1], near0, *diag0))
    with jax.named_scope("pairs1"):
        near1 = gather_sides(turned[1][1])
    attn_c.append(attn_forward(after(info_c[0], turned[1][1]), turned[0][0], slots_c[0]))
    heads_c.append(gather_heads(0, grads_second))
    with jax.named_scope("pairs1"):
        near1 = [after(side, attn_c[0][2]) for side in near1]
        diag1 = gather_diagonal(turned[1][1], near1)
        slots_c.append(gather_slots(turned[1][1], near1, *diag1))
    with jax.named_scope("cotangent"):
        grads_third = third_step(grads_first, grads_second)
    attn_c.append(
        attn_forward(
            after(info_c[1], *early_parts(heads_c[0])), turned[1][0], slots_c[1]
        )
    )
    grad_all = joined_rows(rank, grads_third)

    def middle_of(c, *others):
        return middle_rows(
            after(rank, *others), heads_c[c], ins[c][0], w_out_all, ffn_gain, router, routes_c[c]
        )

    def hidden_of(c, *others):
        _, _, _, ffn_in, probs, routed = mids[c]
        return expert_hidden(
            after(info_c[c], *others), ffn_in, grad_all, probs, routed, w_gate, w_up, w_down, c
        )

    def back_of(c, *others):
        _, gate_grads, up_grads, inner = exps[c]
        return expert_back(
            after(info_c[c], *others),
            gate_grads,
            up_grads,
            inner,
            mids[c][4],
            router,
            mids[c][3],
            w_gate,
            w_up,
            tp_count,
        )

    def ffn_exchange(c, pieces):
        with jax.named_scope(f"ffn_grad{c}"):
            return exchange(pieces)

    def middle_grad_of(c, pieces, *others):
        return middle_back(
            after(info_c[c], *others), pieces, mids[c][1], mids[c][2], grad_all, ffn_gain, w_out_all, c
        )

    def mixture_of(c, *others):
        pieces = mixture(
            after(info_c[c], *others), exps[c][0], w_down, backs[c][2], backs[c][3], tp_count
        )
        with jax.named_scope(f"mixture{c}"):
            return exchange(pieces)

    def output_of(c, pieces):
        total = block_of(mids[c][1], tp_rank, feat, 1)
        for piece in pieces:
            total = total + piece[:rows_n].astype(F32)
        return total.astype(BF16).reshape(per, size, feat).transpose(1, 0, 2)

    def attention_back(c, *others):
        return attn_backward(
            after(info_c[c], *others), turned[c][0], sent[c], *attn_c[c][1:], slots_c[c]
        )

    def cores_of(c):
        with jax.named_scope(f"pair_cores{c}"):
            return scatter_cores(dqs[c][2])

    def diagonal_of(c, received):
        if sq_count != 8:
            return None, []
        with jax.named_scope(f"pair_diagonal{c}"):
            diagonal = scatter_diagonal(dqs[c][1], received)
            return diagonal, send_halves(diagonal)

    def sides_of(c, received, diagonal):
        with jax.named_scope(f"pair_sides{c}"):
            return scatter_sides(dqs[c][1], received, diagonal)

    def stats_of(c, received, blocks):
        query_raw, key_raw, squares = ins[c][3:6]
        operands = (
            dqs[c][0],
            scatter_total(dqs[c][1], received, blocks),
            query_raw,
            key_raw,
            squares,
            query_gain[None, :],
            key_gain[None, :],
            cosine,
            sine,
        )
        stats, gain_qk = back_stats(operands, all_cols)
        with jax.named_scope(f"stats{c}"):
            stats = sum(exchange([stats] * tp_count))
        return operands, stats, gain_qk

    def first_of(c, operands, stats, *others):
        low, _, inv = ins[c][:3]
        raw, pieces, part = back_first(
            after(info_c[c], *others),
            operands,
            stats,
            low,
            inv,
            attn_gain,
            w_query,
            w_key,
            w_value,
            all_cols,
            tp_count,
        )
        with jax.named_scope(f"first{c}"):
            pieces = exchange(pieces)
        return raw, pieces, part

    scatter = lambda g: lax.psum_scatter(g, "sq", scatter_dimension=0, tiled=True)

    backs, dqs = [], []
    mids.append(middle_of(0, attn_c[1][2], *grads_second))
    exps.append(hidden_of(0))
    heads_c.append(gather_heads(1, (), (mids[0][3],), (exps[0][3],)))
    back0, router0 = back_of(0)
    sent0 = ffn_exchange(0, back0)
    mids.append(middle_of(1, back0[0]))
    exps.append(hidden_of(1))
    ffn_list = [m[3] for m in mids]
    w_down_part = weight_grad([grad_all], [e[0] for e in exps])
    backs.append(middle_grad_of(0, sent0, w_down_part))
    sent = [mixture_of(0, backs[0][1])]
    back1, router1 = back_of(1, sent[0][0])
    sent1 = ffn_exchange(1, back1)
    w_up_part = weight_grad(ffn_list, [exps[0][2], after(exps[1][2], back1[0])])
    dqs.append(attention_back(0, w_up_part))
    backs.append(middle_grad_of(1, sent1, dqs[0][0]))
    sent.append(mixture_of(1, backs[1][1]))
    w_gate_part = weight_grad(ffn_list, [exps[0][1], after(exps[1][1], sent[1][0])])
    cores0 = cores_of(0)
    summed0, diagonal0 = diagonal_of(0, cores0)
    sums0, sides0 = sides_of(0, cores0, diagonal0)
    attn_own = [block_of(m[0], tp_rank, quarter, 0) for m in mids]
    w_out_part = weight_grad([backs[0][1], after(backs[1][1], w_gate_part)], attn_own)
    dqs.append(attention_back(1, w_out_part, *diagonal0, *sums0))
    cores1 = cores_of(1)
    operands0, stats0, gain0 = stats_of(0, after(cores0, dqs[1][0]), sides0)
    summed1, diagonal1 = diagonal_of(1, after(cores1, gain0))
    raw0, first0, part0 = first_of(
        0, operands0, stats0, *([cores1] if summed1 is None else [summed1])
    )
    sums1, sides1 = sides_of(1, cores1, diagonal1)

    outputs = [output_of(c, sent[c]) for c in range(2)]
    operands1, stats1, gain1 = stats_of(1, cores1, sides1)
    raw1, first1, part1 = first_of(1, operands1, stats1, *first0[1:])
    w_down_rows = scatter(after(w_down_part, backs[0][1]))
    w_up_rows = scatter(after(w_up_part, backs[1][1], w_down_rows))
    w_out_rows = scatter(after(w_out_part, w_up_rows, raw0))
    w_gate_rows = scatter(after(w_gate_part, w_out_rows, raw1))
    w_down_grad = spread(w_down_rows, experts, True)
    w_up_grad = spread(w_up_rows, experts, False)
    w_gate_grad = spread(w_gate_rows, experts, False)
    with jax.named_scope("weights"):
        own = reduce_cores(info_c[0], [([(i[1], 0) for i in ins], [raw0, raw1])])
        qkv_grad, came = reduce_chips(own)
    with jax.named_scope("out_weight"):
        out_pieces = exchange(
            [block_of(w_out_rows, (tp_rank + k) % tp_count, head_cols, 1) for k in range(tp_count)]
        )
        w_out_grad = sum(p.astype(F32) for p in out_pieces).T
    finals = [
        finish(
            after(info_c[c], own),
            sent[c],
            pieces,
            inputs_c[c],
            ins[c][2],
            attn_gain,
            per,
        )
        for c, pieces in enumerate((first0, first1))
    ]
    small = jnp.concatenate(
        [
            router0 + router1,
            (backs[0][0] + backs[1][0])[None, :],
            (part0 + after(part1, finals[1]))[None, :],
            lax.dynamic_update_slice_in_dim(
                jnp.zeros((2, all_cols), F32), gain0 + gain1, tp_rank * head_cols, 1
            ),
        ],
        axis=0,
    )
    with jax.named_scope("small"):
        small = butterfly(butterfly(small, "sq"), "tp")
    early, late = small[: experts_total + 1], small[experts_total + 1 :]
    return (
        jnp.concatenate(outputs, axis=1),
        jnp.concatenate(finals, axis=0).reshape(seqs, size, feat).transpose(1, 0, 2),
        late[0],
        qkv_grad[:, :head_cols],
        qkv_grad[:, head_cols : 2 * head_cols],
        qkv_grad[:, 2 * head_cols : 3 * head_cols],
        late[1],
        late[2],
        w_out_grad,
        early[experts_total],
        early[:experts_total].T,
        w_gate_grad,
        w_up_grad,
        w_down_grad,
    )


def solution(mesh):
    placed = (
        P("sq", None, "tp"),
        P(),
        P("sq", None, None),
        P(),
        P(None, "tp"),
        P(None, "tp"),
        P(None, "tp"),
        P("tp"),
        P("tp"),
        P("tp", None),
        P(),
        P(),
        P("tp", None, None),
        P("tp", None, None),
        P("tp", None, None),
        P("sq", None, "tp"),
    )
    return jax.shard_map(
        shards,
        mesh=mesh,
        in_specs=placed,
        out_specs=(
            P("sq", None, "tp"),
            P("sq", None, "tp"),
            P(),
            P("sq", "tp"),
            P("sq", "tp"),
            P("sq", "tp"),
            P(),
            P(),
            P("tp", "sq"),
            P(),
            P(),
            P("tp", "sq", None),
            P("tp", "sq", None),
            P("tp", None, "sq"),
        ),
        check_vma=False,
    )
```

```python
import functools

import jax
import jax.numpy as jnp
from jax import lax
from jax.experimental import pallas as pl
from jax.experimental.pallas import tpu as pltpu
from jax.sharding import PartitionSpec as P

HD = 128
EPSILON = 1e-05
ROTARY_BASE = 10000.0
NEGATIVE = -1e30
F32 = jnp.float32
BF16 = jnp.bfloat16
VMEM_LIMIT = 56 * 1024 * 1024
CHUNKS = 2
NT = (((1,), (1,)), ((), ()))
TN = (((0,), (0,)), ((), ()))
NN = (((1,), (0,)), ((), ()))


def dot(left, right, dims=NN):
    return lax.dot_general(left, right, dims, preferred_element_type=F32)


def after(value, *others):
    return lax.optimization_barrier((value, *others))[0]


def shift(block, axis, distance):
    count = lax.axis_size(axis)
    return lax.ppermute(block, axis, [(i, (i + distance) % count) for i in range(count)])


def swap(block, axis, mask):
    return lax.ppermute(block, axis, [(i, i ^ mask) for i in range(lax.axis_size(axis))])


OUTER, INNER = [(0, 1), (1, 0), (2, 3), (3, 2)], [(0, 0), (1, 2), (2, 1), (3, 3)]


def first_step(block):
    count = lax.axis_size("tp")
    if count == 4:
        return [block, lax.ppermute(block, "tp", OUTER), lax.ppermute(block, "tp", INNER)]
    return [block] + [shift(block, "tp", k) for k in range(1, count)]


def second_step(first, *others):
    if lax.axis_size("tp") != 4:
        return []
    _, a1, b1 = first
    return [
        lax.ppermute(after(b1, a1, *others), "tp", OUTER),
        lax.ppermute(after(a1, b1, *others), "tp", INNER),
    ]


def third_step(first, second, *others):
    count = lax.axis_size("tp")
    if count != 4:
        return first, by_distance(count)
    (block, a1, b1), (a2, b2) = first, second
    a3 = lax.ppermute(after(b2, a2, *others), "tp", OUTER)
    return [block, a1, a2, a3, b1, b2], ((0, 1, 2, 3), (1, 0, 4, 5), (5, 4, 0, 1), (3, 2, 1, 0))


def gather_tp(block, second=(), third=()):
    first = first_step(block)
    return third_step(first, second_step(first, *second), *third)


def by_distance(count):
    return tuple(tuple((z - f) % count for f in range(count)) for z in range(count))


def exchange(pieces):
    return [p if k == 0 else shift(p, "tp", k) for k, p in enumerate(pieces)]


def butterfly(value, axis):
    return butterfly_steps(value, axis)[0]


def butterfly_steps(value, axis):
    mask, received = 1, None
    while mask < lax.axis_size(axis):
        received = swap(value, axis, mask)
        value = value + received
        mask *= 2
    return value, received


def block_of(array, index, size, axis):
    return lax.dynamic_slice_in_dim(array, index * size, size, axis)


def gather_sides(pair):
    if lax.axis_size("sq") == 8:
        return swap(pair, "sq", 2), swap(pair, "sq", 4)
    return [swap(pair, "sq", m) for m in range(2, lax.axis_size("sq"), 2)]


def gather_diagonal(pair, sides):
    trio = swap(jnp.stack([pair, *sides]), "sq", 1)
    if lax.axis_size("sq") == 8:
        near, far = sides
        return trio, swap(far[:1], "sq", 2), swap(near[1:], "sq", 4)
    return (trio,)


def gather_slots(pair, sides, trio, *diagonal):
    slots = []
    for k, side in enumerate([pair, *sides]):
        slots += [side, trio[k]]
    if diagonal:
        slots += [diagonal, swap(jnp.concatenate(diagonal), "sq", 1)]
    return slots


def scatter_cores(odd):
    return swap(odd, "sq", 1)


def scatter_diagonal(even, received):
    return add_blocks([[(even, (3, half)), (received, (3, half))] for half in range(2)])


def send_halves(diagonal):
    return [swap(diagonal[half], "sq", 2 + 2 * half) for half in range(2)]


def scatter_sides(even, received, halves):
    sums = []
    for k in range(1, 3 if halves else even.shape[0]):
        terms = [[(even, (k, half)), (received, (k, half))] for half in range(2)]
        if halves:
            terms[2 - k].append((halves[2 - k], ()))
        sums.append(add_blocks(terms))
    return sums, [swap(array, "sq", 2 * k + 2) for k, array in enumerate(sums)]


def scatter_total(even, received, blocks):
    return add_blocks(
        [
            [(even, (0, half)), (received, (0, half))] + [(block, (half,)) for block in blocks]
            for half in range(2)
        ]
    )


def reduce_cores(info, pairs):
    received = swap(relative_grads(info, 1, pairs, None), "sq", 1)
    own = relative_grads(info, 0, pairs, received)
    return own.reshape(lax.axis_size("sq") // 2, -1, own.shape[1])


def reduce_chips(own):
    half = own.shape[2] // 2
    results, came = [], []
    for part in range(2):
        blocks = own[:, :, part * half : (part + 1) * half]
        steps = [1 << b for b in range(own.shape[0].bit_length() - 1)]
        if part:
            steps = steps[::-1]
        kept = {m: blocks[m] for m in range(own.shape[0])}
        for number, step in enumerate(steps):
            give = sorted(m for m in kept if m & step)
            keep = sorted(m for m in kept if not m & step)
            got = swap(jnp.stack([kept[m] for m in give]), "sq", 2 * step)
            if number == 0:
                came.append(got)
            last = number == len(steps) - 1
            kept = {
                m: (kept[m].astype(F32) + got[i].astype(F32)).astype(F32 if last else BF16)
                for i, m in enumerate(keep)
            }
        results.append(kept[0])
    return jnp.concatenate(results, axis=1).astype(F32), came


COST = 100


def cost(flops, bytes_accessed, transcendentals):
    return pl.CostEstimate(
        flops=flops // COST,
        bytes_accessed=bytes_accessed // COST,
        transcendentals=transcendentals // COST,
    )


def add_kernel(counts, *refs):
    first = 0
    for half, count in enumerate(counts):
        total = None
        for ref in refs[first : first + count]:
            part = ref[(0,) * (len(ref.shape) - 2)].astype(F32)
            total = part if total is None else total + part
        refs[-1][half, 0] = total.astype(BF16)
        first += count


def add_blocks(halves):
    shape = halves[0][0][0].shape[-3:]

    def spec(lead):
        return pl.BlockSpec((1,) * (len(lead) + 1) + shape[1:], lambda s: (*lead, s, 0, 0))

    terms = [term for half in halves for term in half]
    return pl.pallas_call(
        functools.partial(add_kernel, [len(half) for half in halves]),
        grid=(shape[0],),
        in_specs=[spec(lead) for _, lead in terms],
        out_specs=pl.BlockSpec((2, 1) + shape[1:], lambda s: (0, s, 0, 0)),
        out_shape=jax.ShapeDtypeStruct((2, *shape), BF16),
        compiler_params=params(),
        name="add_blocks",
    )(*[array for array, _ in terms])


def params():
    return pltpu.CompilerParams(vmem_limit_bytes=VMEM_LIMIT)


def place_columns(rank, table, sources, out_ref):
    width = sources[0].shape[-1]
    for z in range(len(table)):

        @pl.when(rank == z)
        def _(z=z):
            for f, index in enumerate(table[z]):
                out_ref[:, f * width : (f + 1) * width] = sources[index][...]


def row_sums(values):
    cols = values.shape[1]
    total = values[:, :HD]
    for k in range(1, cols // HD):
        total = total + values[:, k * HD : (k + 1) * HD]
    return jnp.sum(total.T, axis=0, keepdims=True)


def as_columns(row):
    return jnp.broadcast_to(row, (HD, row.shape[1])).T


def front_kernel(table, count, info, *refs):
    sources, refs = refs[:count], refs[count:]
    gain_ref, wq_ref, wk_ref, wv_ref = refs[:4]
    low_ref, normed_ref, inv_ref, query_ref, key_ref, value_ref, square_ref = refs[4:]
    place_columns(info[0], table, sources, low_ref)
    rows = low_ref[...].astype(F32)
    inv = lax.rsqrt(jnp.mean(rows * rows, axis=1, keepdims=True) + EPSILON)
    inv_ref[...] = inv
    normed = (rows * inv * gain_ref[...]).astype(BF16)
    normed_ref[...] = normed
    query, key = dot(normed, wq_ref[...]), dot(normed, wk_ref[...])
    query_ref[...] = query
    key_ref[...] = key
    value_ref[...] = dot(normed, wv_ref[...]).astype(BF16)
    square_ref[0:1, :] = row_sums(query * query)
    square_ref[1:2, :] = row_sums(key * key)


def front(rank, gathered, gain, w_query, w_key, w_value):
    sources, table = gathered
    rows, width = sources[0].shape
    total = width * len(table)
    cols = w_query.shape[1]
    tile = min(256, rows)
    spec = lambda cols: pl.BlockSpec((tile, cols), lambda i, info: (i, 0))
    whole = lambda array: pl.BlockSpec(
        array.shape, lambda i, info: (0, 0), pipeline_mode=pl.Buffered(1)
    )
    out = lambda cols, dtype: jax.ShapeDtypeStruct((rows, cols), dtype)
    return pl.pallas_call(
        functools.partial(front_kernel, table, len(sources)),
        grid_spec=pltpu.PrefetchScalarGridSpec(
            num_scalar_prefetch=1,
            grid=(rows // tile,),
            in_specs=[spec(width)] * len(sources)
            + [pl.BlockSpec((1, total), lambda i, info: (0, 0))]
            + [whole(w_query), whole(w_key), whole(w_value)],
            out_specs=[spec(total), spec(total), spec(1), spec(cols), spec(cols), spec(cols)]
            + [pl.BlockSpec((2, tile), lambda i, info: (0, i))],
        ),
        out_shape=[
            out(total, BF16),
            out(total, BF16),
            out(1, F32),
            out(cols, F32),
            out(cols, F32),
            out(cols, BF16),
            jax.ShapeDtypeStruct((2, rows), F32),
        ],
        compiler_params=params(),
        cost_estimate=cost(
            flops=6 * rows * total * cols,
            bytes_accessed=6 * total * cols + 8 * rows * total,
            transcendentals=0,
        ),
        name="front",
    )(rank, *sources, gain[None, :], w_query, w_key, w_value)


def halves(count):
    lane = lax.broadcasted_iota(jnp.int32, (1, HD), 1)
    return jnp.where(lane < HD // 2, 1.0, -1.0)


def rotate_kernel(
    all_cols, q_ref, k_ref, v_ref, square_ref, qg_ref, kg_ref, cos_ref, sin_ref, out_ref, pair_ref
):
    inv = lax.rsqrt(square_ref[...] / all_cols + EPSILON)
    cosine, sine = cos_ref[...], -halves(HD) * sin_ref[...]
    for number, (raw_ref, gain_ref) in enumerate(((q_ref, qg_ref), (k_ref, kg_ref))):
        scale = as_columns(inv[number : number + 1, :])
        for h in range(raw_ref.shape[1] // HD):
            span = slice(h * HD, (h + 1) * HD)
            normed = raw_ref[:, span] * scale * gain_ref[:, span]
            turned = (normed * cosine + pltpu.roll(normed, HD // 2, 1) * sine).astype(BF16)
            if number == 0:
                out_ref[0, :, span] = turned
            else:
                pair_ref[0, 0, :, span] = turned
    pair_ref[1, 0] = v_ref[...]


def rotate(query, key, value, squares, query_gain, key_gain, cosine, sine, all_cols):
    rows, cols = query.shape
    size = cosine.shape[0]
    spec = pl.BlockSpec((size, cols), lambda s: (s, 0))
    one = pl.BlockSpec((1, cols), lambda s: (0, 0))
    turn = pl.BlockSpec((size, HD), lambda s: (0, 0))
    return pl.pallas_call(
        functools.partial(rotate_kernel, all_cols),
        grid=(rows // size,),
        in_specs=[spec, spec, spec, pl.BlockSpec((2, size), lambda s: (0, s))]
        + [one, one, turn, turn],
        out_specs=[
            pl.BlockSpec((1, size, cols), lambda s: (s, 0, 0)),
            pl.BlockSpec((2, 1, size, cols), lambda s: (0, s, 0, 0)),
        ],
        out_shape=[
            jax.ShapeDtypeStruct((rows // size, size, cols), BF16),
            jax.ShapeDtypeStruct((2, rows // size, size, cols), BF16),
        ],
        compiler_params=params(),
        name="rotate",
    )(query, key, value, squares, query_gain[None, :], key_gain[None, :], cosine, sine)


def back_parts(all_cols, refs):
    dq_ref, dkv_ref, q_ref, k_ref, square_ref, qg_ref, kg_ref, cos_ref, sin_ref = refs
    inv = lax.rsqrt(square_ref[...] / all_cols + EPSILON)
    cosine, sine = cos_ref[...], sin_ref[...]
    sign = halves(HD)
    for number, (raw_ref, gain_ref) in enumerate(((q_ref, qg_ref), (k_ref, kg_ref))):
        scale = as_columns(inv[number : number + 1, :])
        for h in range(raw_ref.shape[1] // HD):
            span = slice(h * HD, (h + 1) * HD)
            grad = (dkv_ref[0, 0, :, span] if number else dq_ref[0, :, span]).astype(F32)
            back = grad * cosine + pltpu.roll(grad * sine, HD // 2, 1) * sign
            yield number, span, back, raw_ref[:, span] * scale, scale, gain_ref[:, span]


def back_stats_kernel(all_cols, *refs):
    stat_ref, gain_ref = refs[9:]

    @pl.when(pl.program_id(0) == 0)
    def _():
        gain_ref[...] = jnp.zeros(gain_ref.shape, F32)

    totals = [None, None]
    for number, span, back, hat, _, gain in back_parts(all_cols, refs[:9]):
        product = back * hat
        gain_ref[number : number + 1, span] += jnp.sum(product, axis=0, keepdims=True)
        product = product * gain
        totals[number] = product if totals[number] is None else totals[number] + product
    for number in range(2):
        stat_ref[number : number + 1, :] = row_sums(totals[number])


def back_specs(size, cols):
    spec = pl.BlockSpec((size, cols), lambda s: (s, 0))
    one = pl.BlockSpec((1, cols), lambda s: (0, 0))
    turn = pl.BlockSpec((size, HD), lambda s: (0, 0))
    row = pl.BlockSpec((2, size), lambda s: (0, s))
    return [
        pl.BlockSpec((1, size, cols), lambda s: (s, 0, 0)),
        pl.BlockSpec((2, 1, size, cols), lambda s: (0, s, 0, 0)),
        spec,
        spec,
        row,
        one,
        one,
        turn,
        turn,
    ]


def back_stats(operands, all_cols):
    rows, cols = operands[2].shape
    size = operands[0].shape[1]
    return pl.pallas_call(
        functools.partial(back_stats_kernel, all_cols),
        grid=(rows // size,),
        in_specs=back_specs(size, cols),
        out_specs=[
            pl.BlockSpec((2, size), lambda s: (0, s)),
            pl.BlockSpec((2, cols), lambda s: (0, 0)),
        ],
        out_shape=[
            jax.ShapeDtypeStruct((2, rows), F32),
            jax.ShapeDtypeStruct((2, cols), F32),
        ],
        compiler_params=params(),
        name="back_stats",
    )(*operands)


def back_first_kernel(all_cols, count, info, *refs):
    stat_ref, low_ref, inv_ref, gain_ref, wq_ref, wk_ref, wv_ref = refs[9:16]
    raw_ref, part_ref = refs[16:18]
    first_refs, buffer = refs[18 : 18 + count], refs[18 + count]
    size = buffer.shape[0]
    rows = pl.ds(pl.multiple_of(pl.program_id(0) * size, size), size)
    cols = wq_ref.shape[1]
    stats = stat_ref[...] / all_cols
    for number, span, back, hat, scale, gain in back_parts(all_cols, refs[:9]):
        mean = as_columns(stats[number : number + 1, :])
        raw = scale * (back * gain - hat * mean)
        raw_ref[:, number * cols + span.start : number * cols + span.stop] = raw.astype(BF16)
    raw_ref[:, 2 * cols :] = refs[1][1, 0]
    first = (
        dot(raw_ref[:, :cols], wq_ref[...], NT)
        + dot(raw_ref[:, cols : 2 * cols], wk_ref[...], NT)
        + dot(raw_ref[:, 2 * cols :], wv_ref[...], NT)
    )
    buffer[...] = first.astype(BF16)
    feat = first_refs[0].shape[1]
    for k in range(count):
        target = lax.rem(info[1] + k, count)
        span = pl.ds(pl.multiple_of(target * feat, feat), feat)
        first_refs[k][rows, :] = buffer[:, span]

    @pl.when(pl.program_id(0) == 0)
    def _():
        part_ref[...] = jnp.zeros(part_ref.shape, F32)

    product = first * (low_ref[...].astype(F32) * inv_ref[...])
    part_ref[...] += jnp.sum(product, axis=0, keepdims=True)
    rest = row_sums(product * gain_ref[...])
    line = lax.broadcasted_iota(jnp.int32, (EXTRA, size), 0)
    terms = jnp.zeros((EXTRA, size), F32)
    for term in range(2):
        part = rest.astype(BF16).astype(F32)
        rest = rest - part
        terms = jnp.where(line == 2 * pl.program_id(0) + term, part, terms)
    for ref in first_refs:
        place = ref.shape[0] - EXTRA

        @pl.when(pl.program_id(0) == 0)
        def _(ref=ref, place=place):
            ref[place:, :] = jnp.zeros((EXTRA, feat), BF16)

        ref[place:, :size] += terms.astype(BF16)


EXTRA = 16


def back_first(info, operands, stats, low, inv, gain, w_query, w_key, w_value, all_cols, count):
    rows, cols = operands[2].shape
    size = operands[0].shape[1]
    total = low.shape[1]
    lift = lambda spec: pl.BlockSpec(spec.block_shape, lambda s, info: spec.index_map(s))
    spec = lambda cols: pl.BlockSpec((size, cols), lambda s, info: (s, 0))
    row = lambda count: pl.BlockSpec((count, size), lambda s, info: (0, s))
    whole = lambda array: pl.BlockSpec(
        array.shape, lambda s, info: (0, 0), pipeline_mode=pl.Buffered(1)
    )
    one = pl.BlockSpec((1, total), lambda s, info: (0, 0))
    height = rows + EXTRA
    raw, part, *pieces = pl.pallas_call(
        functools.partial(back_first_kernel, all_cols, count),
        grid_spec=pltpu.PrefetchScalarGridSpec(
            num_scalar_prefetch=1,
            grid=(rows // size,),
            in_specs=[lift(s) for s in back_specs(size, cols)]
            + [row(2), spec(total), spec(1), one]
            + [whole(w_query), whole(w_key), whole(w_value)],
            out_specs=[spec(3 * cols), one]
            + [pl.BlockSpec((height, total // count), lambda s, info: (0, 0))] * count,
            scratch_shapes=[pltpu.VMEM((size, total), BF16)],
        ),
        out_shape=[
            jax.ShapeDtypeStruct((rows, 3 * cols), BF16),
            jax.ShapeDtypeStruct((1, total), F32),
        ]
        + [jax.ShapeDtypeStruct((height, total // count), BF16)] * count,
        compiler_params=params(),
        cost_estimate=cost(
            flops=6 * rows * total * cols,
            bytes_accessed=6 * total * cols + 8 * rows * total,
            transcendentals=0,
        ),
        name="back_first",
    )(info, *operands, stats, low, inv, gain[None, :], w_query, w_key, w_value)
    return raw, pieces, part[0]


def joined_kernel(table, count, info, *refs):
    place_columns(info[0], table, refs[:count], refs[count])


def joined_rows(rank, gathered):
    sources, table = gathered
    rows, width = sources[0].shape
    total = width * len(table)
    tile = min(256, rows)
    spec = lambda cols: pl.BlockSpec((tile, cols), lambda i, info: (i, 0))
    return pl.pallas_call(
        functools.partial(joined_kernel, table, len(sources)),
        grid_spec=pltpu.PrefetchScalarGridSpec(
            num_scalar_prefetch=1,
            grid=(rows // tile,),
            in_specs=[spec(width)] * len(sources),
            out_specs=spec(total),
        ),
        out_shape=jax.ShapeDtypeStruct((rows, total), BF16),
        compiler_params=params(),
        name="joined_rows",
    )(rank, *sources)


def relative_grads_kernel(counts, info, *refs):
    more = refs[2 * sum(counts) : -1]
    first, start = 0, 0
    for count in counts:
        lefts, rights = refs[first : first + count], refs[first + count : first + 2 * count]
        first += 2 * count
        total = dot(lefts[0][...], rights[0][...], TN)
        for left, right in zip(lefts[1:], rights[1:]):
            total += dot(left[...], right[...], TN)
        span = slice(start, start + total.shape[1])
        start = span.stop
        for ref in more:
            total += ref[:, span].astype(F32)
        refs[-1][:, span] = total.astype(BF16)


def relative_grads(info, parity, pairs, more):
    blocks = lax.axis_size("sq")
    height = pairs[0][0][0][0].shape[1] // blocks
    specs, operands, width = [], [], 0
    for lefts, rights in pairs:
        width += rights[0].shape[1]
        for (_, chunk), right in zip(lefts, rights):
            specs.append(
                pl.BlockSpec(
                    (right.shape[0], height),
                    lambda m, info, chunk=chunk: (
                        chunk,
                        jnp.bitwise_xor(info[0], 2 * m + parity),
                    ),
                )
            )
        specs += [
            pl.BlockSpec(right.shape, lambda m, info: (0, 0), pipeline_mode=pl.Buffered(1))
            for right in rights
        ]
        operands += [left for left, _ in lefts] + list(rights)
    out = pl.BlockSpec((height, width), lambda m, info: (m, 0))
    if more is not None:
        specs.append(out)
        operands.append(more)
    return pl.pallas_call(
        functools.partial(relative_grads_kernel, [len(lefts) for lefts, _ in pairs]),
        grid_spec=pltpu.PrefetchScalarGridSpec(
            num_scalar_prefetch=1, grid=(blocks // 2,), in_specs=specs, out_specs=out
        ),
        out_shape=jax.ShapeDtypeStruct((height * blocks // 2, width), BF16),
        compiler_params=params(),
        name="relative_grads",
    )(info, *operands)


def middle_kernel(table, count, info, *refs):
    sources = refs[:count]
    low_ref, w_ref, gain_ref, router_ref, routes_ref = refs[count : count + 5]
    attn_ref, middle_ref, inv_ref, ffn_ref, prob_ref, routed_ref = refs[count + 5 :]
    place_columns(info[0], table, sources, attn_ref)
    middle = low_ref[...].astype(F32) + dot(attn_ref[...], w_ref[...])
    middle_ref[...] = middle
    inv = lax.rsqrt(jnp.mean(middle * middle, axis=1, keepdims=True) + EPSILON)
    inv_ref[...] = inv
    ffn_in = (middle * inv * gain_ref[...]).astype(BF16)
    ffn_ref[...] = ffn_in
    logits = dot(ffn_in, router_ref[...])
    powers = jnp.exp(logits - jnp.max(logits, axis=1, keepdims=True))
    prob_ref[...] = powers / jnp.sum(powers, axis=1, keepdims=True)
    routes = routes_ref[...]
    ids = lax.broadcasted_iota(jnp.int32, logits.shape, 1)
    routed = jnp.zeros(logits.shape, F32)
    for r in range(routes.shape[1]):
        routed = jnp.where(routes[:, r : r + 1] == ids, 1.0, routed)
    routed_ref[...] = routed


def middle_rows(rank, gathered, low, w_out, gain, router, routes):
    sources, table = gathered
    rows, width = sources[0].shape
    total = low.shape[1]
    experts = router.shape[1]
    tile = min(256, rows)
    spec = lambda cols: pl.BlockSpec((tile, cols), lambda i, info: (i, 0))
    whole = lambda array: pl.BlockSpec(
        array.shape, lambda i, info: (0, 0), pipeline_mode=pl.Buffered(1)
    )
    out = lambda cols, dtype: jax.ShapeDtypeStruct((rows, cols), dtype)
    return pl.pallas_call(
        functools.partial(middle_kernel, table, len(sources)),
        grid_spec=pltpu.PrefetchScalarGridSpec(
            num_scalar_prefetch=1,
            grid=(rows // tile,),
            in_specs=[spec(width)] * len(sources)
            + [spec(total), whole(w_out), pl.BlockSpec((1, total), lambda i, info: (0, 0))]
            + [whole(router), spec(routes.shape[1])],
            out_specs=[
                spec(width * len(table)),
                spec(total),
                spec(1),
                spec(total),
                spec(experts),
                spec(experts),
            ],
        ),
        out_shape=[
            out(width * len(table), BF16),
            out(total, F32),
            out(1, F32),
            out(total, BF16),
            out(experts, F32),
            out(experts, F32),
        ],
        compiler_params=params(),
        cost_estimate=cost(
            flops=2 * rows * total * total,
            bytes_accessed=2 * total * total + 12 * rows * total,
            transcendentals=0,
        ),
        name="middle_rows",
    )(rank, *sources, low, w_out, gain[None, :], router, routes)


def weight_grad_kernel(count, parts, *refs):
    height = refs[count].shape[0]
    left = lambda i: refs[i][...] if parts == 1 else refs[0][i * height : (i + 1) * height, :]
    total = dot(left(0), refs[count][...], TN)
    for i in range(1, len(refs) - 1 - count):
        total += dot(left(i), refs[count + i][...], TN)
    refs[-1][...] = total.astype(BF16)


def weight_grad(lefts, rights):
    rows, height = rights[0].shape[0], lefts[0].shape[1]
    width = rights[0].shape[1]
    parts = lefts[0].shape[0] // rows
    tall = min(2048, height)
    cols = min(512, width)
    return pl.pallas_call(
        functools.partial(weight_grad_kernel, len(lefts), parts),
        grid=(width // cols, height // tall),
        in_specs=[pl.BlockSpec((rows * parts, tall), lambda j, i: (0, i))] * len(lefts)
        + [pl.BlockSpec((rows, cols), lambda j, i: (0, j))] * len(rights),
        out_specs=pl.BlockSpec((tall, cols), lambda j, i: (i, j)),
        out_shape=jax.ShapeDtypeStruct((height, width), BF16),
        compiler_params=params(),
        cost_estimate=cost(
            flops=2 * rows * len(rights) * height * width,
            bytes_accessed=2 * (rows * len(rights) * (height + width) + height * width),
            transcendentals=0,
        ),
        name="weight_grad",
    )(*lefts, *rights)


def slot_operands(kv_slots):
    arrays, places = [], []
    for slot in kv_slots:
        if isinstance(slot, tuple):
            places.append(((len(arrays), 0), (len(arrays) + 1, 0)))
            arrays += list(slot)
        else:
            places.append(((len(arrays), 0), (len(arrays), 1)))
            arrays.append(slot)
    size = arrays[0].shape[2]
    specs = [
        pl.BlockSpec((a.shape[0], 1, size, HD), lambda s, h, info: (0, s, 0, h)) for a in arrays
    ]
    return arrays, specs, places


def attn_forward_kernel(places, count, info, q_ref, *refs):
    kv_refs, (low_ref, full_ref, lse_ref, top, total, accum) = refs[:count], refs[count:]
    rank = info[0]
    length = info[2 + pl.program_id(0)]
    queries = q_ref[0]
    size = queries.shape[0]
    top[...] = jnp.full(top.shape, NEGATIVE, F32)
    total[...] = jnp.zeros(total.shape, F32)
    accum[...] = jnp.zeros(accum.shape, F32)
    key_row = lax.broadcasted_iota(jnp.int32, (size, size), 0)
    query_col = lax.broadcasted_iota(jnp.int32, (size, size), 1)
    for slot, ((ka, ki), (va, vi)) in enumerate(places):
        block = rank ^ slot
        start = block * size

        @pl.when((block <= rank) & (start < length))
        def _(slot=slot, start=start, ka=ka, ki=ki, va=va, vi=vi):
            scores = dot(kv_refs[ka][ki, 0], queries, NT) * HD**-0.5
            allowed = key_row + start < length
            if slot == 0:
                allowed = allowed & (key_row <= query_col)
            scores = jnp.where(allowed, scores, NEGATIVE)
            newest = jnp.maximum(top[...], jnp.max(scores, axis=0, keepdims=True))
            weights = jnp.exp(scores - newest)
            factor = jnp.exp(top[...] - newest)
            top[...] = newest
            total[...] = total[...] * factor + jnp.sum(weights, axis=0, keepdims=True)
            accum[...] = accum[...] * factor + dot(kv_refs[va][vi, 0], weights.astype(BF16), TN)

    result = (accum[...] / total[...]).T
    full_ref[0] = result
    low_ref[0] = result.astype(BF16)
    lse_ref[0, 0] = top[...] + jnp.log(total[...])


def attn_forward(info, queries, kv_slots):
    seqs, size, columns = queries.shape
    heads = columns // HD
    slots = len(kv_slots)
    arrays, specs, places = slot_operands(kv_slots)
    row_spec = pl.BlockSpec((1, size, HD), lambda s, h, info: (s, 0, h))
    lse_spec = pl.BlockSpec((1, 1, 1, size), lambda s, h, info: (s, h, 0, 0))
    return pl.pallas_call(
        functools.partial(attn_forward_kernel, places, len(arrays)),
        grid_spec=pltpu.PrefetchScalarGridSpec(
            num_scalar_prefetch=1,
            grid=(seqs, heads),
            in_specs=[row_spec] + specs,
            out_specs=[row_spec, row_spec, lse_spec],
            scratch_shapes=[
                pltpu.VMEM((1, size), F32),
                pltpu.VMEM((1, size), F32),
                pltpu.VMEM((HD, size), F32),
            ],
        ),
        out_shape=[
            jax.ShapeDtypeStruct(queries.shape, BF16),
            jax.ShapeDtypeStruct(queries.shape, F32),
            jax.ShapeDtypeStruct((seqs, heads, 1, size), F32),
        ],
        compiler_params=params(),
        cost_estimate=cost(
            flops=8 * seqs * heads * slots * size * size * HD,
            bytes_accessed=4 * seqs * size * columns * (slots + 2),
            transcendentals=seqs * heads * slots * size * size,
        ),
        name="attn_forward",
    )(info, queries, *arrays)


def attn_backward_kernel(places, count, tp_count, info, q_ref, full_ref, lse_ref, *refs):
    grad_refs, refs = refs[:tp_count], refs[tp_count:]
    kv_refs, (dq_ref, even_ref, odd_ref, accum, grad_buf) = refs[:count], refs[count:]
    rank = info[0]
    length = info[2 + pl.program_id(0)]
    queries = q_ref[0]
    size = queries.shape[0]
    piece = size * pl.num_programs(0) // tp_count
    for i in range(size // piece):
        sender = pl.program_id(0) * (size // piece) + i
        distance = lax.rem(info[1] - sender + tp_count, tp_count)
        for k in range(tp_count):

            @pl.when(distance == k)
            def _(i=i, k=k):
                grad_buf[i * piece : (i + 1) * piece, :] = grad_refs[k][...]

    grads = grad_buf[...]
    lse = lse_ref[0, 0]
    delta = jnp.sum((grads.astype(F32) * full_ref[0]).T, axis=0, keepdims=True)
    accum[...] = jnp.zeros(accum.shape, F32)
    key_row = lax.broadcasted_iota(jnp.int32, (size, size), 0)
    query_col = lax.broadcasted_iota(jnp.int32, (size, size), 1)
    for slot, ((ka, ki), (va, vi)) in enumerate(places):
        block = rank ^ slot
        start = block * size
        out_ref = odd_ref if slot % 2 else even_ref
        live = (block <= rank) & (start < length)

        @pl.when(live)
        def _(slot=slot, start=start, out_ref=out_ref, ka=ka, ki=ki, va=va, vi=vi):
            keys, values = kv_refs[ka][ki, 0], kv_refs[va][vi, 0]
            scores = dot(keys, queries, NT) * HD**-0.5
            allowed = key_row + start < length
            if slot == 0:
                allowed = allowed & (key_row <= query_col)
            weights = jnp.where(allowed, jnp.exp(scores - lse), 0.0)
            back = dot(values, grads, NT)
            score_grad = (weights * (back - delta)).astype(BF16)
            out_ref[slot // 2, 1, 0] = dot(weights.astype(BF16), grads).astype(BF16)
            out_ref[slot // 2, 0, 0] = (dot(score_grad, queries) * HD**-0.5).astype(BF16)
            accum[...] += dot(score_grad, keys, TN)

        @pl.when(jnp.logical_not(live))
        def _(slot=slot, out_ref=out_ref):
            out_ref[slot // 2, :, 0] = jnp.zeros((2,) + queries.shape, BF16)

    dq_ref[0] = (accum[...] * HD**-0.5).astype(BF16)


def attn_backward(info, queries, grad_pieces, full, lse, kv_slots):
    seqs, size, columns = queries.shape
    heads = columns // HD
    slots = len(kv_slots)
    arrays, specs, places = slot_operands(kv_slots)
    piece = size * seqs // len(grad_pieces)
    last = grad_pieces[0].shape[0] // piece - 1
    row_spec = pl.BlockSpec((1, size, HD), lambda s, h, info: (s, 0, h))
    piece_spec = pl.BlockSpec((piece, HD), lambda s, h, info: (last, h))
    lse_spec = pl.BlockSpec((1, 1, 1, size), lambda s, h, info: (s, h, 0, 0))
    out_spec = pl.BlockSpec((slots // 2, 2, 1, size, HD), lambda s, h, info: (0, 0, s, 0, h))
    out_shape = jax.ShapeDtypeStruct((slots // 2, 2, seqs, size, columns), BF16)
    return pl.pallas_call(
        functools.partial(attn_backward_kernel, places, len(arrays), len(grad_pieces)),
        grid_spec=pltpu.PrefetchScalarGridSpec(
            num_scalar_prefetch=1,
            grid=(seqs, heads),
            in_specs=[row_spec, row_spec, lse_spec] + [piece_spec] * len(grad_pieces) + specs,
            out_specs=[row_spec, out_spec, out_spec],
            scratch_shapes=[pltpu.VMEM((size, HD), F32), pltpu.VMEM((size, HD), BF16)],
        ),
        out_shape=[jax.ShapeDtypeStruct(queries.shape, BF16), out_shape, out_shape],
        compiler_params=params(),
        cost_estimate=cost(
            flops=20 * seqs * heads * slots * size * size * HD,
            bytes_accessed=8 * seqs * size * columns * (slots + 2),
            transcendentals=seqs * heads * slots * size * size,
        ),
        name="attn_backward",
    )(info, queries, full, lse, *grad_pieces, *arrays)


def expert_hidden_kernel(
    tile,
    info,
    x_ref,
    g_ref,
    prob_ref,
    routed_ref,
    wg_ref,
    wu_ref,
    wd_ref,
    gh_ref,
    gp_ref,
    up_ref,
    gg_ref,
):
    expert, block = pl.program_id(0), pl.program_id(1)
    rows = x_ref.shape[0]

    @pl.when((expert == 0) & (block == 0))
    def _():
        gg_ref[...] = jnp.zeros(gg_ref.shape, F32)

    for i in range(rows // tile):
        span = slice(i * tile, (i + 1) * tile)
        tokens = x_ref[span, :]
        gate_pre = dot(tokens, wg_ref[0])
        up_pre = dot(tokens, wu_ref[0])
        back = dot(g_ref[span, :], wd_ref[0], NT)
        probs = prob_ref[span, :]
        lane = lax.broadcasted_iota(jnp.int32, probs.shape, 1)
        chosen = (lane == info[1] * pl.num_programs(0) + expert) & (routed_ref[span, :] > 0.5)
        gate = jnp.sum(jnp.where(chosen, probs, 0.0), axis=1, keepdims=True)
        sigmoid = 1.0 / (1.0 + jnp.exp(-gate_pre))
        silu = gate_pre * sigmoid
        hidden = silu * up_pre
        inner = jnp.sum(hidden * back, axis=1, keepdims=True)
        gg_ref[span, :] += jnp.where(chosen, inner, 0.0)
        gh_ref[span, :] = (gate * hidden).astype(BF16)
        hidden_grad = gate * back
        gp_ref[span, :] = (
            hidden_grad * up_pre * (sigmoid + silu * (1.0 - sigmoid))
        ).astype(BF16)
        up_ref[span, :] = (hidden_grad * silu).astype(BF16)


def expert_hidden(info, tokens, grads, probs, routed, w_gate, w_up, w_down, chunk):
    rows, width = tokens.shape
    experts, _, units = w_gate.shape
    cols = min(512, units)
    tile = min(512, rows)
    whole = pl.BlockSpec((rows, width), lambda e, f, info: (0, 0), pipeline_mode=pl.Buffered(1))
    part = pl.BlockSpec((rows, width), lambda e, f, info: (chunk, 0), pipeline_mode=pl.Buffered(1))
    small = pl.BlockSpec(probs.shape, lambda e, f, info: (0, 0))
    wide = pl.BlockSpec((1, width, cols), lambda e, f, info: (e, 0, f))
    tall = pl.BlockSpec((1, cols, width), lambda e, f, info: (e, f, 0))
    result = pl.BlockSpec((rows, cols), lambda e, f, info: (0, e * (units // cols) + f))
    out = jax.ShapeDtypeStruct((rows, experts * units), BF16)
    return pl.pallas_call(
        functools.partial(expert_hidden_kernel, tile),
        grid_spec=pltpu.PrefetchScalarGridSpec(
            num_scalar_prefetch=1,
            grid=(experts, units // cols),
            in_specs=[whole, part, small, small, wide, wide, tall],
            out_specs=[result, result, result, small],
        ),
        out_shape=[out, out, out, jax.ShapeDtypeStruct(probs.shape, F32)],
        compiler_params=params(),
        cost_estimate=cost(
            flops=6 * rows * width * experts * units,
            bytes_accessed=6 * width * experts * units + 6 * rows * experts * units,
            transcendentals=rows * experts * units,
        ),
        name="expert_hidden",
    )(info, tokens, grads, probs, routed, w_gate, w_up, w_down)


def expert_back_kernel(
    count, info, gp_ref, up_ref, gg_ref, prob_ref, router_ref, x_ref, wg_ref, wu_ref, *refs
):
    out_refs, lg_ref, rg_ref, accum = refs[:count], refs[count], refs[count + 1], refs[count + 2]
    expert, block = pl.program_id(0), pl.program_id(1)
    cols = wg_ref.shape[1]
    span = pl.ds(pl.multiple_of(block * cols, cols), cols)

    @pl.when((expert == 0) & (block == 0))
    def _():
        probs, inner = prob_ref[...], gg_ref[...]
        lg_ref[...] = probs * (inner - jnp.sum(probs * inner, axis=1, keepdims=True))

    @pl.when(expert == 0)
    def _():
        accum[:, span] = lax.dot_general(
            lg_ref[...],
            router_ref[...].astype(F32),
            NT,
            precision=lax.Precision.HIGHEST,
            preferred_element_type=F32,
        )

    accum[:, span] += dot(gp_ref[...], wg_ref[0], NT) + dot(up_ref[...], wu_ref[0], NT)

    @pl.when(expert == 0)
    def _():
        rest = lg_ref[...]
        total = jnp.zeros((rest.shape[1], cols), F32)
        for _ in range(3):
            part = rest.astype(BF16)
            rest = rest - part.astype(F32)
            total += dot(part, x_ref[...], TN)
        rg_ref[...] = total

    @pl.when(expert == pl.num_programs(0) - 1)
    def _():
        height = out_refs[0].shape[0]
        for k in range(count):
            target = lax.rem(info[1] + k, count)
            rows = pl.ds(pl.multiple_of(target * height, height), height)
            out_refs[k][:, span] = accum[rows, span].astype(BF16)


def expert_back(info, gate_grads, up_grads, inner, probs, router, tokens, w_gate, w_up, count):
    rows = gate_grads.shape[0]
    experts, width, units = w_gate.shape
    total = router.shape[1]
    cols = min(1024, width)
    left = pl.BlockSpec((rows, units), lambda e, d, info: (0, e))
    small = pl.BlockSpec((rows, total), lambda e, d, info: (0, 0))
    weight = pl.BlockSpec((1, cols, units), lambda e, d, info: (e, d, 0))
    piece = pl.BlockSpec((rows // count, width), lambda e, d, info: (0, 0))
    last = width // cols - 1
    *pieces, _, router_grad = pl.pallas_call(
        functools.partial(expert_back_kernel, count),
        grid_spec=pltpu.PrefetchScalarGridSpec(
            num_scalar_prefetch=1,
            grid=(experts, width // cols),
            in_specs=[
                left,
                left,
                small,
                small,
                pl.BlockSpec((cols, total), lambda e, d, info: (d, 0)),
                pl.BlockSpec((rows, cols), lambda e, d, info: (0, jnp.where(e == 0, d, last))),
                weight,
                weight,
            ],
            out_specs=[piece] * count
            + [
                small,
                pl.BlockSpec((total, cols), lambda e, d, info: (0, jnp.where(e == 0, d, last))),
            ],
            scratch_shapes=[pltpu.VMEM((rows, width), F32)],
        ),
        out_shape=[jax.ShapeDtypeStruct((rows // count, width), BF16)] * count
        + [jax.ShapeDtypeStruct((rows, total), F32), jax.ShapeDtypeStruct((total, width), F32)],
        compiler_params=params(),
        cost_estimate=cost(
            flops=4 * rows * width * experts * units,
            bytes_accessed=4 * width * experts * units + 6 * rows * experts * units,
            transcendentals=0,
        ),
        name="expert_back",
    )(info, gate_grads, up_grads, inner, probs, router, tokens, w_gate, w_up)
    return pieces, router_grad


def mixture_kernel(count, info, hidden_ref, w_ref, *refs):
    head_refs, own_refs, out_refs = refs[:count], refs[count : 2 * count], refs[2 * count :]
    rows, height = hidden_ref.shape[0], own_refs[0].shape[0]
    result = dot(hidden_ref[...], w_ref[...]).astype(BF16)
    for k in range(count):

        @pl.when(pl.program_id(0) == k)
        def _(k=k):
            out_refs[k][:rows] = result
            out_refs[k][rows : rows + height] = own_refs[k][...]
            out_refs[k][rows + height :] = head_refs[k][...]


def mixture(info, hidden, w_down, heads, own, count):
    rows, units = hidden.shape
    width = w_down.shape[-1]
    feat = width // count
    height = heads[0].shape[0]
    piece = pl.BlockSpec((rows + 2 * height, feat), lambda k, info: (0, 0))
    row = pl.BlockSpec((height, feat), lambda k, info: (0, 0))
    return pl.pallas_call(
        functools.partial(mixture_kernel, count),
        grid_spec=pltpu.PrefetchScalarGridSpec(
            num_scalar_prefetch=1,
            grid=(count,),
            in_specs=[
                pl.BlockSpec((rows, units), lambda k, info: (0, 0), pipeline_mode=pl.Buffered(1)),
                pl.BlockSpec((units, feat), lambda k, info: (0, lax.rem(info[1] + k, count))),
            ]
            + [row] * (2 * count),
            out_specs=[piece] * count,
        ),
        out_shape=[jax.ShapeDtypeStruct((rows + 2 * height, feat), BF16)] * count,
        compiler_params=params(),
        cost_estimate=cost(
            flops=2 * rows * units * width,
            bytes_accessed=2 * (rows * units + units * width + rows * width),
            transcendentals=0,
        ),
        name="mixture",
    )(info, hidden, w_down.reshape(units, width), *heads, *own)


def middle_back_kernel(count, info, *refs):
    piece_refs, refs = refs[:count], refs[count:]
    middle_ref, inv_ref, grad_ref, gain_ref, w_ref = refs[:5]
    part_ref, low_ref, out_refs, own_refs = refs[5], refs[6], refs[7 : 7 + count], refs[7 + count :]
    ffn_grad = piece_refs[0][...].astype(F32)
    for k in range(1, count):
        ffn_grad = ffn_grad + piece_refs[k][...].astype(F32)
    inv = inv_ref[...]
    hat = middle_ref[...] * inv
    part_ref[...] = jnp.sum(ffn_grad * hat, axis=0, keepdims=True)
    gained = ffn_grad * gain_ref[...]
    mean = jnp.mean(gained * hat, axis=1, keepdims=True)
    low = (grad_ref[...].astype(F32) + inv * (gained - hat * mean)).astype(BF16)
    low_ref[...] = low
    cols, feat = out_refs[0].shape[1], own_refs[0].shape[1]
    for k in range(count):
        target = lax.rem(info[1] + k, count)
        own_refs[k][...] = low_ref[:, pl.ds(pl.multiple_of(target * feat, feat), feat)]
        rows = pl.ds(pl.multiple_of(target * cols, cols), cols)
        out_refs[k][...] = dot(low, w_ref[rows, :], NT).astype(BF16)


def middle_back(info, pieces, middle, inv, grads, gain, w_out, chunk):
    count = len(pieces)
    height, width = pieces[0].shape
    cols = w_out.shape[0] // count
    whole = lambda array: pl.BlockSpec(array.shape, lambda i, info: (0, 0))
    own = lambda cols: pl.BlockSpec((height, cols), lambda i, info: (info[1], 0))
    part = pl.BlockSpec((height, width), lambda i, info: (chunk * count + info[1], 0))
    first = lambda rows, cols: pl.BlockSpec((rows, cols), lambda i, info: (0, 0))
    out = lambda rows, cols, dtype: jax.ShapeDtypeStruct((rows, cols), dtype)
    part, low, *rest = pl.pallas_call(
        functools.partial(middle_back_kernel, count),
        grid_spec=pltpu.PrefetchScalarGridSpec(
            num_scalar_prefetch=1,
            grid=(1,),
            in_specs=[first(height, width)] * count
            + [own(width), own(1), part, first(1, width), whole(w_out)],
            out_specs=[first(1, width), first(height, width)]
            + [first(height, cols)] * count
            + [first(height, width // count)] * count,
        ),
        out_shape=[out(1, width, F32), out(height, width, BF16)]
        + [out(height, cols, BF16)] * count
        + [out(height, width // count, BF16)] * count,
        compiler_params=params(),
        cost_estimate=cost(
            flops=2 * height * width * width, bytes_accessed=2 * width * width, transcendentals=0
        ),
        name="middle_back",
    )(info, *pieces, middle, inv, grads, gain[None, :], w_out)
    return part[0], low, rest[:count], rest[count:]


def finish_kernel(count, info, *refs):
    sent_refs, first_refs = refs[:count], refs[count : 2 * count]
    x_ref, inv_ref, gain_ref, out_ref = refs[2 * count :]
    height = sent_refs[0].shape[0]
    pieces = out_ref.shape[0] // height
    for i in range(pieces):
        distance = lax.rem(info[1] - pl.program_id(0) * pieces - i + 2 * count, count)
        for k in range(count):

            @pl.when(distance == k)
            def _(i=i, k=k):
                out_ref[i * height : (i + 1) * height, :] = sent_refs[k][...].astype(F32)

    size, width = out_ref.shape[0], count * x_ref.shape[1]
    rows = pl.ds(pl.multiple_of(pl.program_id(0) * size, size), size)
    place = first_refs[0].shape[0] - EXTRA
    first, terms = None, None
    for ref in first_refs:
        part, extra = ref[rows, :].astype(F32), ref[place:, :size].astype(F32)
        first = part if first is None else first + part
        terms = extra if terms is None else terms + extra
    line = lax.broadcasted_iota(jnp.int32, terms.shape, 0)
    own = jnp.where(line // 2 == pl.program_id(0), terms, 0.0)
    inner = as_columns(jnp.sum(own, axis=0, keepdims=True) / width)[:, :1]
    inv = inv_ref[...]
    hat = x_ref[...].astype(F32) * inv
    out_ref[...] += inv * (gain_ref[...] * first - hat * inner)


def finish(info, sent_pieces, first_pieces, x, inv, gain, seqs):
    count = len(first_pieces)
    rows, feat = x.shape
    size = rows // seqs
    one = lambda array: pl.BlockSpec(array.shape, lambda i, info: (0, 0))
    own = lambda cols: pl.BlockSpec((size, cols), lambda i, info: (i, 0))
    return pl.pallas_call(
        functools.partial(finish_kernel, count),
        grid_spec=pltpu.PrefetchScalarGridSpec(
            num_scalar_prefetch=1,
            grid=(seqs,),
            in_specs=[pl.BlockSpec((rows // count, feat), lambda i, info: (count, 0))] * count
            + [one(a) for a in first_pieces]
            + [own(feat), own(1), pl.BlockSpec((1, feat), lambda i, info: (0, info[1]))],
            out_specs=own(feat),
        ),
        out_shape=jax.ShapeDtypeStruct((rows, feat), F32),
        compiler_params=params(),
        name="finish",
    )(info, *sent_pieces, *first_pieces, x, inv, gain[None, :])


def spread_kernel(turned, in_ref, out_ref):
    block = in_ref[...].astype(F32)
    out_ref[0] = block.T if turned else block


def spread(rows, experts, turned):
    height, width = rows.shape
    units = width // experts
    shape = (units, height) if turned else (height, units)
    return pl.pallas_call(
        functools.partial(spread_kernel, turned),
        grid=(experts,),
        in_specs=[pl.BlockSpec((height, units), lambda e: (0, e))],
        out_specs=pl.BlockSpec((1, *shape), lambda e: (e, 0, 0)),
        out_shape=jax.ShapeDtypeStruct((experts, *shape), F32),
        compiler_params=params(),
        name="spread",
    )(rows)


def rotary_tables(positions):
    exponent = jnp.arange(HD // 2, dtype=F32) * 2.0 / HD
    frequency = ROTARY_BASE ** (-exponent)
    angles = positions.astype(F32)[:, None] * frequency[None, :]
    cosine = jnp.concatenate([jnp.cos(angles), jnp.cos(angles)], axis=-1)
    sine = jnp.concatenate([jnp.sin(angles), jnp.sin(angles)], axis=-1)
    return cosine, sine


def shards(
    inputs,
    lengths,
    routes,
    attn_gain,
    w_query,
    w_key,
    w_value,
    query_gain,
    key_gain,
    w_out,
    ffn_gain,
    router,
    w_gate,
    w_up,
    w_down,
    cotangent,
):
    size, seqs, feat = inputs.shape
    width, head_cols = w_query.shape
    heads = head_cols // HD
    tp_rank, tp_count = lax.axis_index("tp"), lax.axis_size("tp")
    sq_rank, sq_count = lax.axis_index("sq"), lax.axis_size("sq")
    experts = w_gate.shape[0]
    experts_total = router.shape[1]
    all_cols = head_cols * tp_count
    block = width // sq_count
    chunks = CHUNKS
    per = seqs // chunks
    rows_n = per * size
    quarter = rows_n // tp_count
    positions = sq_rank * size + jnp.arange(size, dtype=jnp.int32)
    cosine, sine = rotary_tables(positions)
    group = lambda array: [
        array[:, c * per : (c + 1) * per].transpose(1, 0, 2).reshape(rows_n, -1)
        for c in range(chunks)
    ]
    inputs_c, routes_c = group(inputs), group(routes)
    cotangent_rows = cotangent.transpose(1, 0, 2).reshape(seqs * size, feat)
    info_c = [
        jnp.concatenate(
            [sq_rank[None], tp_rank[None], lengths[c * per : (c + 1) * per]]
        ).astype(jnp.int32)
        for c in range(chunks)
    ]
    rank = tp_rank[None].astype(jnp.int32)
    def attention_in(c, gathered, *others):
        low, normed, inv, query_raw, key_raw, value, squares = front(
            after(rank, *others) if others else rank, gathered, attn_gain, w_query, w_key, w_value
        )
        with jax.named_scope(f"squares{c}"):
            got = exchange([squares] * tp_count)
        return low, normed, inv, query_raw, key_raw, sum(got), value, got[1:]

    def rotated(c, *others):
        query_raw, key_raw, squares, value = ins[c][3:7]
        squares = after(squares, *others) if others else squares
        return rotate(
            query_raw, key_raw, value, squares, query_gain, key_gain, cosine, sine, all_cols
        )

    def gather_heads(c, ready, *others):
        with jax.named_scope(f"heads{c}"):
            own = attn_c[c][0].reshape(rows_n, head_cols)
            return gather_tp(after(own, *ready) if ready else own, *others)

    early_parts = lambda gathered: (gathered[0][1], gathered[0][-2])

    ins, turned, slots_c, attn_c, heads_c, mids, exps = [], [], [], [], [], [], []
    with jax.named_scope("inputs0"):
        x0 = gather_tp(inputs_c[0])
    with jax.named_scope("inputs1"):
        x1_first = first_step(after(inputs_c[1], x0[0][3]))
    ins.append(attention_in(0, x0))
    turned.append(rotated(0, *x1_first[1:]))
    with jax.named_scope("inputs1"):
        x1_second = second_step(x1_first, ins[0][1])
        x1 = third_step(x1_first, x1_second, turned[0][1])
    with jax.named_scope("pairs0"):
        near0 = gather_sides(turned[0][1])
    ins.append(attention_in(1, x1))
    slab = w_out.shape[0] // sq_count
    w_slab = after(block_of(w_out, sq_rank, slab, 0), *ins[1][7])
    w_out_all = lax.all_gather(w_slab, ("tp", "sq"), axis=0, tiled=True)
    with jax.named_scope("cotangent"):
        grads_first = first_step(after(cotangent_rows, *ins[1][7]))
    with jax.named_scope("pairs0"):
        diag0 = gather_diagonal(turned[0][1], [after(side, x1[0][3]) for side in near0])
    turned.append(rotated(1, *diag0, *grads_first[1:]))
    with jax.named_scope("cotangent"):
        grads_second = second_step(grads_first, turned[1][1])
    with jax.named_scope("pairs0"):
        slots_c.append(gather_slots(turned[0][1], near0, *diag0))
    with jax.named_scope("pairs1"):
        near1 = gather_sides(turned[1][1])
    attn_c.append(attn_forward(after(info_c[0], turned[1][1]), turned[0][0], slots_c[0]))
    heads_c.append(gather_heads(0, grads_second))
    with jax.named_scope("pairs1"):
        near1 = [after(side, attn_c[0][2]) for side in near1]
        diag1 = gather_diagonal(turned[1][1], near1)
        slots_c.append(gather_slots(turned[1][1], near1, *diag1))
    with jax.named_scope("cotangent"):
        grads_third = third_step(grads_first, grads_second)
    attn_c.append(
        attn_forward(
            after(info_c[1], *early_parts(heads_c[0])), turned[1][0], slots_c[1]
        )
    )
    grad_all = joined_rows(rank, grads_third)

    def middle_of(c, *others):
        return middle_rows(
            after(rank, *others), heads_c[c], ins[c][0], w_out_all, ffn_gain, router, routes_c[c]
        )

    def hidden_of(c, *others):
        _, _, _, ffn_in, probs, routed = mids[c]
        return expert_hidden(
            after(info_c[c], *others), ffn_in, grad_all, probs, routed, w_gate, w_up, w_down, c
        )

    def back_of(c, *others):
        _, gate_grads, up_grads, inner = exps[c]
        return expert_back(
            after(info_c[c], *others),
            gate_grads,
            up_grads,
            inner,
            mids[c][4],
            router,
            mids[c][3],
            w_gate,
            w_up,
            tp_count,
        )

    def ffn_exchange(c, pieces):
        with jax.named_scope(f"ffn_grad{c}"):
            return exchange(pieces)

    def middle_grad_of(c, pieces, *others):
        return middle_back(
            after(info_c[c], *others), pieces, mids[c][1], mids[c][2], grad_all, ffn_gain, w_out_all, c
        )

    def mixture_of(c, *others):
        pieces = mixture(
            after(info_c[c], *others), exps[c][0], w_down, backs[c][2], backs[c][3], tp_count
        )
        with jax.named_scope(f"mixture{c}"):
            return exchange(pieces)

    def output_of(c, pieces):
        total = block_of(mids[c][1], tp_rank, feat, 1)
        for piece in pieces:
            total = total + piece[:rows_n].astype(F32)
        return total.astype(BF16).reshape(per, size, feat).transpose(1, 0, 2)

    def attention_back(c, *others):
        return attn_backward(
            after(info_c[c], *others), turned[c][0], sent[c], *attn_c[c][1:], slots_c[c]
        )

    def cores_of(c):
        with jax.named_scope(f"pair_cores{c}"):
            return scatter_cores(dqs[c][2])

    def diagonal_of(c, received):
        if sq_count != 8:
            return None, []
        with jax.named_scope(f"pair_diagonal{c}"):
            diagonal = scatter_diagonal(dqs[c][1], received)
            return diagonal, send_halves(diagonal)

    def sides_of(c, received, diagonal):
        with jax.named_scope(f"pair_sides{c}"):
            return scatter_sides(dqs[c][1], received, diagonal)

    def stats_of(c, received, blocks):
        query_raw, key_raw, squares = ins[c][3:6]
        operands = (
            dqs[c][0],
            scatter_total(dqs[c][1], received, blocks),
            query_raw,
            key_raw,
            squares,
            query_gain[None, :],
            key_gain[None, :],
            cosine,
            sine,
        )
        stats, gain_qk = back_stats(operands, all_cols)
        with jax.named_scope(f"stats{c}"):
            stats = sum(exchange([stats] * tp_count))
        return operands, stats, gain_qk

    def first_of(c, operands, stats, *others):
        low, _, inv = ins[c][:3]
        raw, pieces, part = back_first(
            after(info_c[c], *others),
            operands,
            stats,
            low,
            inv,
            attn_gain,
            w_query,
            w_key,
            w_value,
            all_cols,
            tp_count,
        )
        with jax.named_scope(f"first{c}"):
            pieces = exchange(pieces)
        return raw, pieces, part

    scatter = lambda g: lax.psum_scatter(g, "sq", scatter_dimension=0, tiled=True)

    backs, dqs = [], []
    mids.append(middle_of(0, attn_c[1][2], *grads_second))
    exps.append(hidden_of(0))
    heads_c.append(gather_heads(1, (), (mids[0][3],), (exps[0][3],)))
    back0, router0 = back_of(0)
    sent0 = ffn_exchange(0, back0)
    mids.append(middle_of(1, back0[0]))
    exps.append(hidden_of(1))
    ffn_list = [m[3] for m in mids]
    w_down_part = weight_grad([grad_all], [e[0] for e in exps])
    backs.append(middle_grad_of(0, sent0, w_down_part))
    sent = [mixture_of(0, backs[0][1])]
    back1, router1 = back_of(1, sent[0][0])
    sent1 = ffn_exchange(1, back1)
    w_up_part = weight_grad(ffn_list, [exps[0][2], after(exps[1][2], back1[0])])
    dqs.append(attention_back(0, w_up_part))
    backs.append(middle_grad_of(1, sent1, dqs[0][0]))
    sent.append(mixture_of(1, backs[1][1]))
    w_gate_part = weight_grad(ffn_list, [exps[0][1], after(exps[1][1], sent[1][0])])
    cores0 = cores_of(0)
    summed0, diagonal0 = diagonal_of(0, cores0)
    sums0, sides0 = sides_of(0, cores0, diagonal0)
    attn_own = [block_of(m[0], tp_rank, quarter, 0) for m in mids]
    w_out_part = weight_grad([backs[0][1], after(backs[1][1], w_gate_part)], attn_own)
    dqs.append(attention_back(1, w_out_part, *diagonal0, *sums0))
    cores1 = cores_of(1)
    operands0, stats0, gain0 = stats_of(0, after(cores0, dqs[1][0]), sides0)
    summed1, diagonal1 = diagonal_of(1, after(cores1, gain0))
    raw0, first0, part0 = first_of(
        0, operands0, stats0, *([cores1] if summed1 is None else [summed1])
    )
    sums1, sides1 = sides_of(1, cores1, diagonal1)

    outputs = [output_of(c, sent[c]) for c in range(2)]
    operands1, stats1, gain1 = stats_of(1, cores1, sides1)
    raw1, first1, part1 = first_of(1, operands1, stats1, *first0[1:])
    w_down_rows = scatter(after(w_down_part, backs[0][1]))
    w_up_rows = scatter(after(w_up_part, backs[1][1], w_down_rows))
    w_out_rows = scatter(after(w_out_part, w_up_rows, raw0))
    w_gate_rows = scatter(after(w_gate_part, w_out_rows, raw1))
    w_down_grad = spread(w_down_rows, experts, True)
    w_up_grad = spread(w_up_rows, experts, False)
    w_gate_grad = spread(w_gate_rows, experts, False)
    with jax.named_scope("weights"):
        own = reduce_cores(info_c[0], [([(i[1], 0) for i in ins], [raw0, raw1])])
        qkv_grad, came = reduce_chips(own)
    with jax.named_scope("out_weight"):
        out_pieces = exchange(
            [block_of(w_out_rows, (tp_rank + k) % tp_count, head_cols, 1) for k in range(tp_count)]
        )
        w_out_grad = sum(p.astype(F32) for p in out_pieces).T
    finals = [
        finish(
            after(info_c[c], own),
            sent[c],
            pieces,
            inputs_c[c],
            ins[c][2],
            attn_gain,
            per,
        )
        for c, pieces in enumerate((first0, first1))
    ]
    small = jnp.concatenate(
        [
            router0 + router1,
            (backs[0][0] + backs[1][0])[None, :],
            (part0 + after(part1, own))[None, :],
            lax.dynamic_update_slice_in_dim(
                jnp.zeros((2, all_cols), F32), gain0 + gain1, tp_rank * head_cols, 1
            ),
        ],
        axis=0,
    )
    with jax.named_scope("small"):
        small = butterfly(butterfly(small, "sq"), "tp")
    early, late = small[: experts_total + 1], small[experts_total + 1 :]
    return (
        jnp.concatenate(outputs, axis=1),
        jnp.concatenate(finals, axis=0).reshape(seqs, size, feat).transpose(1, 0, 2),
        late[0],
        qkv_grad[:, :head_cols],
        qkv_grad[:, head_cols : 2 * head_cols],
        qkv_grad[:, 2 * head_cols : 3 * head_cols],
        late[1],
        late[2],
        w_out_grad,
        early[experts_total],
        early[:experts_total].T,
        w_gate_grad,
        w_up_grad,
        w_down_grad,
    )


def solution(mesh):
    placed = (
        P("sq", None, "tp"),
        P(),
        P("sq", None, None),
        P(),
        P(None, "tp"),
        P(None, "tp"),
        P(None, "tp"),
        P("tp"),
        P("tp"),
        P("tp", None),
        P(),
        P(),
        P("tp", None, None),
        P("tp", None, None),
        P("tp", None, None),
        P("sq", None, "tp"),
    )
    return jax.shard_map(
        shards,
        mesh=mesh,
        in_specs=placed,
        out_specs=(
            P("sq", None, "tp"),
            P("sq", None, "tp"),
            P(),
            P("sq", "tp"),
            P("sq", "tp"),
            P("sq", "tp"),
            P(),
            P(),
            P("tp", "sq"),
            P(),
            P(),
            P("tp", "sq", None),
            P("tp", "sq", None),
            P("tp", None, "sq"),
        ),
        check_vma=False,
    )
```
